512 devices in a mesh: ctx: 32 (over z, y_lo), hid: 16 (over y_hi, x, core).
Axes of the slice: x: 4, y: 4 (y_hi: 2, y_lo: 2; y = y_hi * 2 + y_lo), z: 16, core: 2. Of those that a mesh axis runs over, the one named last changes fastest.
Arguments:
- queries: bfloat16 [16384, 2048], P('ctx', 'hid'), may hold values from -9 to 9
- keys: bfloat16 [16384, 512], P('ctx'), may hold values from -9 to 9
- values: bfloat16 [16384, 512], P('ctx'), may hold values from -7 to 7
- doc_ids: int32 [16384], P('ctx'), may hold values from 0 to 7, never falling along the last dimension, each value on 1 to 12288 neighbouring positions
- hidden: bfloat16 [16384, 3072], P('ctx', 'hid'), may hold values from -6 to 6
- out_weight: bfloat16 [2048, 3072], P(None, 'hid'), may hold values from -0.125 to 0.125
- projector: bfloat16 [3072, 4096], P(None, 'hid'), may hold values from -0.109375 to 0.109375
- teacher: bfloat16 [16384, 4096], P(('ctx', 'hid')), may hold values from -6 to 6
Outputs:
- grad_projector: float32 [3072, 4096], P('ctx', 'hid')
- attended: bfloat16 [16384, 2048], P('ctx', 'hid')
The draws below stay inside these ranges and needn't reach their ends.
Inputs may be any that keep to these rules, and one draw needn't show every extreme that they name: `doc_ids`: document ids never fall along the sequence; every document spans at most three quarters of 16384 positions.
All inputs are finite; a program needn't handle non-finite values.
Results may differ from the reference program's by a relative error of at most 0.0034.
Values may be sent and summed in bfloat16 or wider, within the bound.
No kernel may reach another device: no remote copies, remote signals or barrier semaphores. Data moves between devices by JAX's collectives and lax.ppermute only.
A program may use at most 64 MiB of HBM per device.

```python
import math
import jax
import jax.numpy as jnp
import numpy as np
from jax import lax

DS = 3072
DT = 4096
HEAD = 128
GROUP = 4
HEADS = 16
KV_HEADS = 4
ROWS = 512
LENGTH = 16384
DOCS = 8


def draw_queries(key, part):
    key = jax.random.fold_in(key, 21)
    shape = (LENGTH, HEADS * HEAD)
    return jnp.clip(jax.random.normal(key, shape), -6.0, 6.0).astype(jnp.bfloat16)


def draw_keys(key, part):
    key = jax.random.fold_in(key, 22)
    shape = (LENGTH, KV_HEADS * HEAD)
    return jnp.clip(jax.random.normal(key, shape), -6.0, 6.0).astype(jnp.bfloat16)


def draw_values(key, part):
    key = jax.random.fold_in(key, 23)
    width = KV_HEADS * HEAD
    block_count = LENGTH // ROWS
    offsets = jax.random.uniform(jax.random.fold_in(key, 1), (block_count, width), minval=-3.0, maxval=3.0)
    offsets = jnp.repeat(offsets, ROWS, axis=0)
    noise = jnp.clip(jax.random.normal(key, (LENGTH, width)), -3.5, 3.5)
    return (offsets + noise).astype(jnp.bfloat16)


def strengthened(values, rng, source, target, blocks, factor):
    owner, partner = [(jnp.arange(values.shape[axis_at]) // (values.shape[axis_at] // blocks)).reshape([-1 if axis == axis_at else 1 for axis in range(values.ndim)]) for axis_at in (source, target)]
    chosen = jax.random.permutation(rng, blocks)[partner]
    strong = (owner == chosen) | (owner == (partner + blocks // 2) % blocks)
    return jnp.where(strong, factor * values, values)


def block_scale(stream_key, dims, shards, low, largest):
    def one(dim, shards_of):
        steps = jax.random.uniform(jax.random.fold_in(jax.random.fold_in(stream_key, 6), dim), (shards_of,), jnp.float32, low / len(shards), largest / len(shards))
        return jnp.repeat(jnp.exp(steps), dims[dim] // shards_of).reshape((-1,) + (1,) * (len(dims) - dim - 1))

    level = one(*shards[0])
    for cut in shards[1:]:
        level = level * one(*cut)
    return level


def length_profile(count, total, limit, skew):
    weights = [(1 << 20) // math.isqrt(rank ** skew) + 1 for rank in range(2, count + 1)]
    spare, counts = total - limit - (count - 1), [1] * (count - 1)
    while spare > 0:
        candidates = [i for i in range(count - 1) if counts[i] < limit]
        mass, budget = sum([weights[i] for i in candidates]), spare
        for i in candidates:
            addition = min(limit - counts[i], max(1, budget * weights[i] // mass), spare)
            counts[i] = counts[i] + addition
            spare = spare - addition
    return np.array([limit] + counts)


def uneven_parts(stream_key, amount, total, bound, lean):
    if amount == 2:
        one = jax.random.randint(stream_key, (), max(1, total - bound), min(bound, total - 1) + 1)
        return jnp.stack([one, total - one])
    lengths = jnp.asarray(length_profile(amount, total, bound, lean), jnp.int32)
    couples = (amount - 1) // 2
    donor, taker = lengths[1:1 + 2 * couples:2], lengths[2:2 + 2 * couples:2]
    slack = jnp.minimum(donor - 1, bound - taker)
    moved = jax.random.randint(jax.random.fold_in(stream_key, 1), (couples,), 0, 1 << 20) % (slack + 1)
    lengths = lengths.at[1:1 + 2 * couples:2].set(donor - moved).at[2:2 + 2 * couples:2].set(taker + moved)
    return lengths[jax.random.permutation(jax.random.fold_in(stream_key, 2), amount)]


def normal_values(stream_key, extent, scale, limit, split=(), kind=jnp.bfloat16):
    drawn = jax.random.normal(stream_key, extent, jnp.float32) * scale
    if len(split) > 0:
        drawn = block_scale(stream_key, extent, split, -0.22, 0.18) * drawn
    return jnp.clip(drawn, min=-limit, max=limit).astype(kind)


def noise_with(rng, dims, scale, limit, cuts, heavy, kind=jnp.bfloat16):
    values = scale * jax.random.normal(rng, dims, jnp.float32)
    if cuts:
        values = values * block_scale(rng, dims, cuts, -0.22, 0.18)
    return jnp.clip(strengthened(values, jax.random.fold_in(rng, 3), *heavy), -limit, limit).astype(kind)


def setup_inputs(seed: int = 0) -> dict:
    key_list = jax.random.split(jax.random.key(seed), 9)
    queries = draw_queries(jax.random.fold_in(key_list[8], 71), 0)
    keys = draw_keys(jax.random.fold_in(key_list[8], 71), 0)
    values = draw_values(jax.random.fold_in(key_list[8], 71), 0)
    doc_ids = jnp.searchsorted(jnp.cumsum(uneven_parts(key_list[3], DOCS, LENGTH, (3 * LENGTH) // 4, 2)), jnp.arange(LENGTH), side="right").astype(jnp.int32)
    hidden = noise_with(key_list[4], (LENGTH, DS), 0.5, 6.0, ((0, 32), (1, 16)), (0, 1, 32, 2.75))
    out_weight = normal_values(key_list[5], (HEADS * HEAD, DS), (HEADS * HEAD) ** -0.5, 0.125, ((1, 16),))
    projector = normal_values(key_list[6], (DS, DT), DS ** -0.5, 0.109375, ((1, 16),))
    teacher = normal_values(key_list[7], (LENGTH, DT), 1.0, 6.0, ((0, 512),))
    return {"queries": queries, "keys": keys, "values": values, "doc_ids": doc_ids, "hidden": hidden, "out_weight": out_weight, "projector": projector, "teacher": teacher}


def attention_all(queries, keys, values, doc_ids):
    length = queries.shape[0]
    query_all = queries.astype(jnp.float32).reshape(length, HEADS, HEAD)
    key_all = keys.astype(jnp.float32).reshape(length, KV_HEADS, HEAD)
    value_all = values.astype(jnp.float32).reshape(length, KV_HEADS, HEAD)
    positions = jnp.arange(length, dtype=jnp.int32)
    block_rows = min(512, length)
    block_count = length // block_rows

    def one_block(block_index):
        start = (block_index * block_rows).astype(jnp.int32)
        query_block = lax.dynamic_slice_in_dim(query_all, start, block_rows, 0)
        query_pos = start + jnp.arange(block_rows, dtype=jnp.int32)
        query_doc = lax.dynamic_slice_in_dim(doc_ids, start, block_rows, 0)
        allowed = (positions[None, :] <= query_pos[:, None]) & (doc_ids[None, :] == query_doc[:, None])

        def one_head(head_index):
            shared = (head_index // GROUP).astype(jnp.int32)
            query_head = lax.dynamic_index_in_dim(query_block, head_index, 1, keepdims=False)
            key_head = lax.dynamic_index_in_dim(key_all, shared, 1, keepdims=False)
            value_head = lax.dynamic_index_in_dim(value_all, shared, 1, keepdims=False)
            scores = jnp.dot(query_head, key_head.T, precision=lax.Precision.HIGHEST) * (HEAD ** -0.5)
            masked = jnp.where(allowed, scores, -1e30)
            row_max = jnp.max(masked, axis=1)
            weights = jnp.where(allowed, jnp.exp(masked - row_max[:, None]), 0.0)
            row_total = jnp.sum(weights, axis=1)
            rounded = weights.astype(jnp.bfloat16).astype(jnp.float32)
            summed = jnp.dot(rounded, value_head, precision=lax.Precision.HIGHEST)
            return summed / row_total[:, None]

        heads_out = lax.map(one_head, jnp.arange(HEADS, dtype=jnp.int32))
        return jnp.transpose(heads_out, (1, 0, 2)).reshape(block_rows, HEADS * HEAD)

    blocks = lax.map(one_block, jnp.arange(block_count, dtype=jnp.int32))
    return blocks.reshape(length, HEADS * HEAD).astype(jnp.bfloat16)


def reference(queries, keys, values, doc_ids, hidden, out_weight, projector, teacher):
    length = queries.shape[0]
    attended = attention_all(queries, keys, values, doc_ids)
    mixed = jnp.dot(attended.astype(jnp.float32), out_weight.astype(jnp.float32), precision=lax.Precision.HIGHEST)
    student = (hidden.astype(jnp.float32) + mixed).astype(jnp.bfloat16)
    projected = jnp.dot(student.astype(jnp.float32), projector.astype(jnp.float32), precision=lax.Precision.HIGHEST)
    mismatch = (projected - teacher.astype(jnp.float32)).astype(jnp.bfloat16)
    summed = jnp.dot(student.astype(jnp.float32).T, mismatch.astype(jnp.float32), precision=lax.Precision.HIGHEST)
    return (summed * (length ** -0.5), attended)
```

```python
import functools

import jax
import jax.numpy as jnp
from jax import lax
from jax.experimental import pallas as pl
from jax.experimental.pallas import tpu as pltpu
from jax.sharding import Mesh
from jax.sharding import PartitionSpec as P

HEAD = 128
SCALE2 = HEAD ** -0.5 * 1.4426950408889634
EMPTY = -1e30
MASKED = -2e30
BF = jnp.bfloat16
F32 = jnp.float32
CTX = ("z", "yl")
HID = ("yh", "xh", "xl", "c")
GROUP = ("xl", "c")
OCTET = ("yl", "xl", "c")
HEADSETS = ("yh", "xh")
CHIPS = ("xl", "yh", "xh")
BLOCKS = 4


def attend_kernel(sc, kv, q_own, q_other, qdoc, out, v_turned):
    depth = kv.shape[0]
    z, yl, j = sc[144], sc[145], sc[146]
    for block in range(depth):
        v_turned[:, block * 128:(block + 1) * 128] = kv[block, 128:256, :].T
    key_iota = lax.broadcasted_iota(jnp.int32, (128, 512), 0)
    row_iota = lax.broadcasted_iota(jnp.int32, (1, 512), 1) % 128
    for side, q_ref in ((0, q_own), (1, q_other)):
        yl_q = yl if side == 0 else 1 - yl
        block_q = 2 * z + yl_q

        def one_tile(rc, carry, side=side, q_ref=q_ref, yl_q=yl_q, block_q=block_q):
            row0 = pl.multiple_of(rc * 128, 128)
            q = jnp.concatenate([q_ref[pl.ds(h * 512 + row0, 128), :] for h in range(4)], axis=0)
            docs = qdoc[pl.ds(side * 4 + rc, 1), :]
            docs = jnp.concatenate([docs] * 4, axis=1)
            first, last = sc[128 + side * 4 + rc], sc[136 + side * 4 + rc]
            q_min = block_q * 512 + row0
            q_pos = q_min + row_iota

            def step(ch, state, masked):
                run_max, run_sum, acc = state
                keys = kv[pl.ds(ch * BLOCKS, BLOCKS), 0:128, :].reshape(BLOCKS * 128, 128)
                s = lax.dot_general(keys, q, (((1,), (1,)), ((), ())), preferred_element_type=F32) * SCALE2
                if masked:
                    parts = []
                    for i in range(BLOCKS):
                        block = ch * BLOCKS + i
                        low = jnp.zeros((1, 512), jnp.int32)
                        for d in range(8):
                            low = jnp.where(docs == d, sc[block * 8 + d], low)
                        low = low - j * 128
                        high = q_pos - ((2 * block + yl) * 512 + j * 128)
                        ok = (key_iota >= low) & (key_iota <= high)
                        parts.append(jnp.where(ok, s[i * 128:(i + 1) * 128], MASKED))
                    s = jnp.concatenate(parts, axis=0)
                new_max = jnp.maximum(run_max, jnp.max(s, axis=0, keepdims=True))
                factor = jnp.exp2(run_max - new_max)
                w = jnp.exp2(s - new_max)
                new_sum = run_sum * factor + jnp.sum(w, axis=0, keepdims=True)
                cols = pl.ds(pl.multiple_of(ch * (BLOCKS * 128), BLOCKS * 128), BLOCKS * 128)
                new_acc = acc * factor + jnp.dot(v_turned[:, cols], w.astype(BF), preferred_element_type=F32)
                return new_max, new_sum, new_acc

            def any_step(ch, state):
                k_max = (2 * (ch * BLOCKS + BLOCKS - 1) + yl) * 512 + j * 128 + 127
                full = (k_max <= q_min) & (sc[ch * (BLOCKS * 8) + last] <= j * 128)
                return lax.cond(full, functools.partial(step, ch, masked=False), functools.partial(step, ch, masked=True), state)

            begin = jnp.int32(0)
            for ch in range(depth // BLOCKS):
                none = sc[(ch * BLOCKS + BLOCKS - 1) * 8 + first] >= (j + 1) * 128
                begin = begin + none.astype(jnp.int32)
            end = z // BLOCKS + 1
            state = (jnp.full((1, 512), EMPTY, F32), jnp.zeros((1, 512), F32), jnp.zeros((128, 512), F32))
            run_max, run_sum, acc = lax.fori_loop(begin, end, any_step, state)
            seen = run_sum > 0
            o = (acc * (1.0 / jnp.where(seen, run_sum, 1.0))).astype(BF)
            lse = jnp.where(seen, run_max + jnp.log2(jnp.where(seen, run_sum, 1.0)), EMPTY)
            hi = lse.astype(BF).astype(F32)
            mid = (lse - hi).astype(BF).astype(F32)
            lo = lse - hi - mid
            dest = yl_q * 4 + rc
            rows = [part[:, h * 128:(h + 1) * 128] for part in (hi, mid, lo) for h in range(4)]
            rows.append(jnp.zeros((4, 128), F32))
            for h in range(4):
                out[dest, h * 128:(h + 1) * 128, :] = o[:, h * 128:(h + 1) * 128]
            out[dest, 512:528, :] = jnp.concatenate(rows, axis=0).astype(BF)
            return carry

        lax.fori_loop(0, 4, one_tile, 0)


def combine_kernel(parts, out):
    count = parts.shape[0]
    tails = [parts[s, 512:528, :].astype(F32) for s in range(count)]
    for h in range(4):
        lses = [t[h:h + 1] + t[4 + h:5 + h] + t[8 + h:9 + h] for t in tails]
        top = functools.reduce(jnp.maximum, lses)
        weights = [jnp.exp2(v - top) for v in lses]
        inverse = 1.0 / sum(weights)
        total = sum(w * inverse * parts[s, h * 128:(h + 1) * 128, :].astype(F32) for s, w in enumerate(weights))
        out[h * 128:(h + 1) * 128, :] = total.astype(BF)


VMEM = pl.BlockSpec(memory_space=pltpu.VMEM)
SMEM = pl.BlockSpec(memory_space=pltpu.SMEM)


def attend(scalars, kv, q_own, q_other, qdoc):
    return pl.pallas_call(
        attend_kernel,
        out_shape=jax.ShapeDtypeStruct((8, 528, 128), BF),
        in_specs=[SMEM, VMEM, VMEM, VMEM, VMEM],
        out_specs=VMEM,
        scratch_shapes=[pltpu.VMEM((128, 128 * kv.shape[0]), BF)],
        compiler_params=pltpu.CompilerParams(vmem_limit_bytes=40 * 1024 * 1024),
    )(scalars, kv, q_own, q_other, qdoc)


def combine(parts):
    return pl.pallas_call(
        combine_kernel,
        out_shape=jax.ShapeDtypeStruct((512, 128), BF),
        in_specs=[VMEM],
        out_specs=VMEM,
        compiler_params=pltpu.CompilerParams(vmem_limit_bytes=16 * 1024 * 1024),
    )(parts)


def spread(x, axes):
    count = 1
    for axis in axes:
        count *= lax.axis_size(axis)
    return lax.all_to_all(jnp.broadcast_to(x[None], (count,) + x.shape), axes, 0, 0)


def on_device(queries, keys, values, doc_ids, hidden, out_weight, projector, teacher):
    z, yl, c = lax.axis_index("z"), lax.axis_index("yl"), lax.axis_index("c")
    g = lax.axis_index("yh") * 2 + lax.axis_index("xh")
    j = lax.axis_index("xl") * 2 + c
    swap = [(0, 1), (1, 0)]

    doc_rows = jnp.pad(doc_ids.astype(BF).reshape(4, 128), ((0, 12), (0, 0)))
    own_k = lax.dynamic_slice(keys, (j * 128, g * 128), (128, 128))
    own_v = lax.dynamic_slice(values, (j * 128, g * 128), (128, 128))
    kv = spread(jnp.concatenate([own_k, own_v, doc_rows], axis=0), ("z",))
    q_own = lax.all_gather(queries, GROUP, axis=0, tiled=True)
    q_other = lax.ppermute(jnp.concatenate([q_own, doc_rows], axis=0), "yl", swap)

    weight_g = lax.all_gather(out_weight, GROUP, axis=0)
    hidden_g = lax.all_to_all(hidden.reshape(4, 128, 192), GROUP, 0, 0)
    hidden_t = jnp.transpose(hidden_g, (0, 2, 1)).reshape(768, 128)
    teacher_cols = lax.all_to_all(teacher.reshape(32, 16, 256), HID, 1, 0)
    teacher_t = jnp.transpose(teacher_cols.reshape(2, 2, 128, 256), (1, 0, 3, 2))
    teacher_own = lax.dynamic_index_in_dim(teacher_t, c, 0, keepdims=False)
    teacher_other = lax.dynamic_index_in_dim(teacher_t, 1 - c, 0, keepdims=False)

    docs_z = kv[:, 256:260, :].reshape(16, 512).astype(jnp.int32)
    counts = jnp.sum(docs_z[:, None, :] < jnp.arange(8, dtype=jnp.int32)[None, :, None], axis=2, dtype=jnp.int32)
    q_docs = jnp.concatenate([doc_ids.reshape(4, 128), q_other[2048:2052].astype(jnp.int32)], axis=0)
    scalars = jnp.concatenate([counts.reshape(128), q_docs[:, 0], q_docs[:, 127], jnp.stack([z, yl, j]).astype(jnp.int32)])
    partial = attend(scalars, kv, q_own, q_other, q_docs)
    att_rows = combine(lax.all_to_all(partial, OCTET, 0, 0))

    att_head = lax.all_to_all(att_rows.reshape(4, 128, 128), GROUP, 0, 0)
    attended = jnp.transpose(att_head, (0, 2, 1)).reshape(512, 128)

    att_all = spread(att_rows, HEADSETS).reshape(2048, 128)
    mixed = lax.dot_general(weight_g, att_all, (((1,), (0,)), ((), ())), preferred_element_type=F32)
    student = (hidden_t.astype(F32) + mixed.reshape(768, 128)).astype(BF)
    own = spread(student, CHIPS).reshape(2, 3072, 128)
    other = lax.ppermute(own, "c", swap)

    student_t = jnp.concatenate([own[0], own[1], other[0], other[1]], axis=1)
    teacher_all = jnp.concatenate([teacher_own[0], teacher_own[1], teacher_other[0], teacher_other[1]], axis=1)
    projected = lax.dot_general(projector, student_t, (((0,), (0,)), ((), ())), preferred_element_type=F32)
    mismatch = (projected - teacher_all.astype(F32)).astype(BF)
    grad = lax.dot_general(student_t, mismatch, (((1,), (1,)), ((), ())), preferred_element_type=F32)
    grad = grad.reshape(16, 2, 96, 256)
    keep = lax.dynamic_index_in_dim(grad, yl, 1, keepdims=False)
    send = lax.dynamic_index_in_dim(grad, 1 - yl, 1, keepdims=False).astype(BF)
    half = (keep + lax.ppermute(send, "yl", swap).astype(F32)).astype(BF)
    terms = lax.all_to_all(half, "z", 0, 0)
    summed = jnp.sum(terms.astype(F32), axis=0)
    return summed * (16384 ** -0.5), attended


def solution(mesh):
    fine = Mesh(mesh.devices.reshape(16, 2, 2, 2, 2, 2), ("z", "yl", "yh", "xh", "xl", "c"))
    return jax.shard_map(
        on_device,
        mesh=fine,
        in_specs=(
            P(CTX, HID),
            P(CTX, None),
            P(CTX, None),
            P(CTX),
            P(CTX, HID),
            P(None, HID),
            P(None, HID),
            P(CTX + HID, None),
        ),
        out_specs=(P(CTX, HID), P(CTX, HID)),
        check_vma=False,
    )
```

```python
import functools

import jax
import jax.numpy as jnp
from jax import lax
from jax.experimental import pallas as pl
from jax.experimental.pallas import tpu as pltpu
from jax.sharding import Mesh
from jax.sharding import PartitionSpec as P

HEAD = 128
SCALE2 = HEAD ** -0.5 * 1.4426950408889634
EMPTY = -1e30
MASKED = -2e30
BF = jnp.bfloat16
F32 = jnp.float32
CTX = ("zh", "zl", "yl")
HID = ("yh", "xh", "xl", "c")
GROUP = ("xl", "c")
OCTET = ("yl", "xl", "c")
HEADSETS = ("yh", "xh")
CHIPS = ("xl", "yh", "xh")
BLOCKS = 4


def pack_kernel(place, keys, values, docs, out):
    rows = jnp.concatenate([docs[...].astype(F32), jnp.zeros((12, 128), F32)], axis=0).astype(BF)
    for copy in range(out.shape[0]):
        out[copy, 0:128, :] = keys[...]
        out[copy, 128:256, :] = values[...]
        out[copy, 256:272, :] = rows


def attend_kernel(sc, kv0, kv1, kv2, kv3, q_own, q_other, qdoc, early1, early2, early3, out, v_turned):
    z, yl, j = sc[144], sc[145], sc[146]
    pieces = (kv0, kv1, kv2, kv3)
    place = [(z + shift) % 4 for shift in (0, 3, 1, 2)]
    for ch in range(4):
        for i in range(BLOCKS):
            v_turned[:, (ch * BLOCKS + i) * 128:(ch * BLOCKS + i + 1) * 128] = pieces[i][ch, 128:256, :].T
    key_iota = lax.broadcasted_iota(jnp.int32, (128, 512), 0)
    row_iota = lax.broadcasted_iota(jnp.int32, (1, 512), 1) % 128
    for side, q_ref in ((0, q_own), (1, q_other)):
        yl_q = yl if side == 0 else 1 - yl
        block_q = 2 * z + yl_q

        def one_tile(rc, carry, side=side, q_ref=q_ref, yl_q=yl_q, block_q=block_q):
            row0 = pl.multiple_of(rc * 128, 128)
            q = jnp.concatenate([q_ref[pl.ds(pl.multiple_of((h ^ j) * 512, 512) + row0, 128), :] for h in range(4)], axis=0)
            docs = qdoc[pl.ds(side * 4 + rc, 1), :]
            docs = jnp.concatenate([docs] * 4, axis=1)
            first, last = sc[128 + side * 4 + rc], sc[136 + side * 4 + rc]
            q_min = block_q * 512 + row0
            q_pos = q_min + row_iota

            def step(ch, state, masked):
                run_max, run_sum, acc = state
                keys = jnp.concatenate([piece[ch, 0:128, :] for piece in pieces], axis=0)
                s = lax.dot_general(keys, q, (((1,), (1,)), ((), ())), preferred_element_type=F32) * SCALE2
                if masked:
                    parts = []
                    for i in range(BLOCKS):
                        low = jnp.zeros((1, 512), jnp.int32)
                        for d in range(8):
                            low = jnp.where(docs == d, sc[i * 32 + ch * 8 + d], low)
                        low = low - j * 128
                        high = q_pos - ((2 * (ch * 4 + place[i]) + yl) * 512 + j * 128)
                        ok = (key_iota >= low) & (key_iota <= high)
                        parts.append(jnp.where(ok, s[i * 128:(i + 1) * 128], MASKED))
                    s = jnp.concatenate(parts, axis=0)
                new_max = jnp.maximum(run_max, jnp.max(s, axis=0, keepdims=True))
                factor = jnp.exp2(run_max - new_max)
                w = jnp.exp2(s - new_max)
                new_sum = run_sum * factor + jnp.sum(w, axis=0, keepdims=True)
                cols = pl.ds(pl.multiple_of(ch * (BLOCKS * 128), BLOCKS * 128), BLOCKS * 128)
                new_acc = acc * factor + jnp.dot(v_turned[:, cols], w.astype(BF), preferred_element_type=F32)
                return new_max, new_sum, new_acc

            def any_step(ch, state):
                most = functools.reduce(jnp.maximum, [sc[i * 32 + ch * 8 + last] for i in range(BLOCKS)])
                k_max = (2 * (ch * BLOCKS + BLOCKS - 1) + yl) * 512 + j * 128 + 127
                full = (k_max <= q_min) & (most <= j * 128)
                return lax.cond(full, functools.partial(step, ch, masked=False), functools.partial(step, ch, masked=True), state)

            begin = jnp.int32(0)
            for ch in range(4):
                fewest = functools.reduce(jnp.minimum, [sc[i * 32 + ch * 8 + first] for i in range(BLOCKS)])
                begin = begin + (fewest >= (j + 1) * 128).astype(jnp.int32)
            end = z // BLOCKS + 1
            state = (jnp.full((1, 512), EMPTY, F32), jnp.zeros((1, 512), F32), jnp.zeros((128, 512), F32))
            run_max, run_sum, acc = lax.fori_loop(begin, end, any_step, state)
            seen = run_sum > 0
            o = (acc * (1.0 / jnp.where(seen, run_sum, 1.0))).astype(BF)
            lse = jnp.where(seen, run_max + jnp.log2(jnp.where(seen, run_sum, 1.0)), EMPTY)
            hi = lse.astype(BF).astype(F32)
            mid = (lse - hi).astype(BF).astype(F32)
            lo = lse - hi - mid
            dest = yl_q * 4 + rc
            rows = [part[:, h * 128:(h + 1) * 128] for part in (hi, mid, lo) for h in range(4)]
            rows.append(jnp.zeros((4, 128), F32))
            for h in range(4):
                out[dest, h * 128:(h + 1) * 128, :] = o[:, h * 128:(h + 1) * 128]
            out[dest, 512:528, :] = jnp.concatenate(rows, axis=0).astype(BF)
            return carry

        lax.fori_loop(0, 4, one_tile, 0)


def combine_kernel(parts, out, copies):
    count = parts.shape[0]
    tails = [parts[s, 512:528, :].astype(F32) for s in range(count)]
    for h in range(4):
        lses = [t[h:h + 1] + t[4 + h:5 + h] + t[8 + h:9 + h] for t in tails]
        top = functools.reduce(jnp.maximum, lses)
        weights = [jnp.exp2(v - top) for v in lses]
        inverse = 1.0 / sum(weights)
        rows = slice(h * 128, (h + 1) * 128)
        total = sum(w * inverse * parts[s, rows, :].astype(F32) for s, w in enumerate(weights)).astype(BF)
        out[rows, :] = total
        for copy in range(copies.shape[0]):
            copies[copy, rows, :] = total


def student_kernel(weight_t, att, hidden_t, out):
    att_all = att[...].reshape(2048, 128)
    for part in range(4):
        rows = slice(part * 192, (part + 1) * 192)
        mixed = jnp.dot(weight_t[rows, :], att_all, preferred_element_type=F32)
        student = (hidden_t[rows, :].astype(F32) + mixed).astype(BF)
        for copy in range(out.shape[0]):
            out[copy, rows, :] = student


def mismatch_of(student, projector_t, teacher_t, core):
    both = jnp.concatenate([student[0], student[1]], axis=1)
    projected = jnp.dot(projector_t[...], both, preferred_element_type=F32)
    taught = [teacher_t[:, pl.ds(pl.multiple_of((xl * 2 + core) * 128, 128), 128)] for xl in range(2)]
    return (projected - jnp.concatenate(taught, axis=1).astype(F32)).astype(BF)


def gradient_rows(own, other, turned, half, out):
    def one(zl, carry):
        rows = []
        for zh in range(4):
            start = pl.multiple_of((zh * 4 + zl) * 192 + half * 96, 32)
            rows.append(jnp.concatenate([ref[xl, pl.ds(start, 96), :] for ref in (own, other) for xl in range(2)], axis=1))
        grad = jnp.dot(jnp.concatenate(rows, axis=0), turned[...], preferred_element_type=F32)
        for zh in range(4):
            out[zl, zh] = grad[zh * 96:(zh + 1) * 96].astype(out.dtype)
        return carry

    lax.fori_loop(0, 4, one, 0)


def own_mismatch_kernel(place, own, projector_t, teacher_t, out):
    out[...] = mismatch_of(own, projector_t, teacher_t, place[0]).T


def sent_kernel(place, own, other, projector_t, teacher_t, own_mismatch, mismatch, out):
    mismatch[0:256, :] = own_mismatch[...]
    mismatch[256:512, :] = mismatch_of(other, projector_t, teacher_t, 1 - place[0]).T
    gradient_rows(own, other, mismatch, 1 - place[1], out)


def kept_kernel(place, own, other, mismatch, out):
    gradient_rows(own, other, mismatch, place[1], out)


VMEM = pl.BlockSpec(memory_space=pltpu.VMEM)
SMEM = pl.BlockSpec(memory_space=pltpu.SMEM)
ANY = pl.BlockSpec(memory_space=pl.ANY)


def call(kernel, out_shape, specs, operands, limit, flops=0, scratch=()):
    single = not isinstance(out_shape, list)
    return pl.pallas_call(
        kernel,
        out_shape=out_shape,
        in_specs=specs,
        out_specs=VMEM if single else [VMEM] * len(out_shape),
        scratch_shapes=list(scratch),
        compiler_params=pltpu.CompilerParams(vmem_limit_bytes=limit * 1024 * 1024),
        cost_estimate=pl.CostEstimate(flops=flops, bytes_accessed=4 * 1024 * 1024, transcendentals=0),
    )(*operands)


def shape(*dims, dtype=BF):
    return jax.ShapeDtypeStruct(dims, dtype)


def pack(place, keys, values, docs):
    return pl.pallas_call(
        pack_kernel,
        grid_spec=pltpu.PrefetchScalarGridSpec(
            num_scalar_prefetch=1,
            grid=(1,),
            in_specs=[
                pl.BlockSpec((128, 128), lambda i, place: (place[0], place[1])),
                pl.BlockSpec((128, 128), lambda i, place: (place[0], place[1])),
                pl.BlockSpec((4, 128), lambda i, place: (0, 0)),
            ],
            out_specs=pl.BlockSpec((4, 272, 128), lambda i, place: (0, 0, 0)),
        ),
        out_shape=shape(4, 272, 128),
    )(place, keys, values, docs)


def on_device(queries, keys, values, doc_ids, hidden, out_weight, projector, teacher):
    zl, yl, c = lax.axis_index("zl"), lax.axis_index("yl"), lax.axis_index("c")
    z = lax.axis_index("zh") * 4 + zl
    g = lax.axis_index("yh") * 2 + lax.axis_index("xh")
    j = lax.axis_index("xl") * 2 + c
    swap = [(0, 1), (1, 0)]

    def from_z(x, shift):
        return lax.ppermute(x, ("zh", "zl"), [((i + shift) % 16, i) for i in range(16)])

    docs = doc_ids.reshape(4, 128)
    packed = pack(jnp.stack([j, g]).astype(jnp.int32), keys, values, docs)
    kv_own = lax.all_to_all(packed, "zh", 0, 0)
    kv_below, kv_above = from_z(kv_own, -1), from_z(kv_own, 1)
    kv_far = jnp.concatenate([from_z(kv_own[0:2], -2), from_z(kv_own[2:4], 2)], axis=0)

    doc_rows = jnp.pad(docs.astype(BF), ((0, 12), (0, 0)))
    q_two = jnp.concatenate([queries, lax.ppermute(queries, "c", swap)], axis=0)
    q_own = jnp.concatenate([q_two, lax.ppermute(q_two, "xl", swap), doc_rows], axis=0)
    q_other = lax.ppermute(q_own, "yl", swap)

    weight_t = lax.all_gather(out_weight.T, GROUP, axis=0, tiled=True)
    hidden_t = jnp.transpose(hidden.T.reshape(192, 4, 128), (1, 0, 2))
    hidden_t = lax.all_to_all(hidden_t, GROUP, 0, 0).reshape(768, 128)
    teacher_cols = jnp.transpose(teacher.reshape(32, 16, 256), (1, 0, 2))
    teacher_t = lax.all_to_all(teacher_cols, HID, 0, 0).reshape(512, 256).T
    projector_t = projector.T

    pieces = (kv_own, kv_below, kv_above, kv_far)
    docs_z = jnp.stack([piece[:, 256:260, :].reshape(4, 512) for piece in pieces]).astype(jnp.int32)
    counts = jnp.sum(docs_z[:, :, None, :] < jnp.arange(8, dtype=jnp.int32)[None, None, :, None], axis=3, dtype=jnp.int32)
    q_docs = jnp.concatenate([docs, q_other[2048:2052].astype(jnp.int32)], axis=0)
    scalars = jnp.concatenate([counts.reshape(128), q_docs[:, 0], q_docs[:, 127], jnp.stack([z, yl, j]).astype(jnp.int32)])
    partial = call(
        attend_kernel,
        shape(8, 528, 128),
        [SMEM] + [VMEM] * 7 + [ANY] * 3,
        (scalars, *pieces, q_own, q_other, q_docs, hidden_t, teacher_t, projector_t),
        40,
        scratch=[pltpu.VMEM((128, 2048), BF)],
    )
    att_rows, att_copies = call(
        combine_kernel, [shape(512, 128), shape(4, 512, 128)], [VMEM], (lax.all_to_all(partial, OCTET, 0, 0),), 16
    )

    att_head = lax.all_to_all(att_rows.reshape(4, 128, 128), GROUP, 0, 0)
    attended = jnp.transpose(att_head, (0, 2, 1)).reshape(512, 128)

    att_all = lax.all_to_all(att_copies, HEADSETS, 0, 0)
    student = call(student_kernel, shape(8, 768, 128), [VMEM] * 3, (weight_t, att_all, hidden_t), 24)
    own = lax.all_to_all(student, CHIPS, 0, 0).reshape(2, 3072, 128)
    other = lax.ppermute(own, "c", swap)

    place = jnp.stack([c, yl]).astype(jnp.int32)
    own_mismatch = call(own_mismatch_kernel, shape(256, 256), [SMEM] + [VMEM] * 3, (place, own, projector_t, teacher_t), 24, 4 * 10 ** 8)
    mismatch, sent = call(
        sent_kernel,
        [shape(512, 256), shape(4, 4, 96, 256)],
        [SMEM] + [VMEM] * 5,
        (place, own, other, projector_t, teacher_t, own_mismatch),
        32,
        8 * 10 ** 8,
    )
    received = lax.ppermute(sent, "yl", swap)
    kept = call(kept_kernel, shape(4, 4, 96, 256, dtype=F32), [SMEM] + [VMEM] * 3, (place, own, other, mismatch), 32, 4 * 10 ** 8)
    half = (kept + received.astype(F32)).astype(BF)
    near = jnp.sum(lax.all_to_all(half, "zl", 0, 0).astype(F32), axis=0).astype(BF)
    summed = jnp.sum(lax.all_to_all(near, "zh", 0, 0).astype(F32), axis=0)
    return summed * (16384 ** -0.5), attended


def solution(mesh):
    fine = Mesh(mesh.devices.reshape(4, 4, 2, 2, 2, 2, 2), ("zh", "zl", "yl", "yh", "xh", "xl", "c"))
    return jax.shard_map(
        on_device,
        mesh=fine,
        in_specs=(
            P(CTX, HID),
            P(CTX, None),
            P(CTX, None),
            P(CTX),
            P(CTX, HID),
            P(None, HID),
            P(None, HID),
            P(CTX + HID, None),
        ),
        out_specs=(P(CTX, HID), P(CTX, HID)),
        check_vma=False,
    )
```

```python
import functools

import jax
import jax.numpy as jnp
from jax import lax
from jax.experimental import pallas as pl
from jax.experimental.pallas import tpu as pltpu
from jax.sharding import Mesh
from jax.sharding import PartitionSpec as P

HEAD = 128
SCALE2 = HEAD ** -0.5 * 1.4426950408889634
EMPTY = -1e30
MASKED = -2e30
BF = jnp.bfloat16
F32 = jnp.float32
CTX = ("zh", "zl", "yl")
HID = ("yh", "xh", "xl", "c")
GROUP = ("xl", "c")
OCTET = ("yl", "xl", "c")
HEADSETS = ("yh", "xh")
CHIPS = ("xl", "yh", "xh")
BLOCKS = 4


def pack_kernel(place, keys, values, docs, out):
    rows = jnp.concatenate([docs[...].astype(F32), jnp.zeros((12, 128), F32)], axis=0).astype(BF)
    for copy in range(out.shape[0]):
        out[copy, 0:128, :] = keys[...]
        out[copy, 128:256, :] = values[...]
        out[copy, 256:272, :] = rows


def attend_kernel(sc, kv0, kv1, kv2, kv3, q_own, q_other, qdoc, early1, early2, early3, out, v_turned):
    z, yl, j = sc[144], sc[145], sc[146]
    pieces = (kv0, kv1, kv2, kv3)
    place = [(z + shift) % 4 for shift in (0, 3, 1, 2)]
    for ch in range(4):
        for i in range(BLOCKS):
            v_turned[:, (ch * BLOCKS + i) * 128:(ch * BLOCKS + i + 1) * 128] = pieces[i][ch, 128:256, :].T
    key_iota = lax.broadcasted_iota(jnp.int32, (128, 512), 0)
    row_iota = lax.broadcasted_iota(jnp.int32, (1, 512), 1) % 128
    for side, q_ref in ((0, q_own), (1, q_other)):
        yl_q = yl if side == 0 else 1 - yl
        block_q = 2 * z + yl_q

        def one_tile(rc, carry, side=side, q_ref=q_ref, yl_q=yl_q, block_q=block_q):
            row0 = pl.multiple_of(rc * 128, 128)
            q = jnp.concatenate([q_ref[pl.ds(pl.multiple_of((h ^ j) * 512, 512) + row0, 128), :] for h in range(4)], axis=0)
            docs = qdoc[pl.ds(side * 4 + rc, 1), :]
            docs = jnp.concatenate([docs] * 4, axis=1)
            first, last = sc[128 + side * 4 + rc], sc[136 + side * 4 + rc]
            q_min = block_q * 512 + row0
            q_pos = q_min + row_iota

            def step(ch, state, masked):
                run_max, run_sum, acc = state
                keys = jnp.concatenate([piece[ch, 0:128, :] for piece in pieces], axis=0)
                s = lax.dot_general(keys, q, (((1,), (1,)), ((), ())), preferred_element_type=F32) * SCALE2
                if masked:
                    parts = []
                    for i in range(BLOCKS):
                        low = jnp.zeros((1, 512), jnp.int32)
                        for d in range(8):
                            low = jnp.where(docs == d, sc[i * 32 + ch * 8 + d], low)
                        low = low - j * 128
                        high = q_pos - ((2 * (ch * 4 + place[i]) + yl) * 512 + j * 128)
                        ok = (key_iota >= low) & (key_iota <= high)
                        parts.append(jnp.where(ok, s[i * 128:(i + 1) * 128], MASKED))
                    s = jnp.concatenate(parts, axis=0)
                new_max = jnp.maximum(run_max, jnp.max(s, axis=0, keepdims=True))
                factor = jnp.exp2(run_max - new_max)
                w = jnp.exp2(s - new_max)
                new_sum = run_sum * factor + jnp.sum(w, axis=0, keepdims=True)
                cols = pl.ds(pl.multiple_of(ch * (BLOCKS * 128), BLOCKS * 128), BLOCKS * 128)
                new_acc = acc * factor + jnp.dot(v_turned[:, cols], w.astype(BF), preferred_element_type=F32)
                return new_max, new_sum, new_acc

            def any_step(ch, state):
                most = functools.reduce(jnp.maximum, [sc[i * 32 + ch * 8 + last] for i in range(BLOCKS)])
                k_max = (2 * (ch * BLOCKS + BLOCKS - 1) + yl) * 512 + j * 128 + 127
                full = (k_max <= q_min) & (most <= j * 128)
                return lax.cond(full, functools.partial(step, ch, masked=False), functools.partial(step, ch, masked=True), state)

            begin = jnp.int32(0)
            for ch in range(4):
                fewest = functools.reduce(jnp.minimum, [sc[i * 32 + ch * 8 + first] for i in range(BLOCKS)])
                begin = begin + (fewest >= (j + 1) * 128).astype(jnp.int32)
            end = z // BLOCKS + 1
            state = (jnp.full((1, 512), EMPTY, F32), jnp.zeros((1, 512), F32), jnp.zeros((128, 512), F32))
            run_max, run_sum, acc = lax.fori_loop(begin, end, any_step, state)
            seen = run_sum > 0
            o = (acc * (1.0 / jnp.where(seen, run_sum, 1.0))).astype(BF)
            lse = jnp.where(seen, run_max + jnp.log2(jnp.where(seen, run_sum, 1.0)), EMPTY)
            hi = lse.astype(BF).astype(F32)
            mid = (lse - hi).astype(BF).astype(F32)
            lo = lse - hi - mid
            dest = yl_q * 4 + rc
            rows = [part[:, h * 128:(h + 1) * 128] for part in (hi, mid, lo) for h in range(4)]
            rows.append(jnp.zeros((4, 128), F32))
            for h in range(4):
                out[dest, h * 128:(h + 1) * 128, :] = o[:, h * 128:(h + 1) * 128]
            out[dest, 512:528, :] = jnp.concatenate(rows, axis=0).astype(BF)
            return carry

        lax.fori_loop(0, 4, one_tile, 0)


def combine_kernel(parts, out, copies):
    count = parts.shape[0]
    tails = [parts[s, 512:528, :].astype(F32) for s in range(count)]
    for h in range(4):
        lses = [t[h:h + 1] + t[4 + h:5 + h] + t[8 + h:9 + h] for t in tails]
        top = functools.reduce(jnp.maximum, lses)
        weights = [jnp.exp2(v - top) for v in lses]
        inverse = 1.0 / sum(weights)
        rows = slice(h * 128, (h + 1) * 128)
        total = sum(w * inverse * parts[s, rows, :].astype(F32) for s, w in enumerate(weights)).astype(BF)
        out[rows, :] = total
        for copy in range(copies.shape[0]):
            copies[copy, rows, :] = total


def student_kernel(weight_t, att, hidden_t, out):
    att_all = att[...].reshape(2048, 128)
    for part in range(4):
        rows = slice(part * 192, (part + 1) * 192)
        mixed = jnp.dot(weight_t[rows, :], att_all, preferred_element_type=F32)
        student = (hidden_t[rows, :].astype(F32) + mixed).astype(BF)
        for copy in range(out.shape[0]):
            out[copy, rows, :] = student


def mismatch_of(student, projector_t, teacher_t, core):
    both = jnp.concatenate([student[0], student[1]], axis=1)
    projected = jnp.dot(projector_t[...], both, preferred_element_type=F32)
    taught = [teacher_t[:, pl.ds(pl.multiple_of((xl * 2 + core) * 128, 128), 128)] for xl in range(2)]
    return (projected - jnp.concatenate(taught, axis=1).astype(F32)).astype(BF)


def gradient_rows(own, other, turned, near):
    rows = []
    for zh in range(4):
        start = pl.multiple_of((zh * 4 + near) * 192, 64)
        rows.append(jnp.concatenate([ref[xl, pl.ds(start, 192), :] for ref in (own, other) for xl in range(2)], axis=1))
    return jnp.dot(jnp.concatenate(rows, axis=0), turned[...], preferred_element_type=F32).reshape(8, 96, 256)


def own_mismatch_kernel(place, own, projector_t, teacher_t, out):
    out[...] = mismatch_of(own, projector_t, teacher_t, place[0]).T


def second_kernel(place, own, other, projector_t, teacher_t, own_mismatch, mismatch, up, down):
    mismatch[0:256, :] = own_mismatch[...]
    mismatch[256:512, :] = mismatch_of(other, projector_t, teacher_t, 1 - place[0]).T
    grad = gradient_rows(own, other, mismatch, (place[1] + 2) % 4).astype(BF)
    up[...] = grad[0:4]
    down[...] = grad[4:8]


def first_kernel(place, own, other, mismatch, up, down):
    up[...] = gradient_rows(own, other, mismatch, (place[1] + 1) % 4).astype(BF)
    down[...] = gradient_rows(own, other, mismatch, (place[1] + 3) % 4).astype(BF)


def kept_kernel(place, own, other, mismatch, out):
    out[...] = gradient_rows(own, other, mismatch, place[1])


def add_kernel(kept, below, above, far_below, far_above, out):
    near = kept[...] + below[...].astype(F32) + above[...].astype(F32)
    out[0:4] = (near[0:4] + far_below[...].astype(F32)).astype(BF)
    out[4:8] = (near[4:8] + far_above[...].astype(F32)).astype(BF)


def side_kernel(teacher, hidden_t, early, teacher_out, hidden_out):
    for part in range(16):
        teacher_out[part] = teacher[:, part * 256:(part + 1) * 256]
    for part in range(4):
        hidden_out[part] = hidden_t[:, part * 128:(part + 1) * 128]


VMEM = pl.BlockSpec(memory_space=pltpu.VMEM)
SMEM = pl.BlockSpec(memory_space=pltpu.SMEM)
ANY = pl.BlockSpec(memory_space=pl.ANY)


def call(kernel, out_shape, specs, operands, limit, flops=0, scratch=()):
    single = not isinstance(out_shape, list)
    return pl.pallas_call(
        kernel,
        out_shape=out_shape,
        in_specs=specs,
        out_specs=VMEM if single else [VMEM] * len(out_shape),
        scratch_shapes=list(scratch),
        compiler_params=pltpu.CompilerParams(vmem_limit_bytes=limit * 1024 * 1024),
        cost_estimate=pl.CostEstimate(flops=flops, bytes_accessed=4 * 1024 * 1024, transcendentals=0),
    )(*operands)


def shape(*dims, dtype=BF):
    return jax.ShapeDtypeStruct(dims, dtype)


def pack(place, keys, values, docs):
    return pl.pallas_call(
        pack_kernel,
        grid_spec=pltpu.PrefetchScalarGridSpec(
            num_scalar_prefetch=1,
            grid=(1,),
            in_specs=[
                pl.BlockSpec((128, 128), lambda i, place: (place[0], place[1])),
                pl.BlockSpec((128, 128), lambda i, place: (place[0], place[1])),
                pl.BlockSpec((4, 128), lambda i, place: (0, 0)),
            ],
            out_specs=pl.BlockSpec((4, 272, 128), lambda i, place: (0, 0, 0)),
        ),
        out_shape=shape(4, 272, 128),
    )(place, keys, values, docs)


def on_device(queries, keys, values, doc_ids, hidden, out_weight, projector, teacher):
    zl, yl, c = lax.axis_index("zl"), lax.axis_index("yl"), lax.axis_index("c")
    z = lax.axis_index("zh") * 4 + zl
    g = lax.axis_index("yh") * 2 + lax.axis_index("xh")
    j = lax.axis_index("xl") * 2 + c
    swap = [(0, 1), (1, 0)]

    def from_z(x, shift):
        return lax.ppermute(x, ("zh", "zl"), [((i + shift) % 16, i) for i in range(16)])

    docs = doc_ids.reshape(4, 128)
    packed = pack(jnp.stack([j, g]).astype(jnp.int32), keys, values, docs)
    kv_own = lax.all_to_all(packed, "zh", 0, 0)
    kv_below, kv_above = from_z(kv_own, -1), from_z(kv_own, 1)
    kv_far = jnp.concatenate([from_z(kv_own[0:2], -2), from_z(kv_own[2:4], 2)], axis=0)

    doc_rows = jnp.pad(docs.astype(BF), ((0, 12), (0, 0)))
    q_two = jnp.concatenate([queries, lax.ppermute(queries, "c", swap)], axis=0)
    q_own = jnp.concatenate([q_two, lax.ppermute(q_two, "xl", swap), doc_rows], axis=0)
    q_other = lax.ppermute(q_own, "yl", swap)

    weight_t = lax.all_gather(out_weight.T, GROUP, axis=0, tiled=True)
    teacher_cols, hidden_cut = call(
        side_kernel, [shape(16, 32, 256), shape(4, 192, 128)], [VMEM, VMEM, ANY], (teacher, hidden.T, kv_own), 8
    )
    hidden_t = lax.all_to_all(hidden_cut, GROUP, 0, 0).reshape(768, 128)
    teacher_t = lax.all_to_all(teacher_cols, HID, 0, 0).reshape(512, 256).T
    projector_t = projector.T

    pieces = (kv_own, kv_below, kv_above, kv_far)
    docs_z = jnp.stack([piece[:, 256:260, :].reshape(4, 512) for piece in pieces]).astype(jnp.int32)
    counts = jnp.sum(docs_z[:, :, None, :] < jnp.arange(8, dtype=jnp.int32)[None, None, :, None], axis=3, dtype=jnp.int32)
    q_docs = jnp.concatenate([docs, q_other[2048:2052].astype(jnp.int32)], axis=0)
    scalars = jnp.concatenate([counts.reshape(128), q_docs[:, 0], q_docs[:, 127], jnp.stack([z, yl, j]).astype(jnp.int32)])
    partial = call(
        attend_kernel,
        shape(8, 528, 128),
        [SMEM] + [VMEM] * 7 + [ANY] * 3,
        (scalars, *pieces, q_own, q_other, q_docs, hidden_t, teacher_t, projector_t),
        40,
        scratch=[pltpu.VMEM((128, 2048), BF)],
    )
    att_rows, att_copies = call(
        combine_kernel, [shape(512, 128), shape(4, 512, 128)], [VMEM], (lax.all_to_all(partial, OCTET, 0, 0),), 16
    )

    att_head = lax.all_to_all(att_rows.reshape(4, 128, 128), GROUP, 0, 0)
    attended = jnp.transpose(att_head, (0, 2, 1)).reshape(512, 128)

    att_all = lax.all_to_all(att_copies, HEADSETS, 0, 0)
    student = call(student_kernel, shape(8, 768, 128), [VMEM] * 3, (weight_t, att_all, hidden_t), 24)
    own = lax.all_to_all(student, CHIPS, 0, 0).reshape(2, 3072, 128)
    other = lax.ppermute(own, "c", swap)

    place = jnp.stack([c, zl]).astype(jnp.int32)
    own_mismatch = call(own_mismatch_kernel, shape(256, 256), [SMEM] + [VMEM] * 3, (place, own, projector_t, teacher_t), 24, 4 * 10 ** 8)
    mismatch, up, down = call(
        second_kernel,
        [shape(512, 256), shape(4, 96, 256), shape(4, 96, 256)],
        [SMEM] + [VMEM] * 5,
        (place, own, other, projector_t, teacher_t, own_mismatch),
        32,
        8 * 10 ** 8,
    )
    far_below, far_above = from_z(up, -2), from_z(down, 2)
    up, down = call(
        first_kernel, [shape(8, 96, 256), shape(8, 96, 256)], [SMEM] + [VMEM] * 3, (place, own, other, mismatch), 32, 4 * 10 ** 8
    )
    below, above = from_z(up, -1), from_z(down, 1)
    kept = call(kept_kernel, shape(8, 96, 256, dtype=F32), [SMEM] + [VMEM] * 3, (place, own, other, mismatch), 32, 2 * 10 ** 8)
    near = call(add_kernel, shape(8, 96, 256), [VMEM] * 5, (kept, below, above, far_below, far_above), 16)
    summed = jnp.sum(lax.all_to_all(near, ("zh", "yl"), 0, 0).astype(F32), axis=0)
    return summed * (16384 ** -0.5), attended


def solution(mesh):
    fine = Mesh(mesh.devices.reshape(4, 4, 2, 2, 2, 2, 2), ("zh", "zl", "yl", "yh", "xh", "xl", "c"))
    return jax.shard_map(
        on_device,
        mesh=fine,
        in_specs=(
            P(CTX, HID),
            P(CTX, None),
            P(CTX, None),
            P(CTX),
            P(CTX, HID),
            P(None, HID),
            P(None, HID),
            P(CTX + HID, None),
        ),
        out_specs=(P(CTX, HID), P(CTX, HID)),
        check_vma=False,
    )
```

```python
import functools

import jax
import jax.numpy as jnp
from jax import lax
from jax.experimental import pallas as pl
from jax.experimental.pallas import tpu as pltpu
from jax.sharding import Mesh
from jax.sharding import PartitionSpec as P

HEAD = 128
SCALE2 = HEAD ** -0.5 * 1.4426950408889634
EMPTY = -1e30
MASKED = -2e30
BF = jnp.bfloat16
F32 = jnp.float32
CTX = ("zh", "zl", "yl")
HID = ("yh", "xh", "xl", "c")
GROUP = ("xl", "c")
OCTET = ("yl", "xl", "c")
HEADSETS = ("yh", "xh")
CHIPS = ("xl", "yh", "xh")
BLOCKS = 4


def start_kernel(place, keys, values, docs, hidden_t, queries, packed, doc_rows, kept, sent, q_out):
    rows = jnp.concatenate([docs[...].astype(F32), jnp.zeros((12, 128), F32)], axis=0).astype(BF)
    doc_rows[...] = rows
    for copy in range(4):
        packed[copy, 0:128, :] = keys[...]
        packed[copy, 128:256, :] = values[...]
        packed[copy, 256:272, :] = rows
    q_out[...] = queries[...]
    core = place[2]
    for xl in range(2):
        kept[xl] = hidden_t[:, pl.ds(pl.multiple_of((xl * 2 + core) * 128, 128), 128)]
        sent[xl] = hidden_t[:, pl.ds(pl.multiple_of((xl * 2 + 1 - core) * 128, 128), 128)]


def turn_kernel(place, kept, received, kept_out, sent_out):
    xl = place[3]
    for i, ref in enumerate((kept, received)):
        kept_out[i] = ref[xl]
        sent_out[i] = ref[1 - xl]


def attend_kernel(place, kv0, kv1, kv2, kv3_low, kv3_high, q_own, q_other, docs, early1, early2, early3, out, kv, q_all, v_turned, s_buf, info_v, info, sem):
    j, yl, z = place[0], place[4], place[5]
    copies = [
        pltpu.make_async_copy(src, dst, sem.at[i])
        for i, (src, dst) in enumerate((
            (kv0, kv.at[0]), (kv1, kv.at[1]), (kv2, kv.at[2]), (kv3_low, kv.at[3, pl.ds(0, 2)]), (kv3_high, kv.at[3, pl.ds(2, 2)]),
            (q_own, q_all.at[0]), (q_other, q_all.at[1]),
        ))
    ]
    for copy in copies:
        copy.start()
    for copy in copies:
        copy.wait()
    info_v[16:20, :] = docs[...]
    info_v[20:24, :] = q_all[1, 2048:2064, :].astype(F32)[0:4].astype(jnp.int32)
    block_docs = []
    for ch in range(4):
        for i in range(BLOCKS):
            rows = kv[i, ch, 256:272, :].astype(F32)
            block_docs.append(jnp.concatenate([rows[r:r + 1] for r in range(4)], axis=1))
    block_docs = jnp.concatenate(block_docs, axis=0)
    lane = lax.broadcasted_iota(jnp.int32, (16, 128), 1)
    counts = jnp.zeros((16, 128), F32)
    for d in range(8):
        below = jnp.sum((block_docs < d).astype(F32), axis=1, keepdims=True)
        counts = jnp.where(lane == d, below, counts)
    info_v[0:16, :] = counts.astype(jnp.int32)
    to_scalars = pltpu.make_async_copy(info_v, info, sem.at[7])
    to_scalars.start()
    for ch in range(4):
        for i in range(BLOCKS):
            v_turned[:, (ch * BLOCKS + i) * 128:(ch * BLOCKS + i + 1) * 128] = kv[i, ch, 128:256, :].T
    to_scalars.wait()
    where = [(z + shift) % 4 for shift in (0, 3, 1, 2)]
    key_iota = lax.broadcasted_iota(jnp.int32, (128, 512), 0)
    row_iota = lax.broadcasted_iota(jnp.int32, (1, 512), 1) % 128

    def one_tile(tile, carry):
        side, rc = tile // 4, tile % 4
        yl_q = jnp.where(side == 0, yl, 1 - yl)
        row0 = pl.multiple_of(rc * 128, 128)
        q = jnp.concatenate([q_all[side, pl.ds(pl.multiple_of((h ^ j) * 512, 512) + row0, 128), :] for h in range(4)], axis=0)
        row_docs = jnp.concatenate([info_v[pl.ds(16 + tile, 1), :]] * 4, axis=1)
        first, last = info[16 + tile, 0], info[16 + tile, 127]
        q_min = (2 * z + yl_q) * 512 + row0
        q_pos = q_min + row_iota

        def scores(ch):
            keys = jnp.concatenate([kv[i, ch, 0:128, :] for i in range(BLOCKS)], axis=0)
            return lax.dot_general(keys, q, (((1,), (1,)), ((), ())), preferred_element_type=F32) * SCALE2

        def mask(ch, s):
            parts = []
            for i in range(BLOCKS):
                low = jnp.zeros((1, 512), jnp.int32)
                for d in range(8):
                    low = jnp.where(row_docs == d, info[ch * BLOCKS + i, d], low)
                low = low - j * 128
                high = q_pos - ((2 * (ch * 4 + where[i]) + yl) * 512 + j * 128)
                ok = (key_iota >= low) & (key_iota <= high)
                parts.append(jnp.where(ok, s[i * 128:(i + 1) * 128], MASKED))
            return jnp.concatenate(parts, axis=0)

        def find_max(ch, run_max):
            most = functools.reduce(jnp.maximum, [info[ch * BLOCKS + i, last] for i in range(BLOCKS)])
            k_max = (2 * (ch * BLOCKS + BLOCKS - 1) + yl) * 512 + j * 128 + 127
            full = (k_max <= q_min) & (most <= j * 128)

            def keep(s):
                s_buf[ch] = s
                return jnp.max(s, axis=0, keepdims=True)

            return jnp.maximum(run_max, lax.cond(full, lambda: keep(scores(ch)), lambda: keep(mask(ch, scores(ch)))))

        def add_up(ch, state):
            run_sum, acc = state
            w = jnp.exp2(s_buf[ch] - run_max)
            cols = pl.ds(pl.multiple_of(ch * (BLOCKS * 128), BLOCKS * 128), BLOCKS * 128)
            blended = jnp.dot(v_turned[:, cols], w.astype(BF), preferred_element_type=F32)
            return run_sum + jnp.sum(w, axis=0, keepdims=True), acc + blended

        begin = jnp.int32(0)
        for ch in range(4):
            fewest = functools.reduce(jnp.minimum, [info[ch * BLOCKS + i, first] for i in range(BLOCKS)])
            begin = begin + (fewest >= (j + 1) * 128).astype(jnp.int32)
        end = z // BLOCKS + 1
        run_max = lax.fori_loop(begin, end, find_max, jnp.full((1, 512), EMPTY, F32))
        run_sum, acc = lax.fori_loop(begin, end, add_up, (jnp.zeros((1, 512), F32), jnp.zeros((128, 512), F32)))
        seen = run_sum > 0
        o = (acc * (1.0 / jnp.where(seen, run_sum, 1.0))).astype(BF)
        lse = jnp.where(seen, run_max + jnp.log2(jnp.where(seen, run_sum, 1.0)), EMPTY)
        hi = lse.astype(BF).astype(F32)
        mid = (lse - hi).astype(BF).astype(F32)
        lo = lse - hi - mid
        dest = yl_q * 4 + rc
        rows = [part[:, h * 128:(h + 1) * 128] for part in (hi, mid, lo) for h in range(4)]
        rows.append(jnp.zeros((4, 128), F32))
        for h in range(4):
            out[dest, h * 128:(h + 1) * 128, :] = o[:, h * 128:(h + 1) * 128]
        out[dest, 512:528, :] = jnp.concatenate(rows, axis=0).astype(BF)
        return carry

    lax.fori_loop(0, 8, one_tile, 0)


def combine_kernel(parts, out, copies):
    count = parts.shape[0]
    tails = [parts[s, 512:528, :].astype(F32) for s in range(count)]
    for h in range(4):
        lses = [t[h:h + 1] + t[4 + h:5 + h] + t[8 + h:9 + h] for t in tails]
        top = functools.reduce(jnp.maximum, lses)
        weights = [jnp.exp2(v - top) for v in lses]
        inverse = 1.0 / sum(weights)
        rows = slice(h * 128, (h + 1) * 128)
        total = sum(w * inverse * parts[s, rows, :].astype(F32) for s, w in enumerate(weights)).astype(BF)
        out[rows, :] = total
        for copy in range(copies.shape[0]):
            copies[copy, rows, :] = total


def student_kernel(place, weight_t, att, kept, received, teacher, out):
    part = pl.program_id(0)

    @pl.when(part == 0)
    def _():
        for chip in range(8):
            first = (chip % 4 * 4 + chip // 4 * 2) * 256
            for i in range(4):
                out[chip, 768 + i * 32:800 + i * 32, :] = teacher[:, first + i * 128:first + (i + 1) * 128]

    source = part ^ place[0]
    hidden = jnp.where(source < 2, kept[source % 2].astype(F32), received[source % 2].astype(F32))
    mixed = jnp.dot(weight_t[...], att[...].reshape(2048, 128), preferred_element_type=F32)
    student = (hidden + mixed).astype(BF)
    for copy in range(out.shape[0]):
        out[copy, pl.ds(pl.multiple_of(part * 192, 64), 192), :] = student


def projected(student, projector_t):
    total = 0.0
    for g in range(4):
        both = jnp.concatenate([student[g, 0:768, :], student[4 + g, 0:768, :]], axis=1)
        total = total + jnp.dot(projector_t[:, g * 768:(g + 1) * 768], both, preferred_element_type=F32)
    return total


def teacher_rows(own, other, core, chunk_core):
    pieces = []
    for xl in range(2):
        for t in range(4):
            source = t // 2 * 4 + xl * 2 + chunk_core
            halves = []
            for i in range(2):
                rows = pl.ds(pl.multiple_of(768 + core * 64 + i * 32, 32), 32)
                halves.append(jnp.where(core == t % 2, own[source, rows, :].astype(F32), other[source, rows, :].astype(F32)))
            pieces.append(jnp.concatenate(halves, axis=1))
    return jnp.concatenate(pieces, axis=0)


def gradient_rows(own, other, mismatch, near):
    rows = []
    for zh in range(4):
        cut = pl.ds(pl.multiple_of(near * 192, 64), 192)
        rows.append(jnp.concatenate([ref[xl * 4 + zh, cut, :] for ref in (own, other) for xl in range(2)], axis=1))
    return jnp.dot(jnp.concatenate(rows, axis=0), mismatch[...], preferred_element_type=F32).reshape(8, 96, 256)


def own_projected_kernel(own, projector_t, out):
    out[...] = projected(own, projector_t).T


def second_kernel(place, own, other, projector_t, own_projected, mismatch, up, down):
    core = place[2]
    mismatch[0:256, :] = (own_projected[...] - teacher_rows(own, other, core, core)).astype(BF)
    mismatch[256:512, :] = (projected(other, projector_t).T - teacher_rows(own, other, core, 1 - core)).astype(BF)
    grad = gradient_rows(own, other, mismatch, (place[6] + 2) % 4).astype(BF)
    up[...] = grad[0:4]
    down[...] = grad[4:8]


def first_kernel(place, own, other, mismatch, up, down):
    up[...] = gradient_rows(own, other, mismatch, (place[6] + 1) % 4).astype(BF)
    down[...] = gradient_rows(own, other, mismatch, (place[6] + 3) % 4).astype(BF)


def kept_kernel(place, own, other, mismatch, out):
    out[...] = gradient_rows(own, other, mismatch, place[6])


def add_kernel(kept, below, above, far_below, far_above, out):
    near = kept[...] + below[...].astype(F32) + above[...].astype(F32)
    out[0:4] = (near[0:4] + far_below[...].astype(F32)).astype(BF)
    out[4:8] = (near[4:8] + far_above[...].astype(F32)).astype(BF)


def final_kernel(terms, out):
    out[...] = sum(terms[i].astype(F32) for i in range(terms.shape[0])) * (16384 ** -0.5)


VMEM = pl.BlockSpec(memory_space=pltpu.VMEM)
SMEM = pl.BlockSpec(memory_space=pltpu.SMEM)
ANY = pl.BlockSpec(memory_space=pl.ANY)


def call(kernel, out_shape, specs, operands, limit, flops=0, scratch=()):
    single = not isinstance(out_shape, list)
    return pl.pallas_call(
        kernel,
        out_shape=out_shape,
        in_specs=specs,
        out_specs=VMEM if single else [VMEM] * len(out_shape),
        scratch_shapes=list(scratch),
        compiler_params=pltpu.CompilerParams(vmem_limit_bytes=limit * 1024 * 1024),
        cost_estimate=pl.CostEstimate(flops=flops, bytes_accessed=4 * 1024 * 1024, transcendentals=0),
    )(*operands)


def shape(*dims, dtype=BF):
    return jax.ShapeDtypeStruct(dims, dtype)


def start(place, keys, values, docs, hidden_t, queries):
    def block(*dims):
        return pl.BlockSpec(dims, lambda i, place: (0,) * len(dims))

    picked = pl.BlockSpec((128, 128), lambda i, place: (place[0], place[1]))
    outs = [(4, 272, 128), (16, 128), (2, 192, 128), (2, 192, 128), (512, 128)]
    return pl.pallas_call(
        start_kernel,
        grid_spec=pltpu.PrefetchScalarGridSpec(
            num_scalar_prefetch=1,
            grid=(1,),
            in_specs=[picked, picked, block(4, 128), block(192, 512), block(512, 128)],
            out_specs=[block(*dims) for dims in outs],
        ),
        out_shape=[shape(*dims) for dims in outs],
    )(place, keys, values, docs, hidden_t, queries)


def student_of(place, weight_t, att, kept, received, teacher):
    def block(*dims):
        return pl.BlockSpec(dims, lambda i: (0,) * len(dims))

    return pl.pallas_call(
        student_kernel,
        grid=(4,),
        out_shape=shape(8, 896, 128),
        in_specs=[
            SMEM, pl.BlockSpec((192, 2048), lambda i: (i, 0)), block(4, 512, 128), block(2, 192, 128), block(2, 192, 128), block(32, 4096),
        ],
        out_specs=block(8, 896, 128),
        compiler_params=pltpu.CompilerParams(vmem_limit_bytes=24 * 1024 * 1024),
    )(place, weight_t, att, kept, received, teacher)


def on_device(queries, keys, values, doc_ids, hidden, out_weight, projector, teacher):
    zl, yl, xl, c = lax.axis_index("zl"), lax.axis_index("yl"), lax.axis_index("xl"), lax.axis_index("c")
    z = lax.axis_index("zh") * 4 + zl
    g = lax.axis_index("yh") * 2 + lax.axis_index("xh")
    swap = [(0, 1), (1, 0)]
    place = jnp.stack([xl * 2 + c, g, c, xl, yl, z, zl]).astype(jnp.int32)

    def from_z(x, shift):
        return lax.ppermute(x, ("zh", "zl"), [((i + shift) % 16, i) for i in range(16)])

    docs = doc_ids.reshape(4, 128)
    packed, doc_rows, hidden_kept, hidden_sent, q_first = start(place, keys, values, docs, hidden.T, queries)
    kv_own = lax.all_to_all(packed, "zh", 0, 0)
    kv_below, kv_above = from_z(kv_own, -1), from_z(kv_own, 1)
    kv_low, kv_high = from_z(kv_own[0:2], -2), from_z(kv_own[2:4], 2)

    q_two = jnp.concatenate([q_first, lax.ppermute(q_first, "c", swap)], axis=0)
    q_own = jnp.concatenate([q_two, lax.ppermute(q_two, "xl", swap), doc_rows], axis=0)
    q_other = lax.ppermute(q_own, "yl", swap)
    half = shape(2, 192, 128)
    hidden_kept, hidden_sent = call(
        turn_kernel, [half, half], [SMEM, VMEM, VMEM], (place, hidden_kept, lax.ppermute(hidden_sent, "c", swap)), 8
    )
    hidden_received = lax.ppermute(hidden_sent, "xl", swap)

    weight_t = lax.all_gather(out_weight.T, GROUP, axis=0, tiled=True)
    projector_t = projector.T

    partial = call(
        attend_kernel,
        shape(8, 528, 128),
        [SMEM] + [ANY] * 7 + [VMEM] + [ANY] * 3,
        (place, kv_own, kv_below, kv_above, kv_low, kv_high, q_own, q_other, docs, hidden_kept, hidden_received, projector_t),
        40,
        2 * 10 ** 10,
        scratch=[
            pltpu.VMEM((4, 4, 272, 128), BF),
            pltpu.VMEM((2, 2064, 128), BF),
            pltpu.VMEM((128, 2048), BF),
            pltpu.VMEM((4, 512, 512), F32),
            pltpu.VMEM((24, 128), jnp.int32),
            pltpu.SMEM((24, 128), jnp.int32),
            pltpu.SemaphoreType.DMA((8,)),
        ],
    )
    att_rows, att_copies = call(
        combine_kernel, [shape(512, 128), shape(4, 512, 128)], [VMEM], (lax.all_to_all(partial, OCTET, 0, 0),), 16
    )

    att_head = lax.all_to_all(att_rows.reshape(4, 128, 128), GROUP, 0, 0)
    attended = jnp.transpose(att_head, (0, 2, 1)).reshape(512, 128)

    att_all = lax.all_to_all(att_copies, HEADSETS, 0, 0)
    student = student_of(place, weight_t, att_all, hidden_kept, hidden_received, teacher)
    own = lax.all_to_all(student, CHIPS, 0, 0)
    other = lax.ppermute(own, "c", swap)

    own_projected = call(own_projected_kernel, shape(256, 256, dtype=F32), [VMEM] * 2, (own, projector_t), 24, 4 * 10 ** 8)
    mismatch, up, down = call(
        second_kernel,
        [shape(512, 256), shape(4, 96, 256), shape(4, 96, 256)],
        [SMEM] + [VMEM] * 4,
        (place, own, other, projector_t, own_projected),
        32,
        8 * 10 ** 8,
    )
    far_below, far_above = from_z(up, -2), from_z(down, 2)
    up, down = call(
        first_kernel, [shape(8, 96, 256), shape(8, 96, 256)], [SMEM] + [VMEM] * 3, (place, own, other, mismatch), 32, 4 * 10 ** 8
    )
    below, above = from_z(up, -1), from_z(down, 1)
    kept = call(kept_kernel, shape(8, 96, 256, dtype=F32), [SMEM] + [VMEM] * 3, (place, own, other, mismatch), 32, 2 * 10 ** 8)
    near = call(add_kernel, shape(8, 96, 256), [VMEM] * 5, (kept, below, above, far_below, far_above), 16)
    grad = call(final_kernel, shape(96, 256, dtype=F32), [VMEM], (lax.all_to_all(near, ("zh", "yl"), 0, 0),), 8)
    return grad, attended


def solution(mesh):
    fine = Mesh(mesh.devices.reshape(4, 4, 2, 2, 2, 2, 2), ("zh", "zl", "yl", "yh", "xh", "xl", "c"))
    return jax.shard_map(
        on_device,
        mesh=fine,
        in_specs=(
            P(CTX, HID),
            P(CTX, None),
            P(CTX, None),
            P(CTX),
            P(CTX, HID),
            P(None, HID),
            P(None, HID),
            P(CTX + HID, None),
        ),
        out_specs=(P(CTX, HID), P(CTX, HID)),
        check_vma=False,
    )
```

```python
import functools

import jax
import jax.numpy as jnp
from jax import lax
from jax.experimental import pallas as pl
from jax.experimental.pallas import tpu as pltpu
from jax.sharding import Mesh
from jax.sharding import PartitionSpec as P

HEAD = 128
SCALE2 = HEAD ** -0.5 * 1.4426950408889634
EMPTY = -1e30
MASKED = -2e30
BF = jnp.bfloat16
F32 = jnp.float32
CTX = ("zh", "zl", "yl")
HID = ("yh", "xh", "xl", "c")
GROUP = ("xl", "c")
OCTET = ("yl", "xl", "c")
HEADSETS = ("yh", "xh")
CHIPS = ("xl", "yh", "xh")
BLOCKS = 4


def start_kernel(place, keys, values, docs, queries, packed, q_rows):
    rows = jnp.concatenate([docs[...].astype(F32), jnp.zeros((12, 128), F32)], axis=0).astype(BF)
    for copy in range(4):
        packed[copy, 0:128, :] = keys[...]
        packed[copy, 128:256, :] = values[...]
        packed[copy, 256:272, :] = rows
    q_rows[0:512, :] = queries[...]
    q_rows[512:528, :] = rows


def attend_kernel(place, kv0, kv1, kv2, kv3_low, kv3_high, queries, early, out, kv, q_all, v_turned, s_buf, info_v, info, sem):
    j, yl, z = place[0], place[4], place[5]
    copies = [
        pltpu.make_async_copy(src, dst, sem.at[i])
        for i, (src, dst) in enumerate((
            (kv0, kv.at[0]), (kv1, kv.at[1]), (kv2, kv.at[2]), (kv3_low, kv.at[3, pl.ds(0, 2)]), (kv3_high, kv.at[3, pl.ds(2, 2)]),
            (queries, q_all),
        ))
    ]
    for copy in copies:
        copy.start()
    for copy in copies:
        copy.wait()
    for side in range(2):
        info_v[16 + 4 * side:20 + 4 * side, :] = q_all[4 * side, 512:528, :].astype(F32)[0:4].astype(jnp.int32)
    block_docs = []
    for ch in range(4):
        for i in range(BLOCKS):
            rows = kv[i, ch, 256:272, :].astype(F32)
            block_docs.append(jnp.concatenate([rows[r:r + 1] for r in range(4)], axis=1))
    block_docs = jnp.concatenate(block_docs, axis=0)
    lane = lax.broadcasted_iota(jnp.int32, (16, 128), 1)
    counts = jnp.zeros((16, 128), F32)
    for d in range(8):
        below = jnp.sum((block_docs < d).astype(F32), axis=1, keepdims=True)
        counts = jnp.where(lane == d, below, counts)
    info_v[0:16, :] = counts.astype(jnp.int32)
    to_scalars = pltpu.make_async_copy(info_v, info, sem.at[6])
    to_scalars.start()
    for ch in range(4):
        for i in range(BLOCKS):
            v_turned[:, (ch * BLOCKS + i) * 128:(ch * BLOCKS + i + 1) * 128] = kv[i, ch, 128:256, :].T
    to_scalars.wait()
    where = [(z + shift) % 4 for shift in (0, 3, 1, 2)]
    key_iota = lax.broadcasted_iota(jnp.int32, (128, 512), 0)
    row_iota = lax.broadcasted_iota(jnp.int32, (1, 512), 1) % 128

    def one_tile(tile, carry):
        yl_q, rc = tile // 4, tile % 4
        row0 = pl.multiple_of(rc * 128, 128)
        q = jnp.concatenate([q_all[yl_q * 4 + h, pl.ds(row0, 128), :] for h in range(4)], axis=0)
        row_docs = jnp.concatenate([info_v[pl.ds(16 + tile, 1), :]] * 4, axis=1)
        first, last = info[16 + tile, 0], info[16 + tile, 127]
        q_min = (2 * z + yl_q) * 512 + row0
        q_pos = q_min + row_iota

        def scores(ch):
            keys = jnp.concatenate([kv[i, ch, 0:128, :] for i in range(BLOCKS)], axis=0)
            return lax.dot_general(keys, q, (((1,), (1,)), ((), ())), preferred_element_type=F32) * SCALE2

        def mask(ch, s):
            parts = []
            for i in range(BLOCKS):
                low = jnp.zeros((1, 512), jnp.int32)
                for d in range(8):
                    low = jnp.where(row_docs == d, info[ch * BLOCKS + i, d], low)
                low = low - j * 128
                high = q_pos - ((2 * (ch * 4 + where[i]) + yl) * 512 + j * 128)
                ok = (key_iota >= low) & (key_iota <= high)
                parts.append(jnp.where(ok, s[i * 128:(i + 1) * 128], MASKED))
            return jnp.concatenate(parts, axis=0)

        def find_max(ch, run_max):
            most = functools.reduce(jnp.maximum, [info[ch * BLOCKS + i, last] for i in range(BLOCKS)])
            k_max = (2 * (ch * BLOCKS + BLOCKS - 1) + yl) * 512 + j * 128 + 127
            full = (k_max <= q_min) & (most <= j * 128)

            def keep(s):
                s_buf[ch] = s
                return jnp.max(s, axis=0, keepdims=True)

            return jnp.maximum(run_max, lax.cond(full, lambda: keep(scores(ch)), lambda: keep(mask(ch, scores(ch)))))

        def add_up(ch, state):
            run_sum, acc = state
            w = jnp.exp2(s_buf[ch] - run_max)
            cols = pl.ds(pl.multiple_of(ch * (BLOCKS * 128), BLOCKS * 128), BLOCKS * 128)
            blended = jnp.dot(v_turned[:, cols], w.astype(BF), preferred_element_type=F32)
            return run_sum + jnp.sum(w, axis=0, keepdims=True), acc + blended

        begin = jnp.int32(0)
        for ch in range(4):
            fewest = functools.reduce(jnp.minimum, [info[ch * BLOCKS + i, first] for i in range(BLOCKS)])
            begin = begin + (fewest >= (j + 1) * 128).astype(jnp.int32)
        end = z // BLOCKS + 1
        run_max = lax.fori_loop(begin, end, find_max, jnp.full((1, 512), EMPTY, F32))
        run_sum, acc = lax.fori_loop(begin, end, add_up, (jnp.zeros((1, 512), F32), jnp.zeros((128, 512), F32)))
        seen = run_sum > 0
        o = (acc * (1.0 / jnp.where(seen, run_sum, 1.0))).astype(BF)
        lse = jnp.where(seen, run_max + jnp.log2(jnp.where(seen, run_sum, 1.0)), EMPTY)
        hi = lse.astype(BF).astype(F32)
        mid = (lse - hi).astype(BF).astype(F32)
        lo = lse - hi - mid
        rows = [part[:, h * 128:(h + 1) * 128] for part in (hi, mid, lo) for h in range(4)]
        rows.append(jnp.zeros((4, 128), F32))
        for h in range(4):
            out[tile, h * 128:(h + 1) * 128, :] = o[:, h * 128:(h + 1) * 128]
        out[tile, 512:528, :] = jnp.concatenate(rows, axis=0).astype(BF)
        return carry

    lax.fori_loop(0, 8, one_tile, 0)


def combine_kernel(parts, out, copies):
    count = parts.shape[0]
    tails = [parts[s, 512:528, :].astype(F32) for s in range(count)]
    for h in range(4):
        lses = [t[h:h + 1] + t[4 + h:5 + h] + t[8 + h:9 + h] for t in tails]
        top = functools.reduce(jnp.maximum, lses)
        weights = [jnp.exp2(v - top) for v in lses]
        inverse = 1.0 / sum(weights)
        rows = slice(h * 128, (h + 1) * 128)
        total = sum(w * inverse * parts[s, rows, :].astype(F32) for s, w in enumerate(weights)).astype(BF)
        out[rows, :] = total
        for copy in range(copies.shape[0]):
            copies[copy, rows, :] = total


def student_kernel(place, gathered, att, teacher, out, weights, hidden, sem):
    copies = []
    own_rows = pl.ds(pl.multiple_of(2048 + place[0] * 128, 128), 128)
    hidden_copy = pltpu.make_async_copy(gathered.at[:, own_rows], hidden, sem.at[4])
    for part in range(4):
        rows = pl.ds(part * 192, 192)
        copies.append(pltpu.make_async_copy(gathered.at[rows, pl.ds(0, 2048)], weights.at[rows], sem.at[part]))
    copies[0].start()
    hidden_copy.start()
    for copy in copies[1:]:
        copy.start()
    for chip in range(8):
        first = (chip % 4 * 4 + chip // 4 * 2) * 256
        for i in range(4):
            out[chip, 768 + i * 32:800 + i * 32, :] = teacher[:, first + i * 128:first + (i + 1) * 128]
    att_all = att[...].reshape(2048, 128)
    hidden_copy.wait()
    for part in range(4):
        copies[part].wait()
        rows = slice(part * 192, (part + 1) * 192)
        mixed = jnp.dot(weights[rows, :], att_all, preferred_element_type=F32)
        student = (hidden[rows, :].astype(F32) + mixed).astype(BF)
        for copy in range(8):
            out[copy, rows, :] = student


def projected(student, projector_t):
    total = 0.0
    for g in range(4):
        both = jnp.concatenate([student[g, 0:768, :], student[4 + g, 0:768, :]], axis=1)
        total = total + jnp.dot(projector_t[:, g * 768:(g + 1) * 768], both, preferred_element_type=F32)
    return total


def teacher_rows(own, other, core, chunk_core):
    pieces = []
    for xl in range(2):
        for t in range(4):
            source = t // 2 * 4 + xl * 2 + chunk_core
            halves = []
            for i in range(2):
                rows = pl.ds(pl.multiple_of(768 + core * 64 + i * 32, 32), 32)
                halves.append(jnp.where(core == t % 2, own[source, rows, :].astype(F32), other[source, rows, :].astype(F32)))
            pieces.append(jnp.concatenate(halves, axis=1))
    return jnp.concatenate(pieces, axis=0)


def gradient_rows(own, other, mismatch, near):
    rows = []
    for zh in range(4):
        cut = pl.ds(pl.multiple_of(near * 192, 64), 192)
        rows.append(jnp.concatenate([ref[xl * 4 + zh, cut, :] for ref in (own, other) for xl in range(2)], axis=1))
    return jnp.dot(jnp.concatenate(rows, axis=0), mismatch[...], preferred_element_type=F32).reshape(8, 96, 256)


def own_projected_kernel(own, projector_t, out):
    out[...] = projected(own, projector_t).T


def second_kernel(place, own, other, projector_t, own_projected, mismatch, up, down):
    core = place[2]
    mismatch[0:256, :] = (own_projected[...] - teacher_rows(own, other, core, core)).astype(BF)
    mismatch[256:512, :] = (projected(other, projector_t).T - teacher_rows(own, other, core, 1 - core)).astype(BF)
    grad = gradient_rows(own, other, mismatch, (place[6] + 2) % 4).astype(BF)
    up[...] = grad[0:4]
    down[...] = grad[4:8]


def first_kernel(place, own, other, mismatch, up, down):
    up[...] = gradient_rows(own, other, mismatch, (place[6] + 1) % 4).astype(BF)
    down[...] = gradient_rows(own, other, mismatch, (place[6] + 3) % 4).astype(BF)


def kept_kernel(place, own, other, mismatch, out):
    out[...] = gradient_rows(own, other, mismatch, place[6])


def add_kernel(kept, below, above, far_below, far_above, out):
    near = kept[...] + below[...].astype(F32) + above[...].astype(F32)
    out[0:4] = (near[0:4] + far_below[...].astype(F32)).astype(BF)
    out[4:8] = (near[4:8] + far_above[...].astype(F32)).astype(BF)


def final_kernel(terms, out):
    out[...] = sum(terms[i].astype(F32) for i in range(terms.shape[0])) * (16384 ** -0.5)


VMEM = pl.BlockSpec(memory_space=pltpu.VMEM)
SMEM = pl.BlockSpec(memory_space=pltpu.SMEM)
ANY = pl.BlockSpec(memory_space=pl.ANY)
HBM = pl.BlockSpec(memory_space=pltpu.HBM)


def call(kernel, out_shape, specs, operands, limit, flops=0, scratch=()):
    single = not isinstance(out_shape, list)
    return pl.pallas_call(
        kernel,
        out_shape=out_shape,
        in_specs=specs,
        out_specs=VMEM if single else [VMEM] * len(out_shape),
        scratch_shapes=list(scratch),
        compiler_params=pltpu.CompilerParams(vmem_limit_bytes=limit * 1024 * 1024),
        cost_estimate=pl.CostEstimate(flops=flops, bytes_accessed=4 * 1024 * 1024, transcendentals=0),
    )(*operands)


def shape(*dims, dtype=BF):
    return jax.ShapeDtypeStruct(dims, dtype)


def start(place, keys, values, docs, queries):
    def block(*dims):
        return pl.BlockSpec(dims, lambda i, place: (0,) * len(dims))

    picked = pl.BlockSpec((128, 128), lambda i, place: (place[0], place[1]))
    outs = [(4, 272, 128), (528, 128)]
    return pl.pallas_call(
        start_kernel,
        grid_spec=pltpu.PrefetchScalarGridSpec(
            num_scalar_prefetch=1,
            grid=(1,),
            in_specs=[picked, picked, block(4, 128), block(512, 128)],
            out_specs=[block(*dims) for dims in outs],
        ),
        out_shape=[shape(*dims) for dims in outs],
    )(place, keys, values, docs, queries)


def on_device(queries, keys, values, doc_ids, hidden, out_weight, projector, teacher):
    zl, yl, c = lax.axis_index("zl"), lax.axis_index("yl"), lax.axis_index("c")
    j = lax.axis_index("xl") * 2 + c
    z = lax.axis_index("zh") * 4 + zl
    g = lax.axis_index("yh") * 2 + lax.axis_index("xh")
    swap = [(0, 1), (1, 0)]
    place = jnp.stack([j, g, c, c, yl, z, zl]).astype(jnp.int32)

    def from_z(x, shift):
        return lax.ppermute(x, ("zh", "zl"), [((i + shift) % 16, i) for i in range(16)])

    docs = doc_ids.reshape(4, 128)
    packed, q_rows = start(place, keys, values, docs, queries)
    kv_own = lax.all_to_all(packed, "zh", 0, 0)
    kv_below, kv_above = from_z(kv_own, -1), from_z(kv_own, 1)
    kv_low, kv_high = from_z(kv_own[0:2], -2), from_z(kv_own[2:4], 2)

    q_all = lax.all_gather(q_rows, OCTET, axis=0)
    gathered = lax.all_gather(jnp.concatenate([out_weight.T, hidden.T], axis=1), GROUP, axis=0, tiled=True)
    projector_t = projector.T

    partial = call(
        attend_kernel,
        shape(8, 528, 128),
        [SMEM] + [ANY] * 5 + [HBM, ANY],
        (place, kv_own, kv_below, kv_above, kv_low, kv_high, q_all, projector_t),
        40,
        2 * 10 ** 10,
        scratch=[
            pltpu.VMEM((4, 4, 272, 128), BF),
            pltpu.VMEM((8, 528, 128), BF),
            pltpu.VMEM((128, 2048), BF),
            pltpu.VMEM((4, 512, 512), F32),
            pltpu.VMEM((24, 128), jnp.int32),
            pltpu.SMEM((24, 128), jnp.int32),
            pltpu.SemaphoreType.DMA((7,)),
        ],
    )
    att_rows, att_copies = call(
        combine_kernel, [shape(512, 128), shape(4, 512, 128)], [VMEM], (lax.all_to_all(partial, OCTET, 0, 0),), 16
    )

    att_head = lax.all_to_all(att_rows.reshape(4, 128, 128), GROUP, 0, 0)
    attended = jnp.transpose(att_head, (0, 2, 1)).reshape(512, 128)

    att_all = lax.all_to_all(att_copies, HEADSETS, 0, 0)
    student = call(
        student_kernel,
        shape(8, 896, 128),
        [SMEM, HBM, VMEM, VMEM],
        (place, gathered, att_all, teacher),
        24,
        scratch=[pltpu.VMEM((768, 2048), BF), pltpu.VMEM((768, 128), BF), pltpu.SemaphoreType.DMA((5,))],
    )
    own = lax.all_to_all(student, CHIPS, 0, 0)
    other = lax.ppermute(own, "c", swap)

    own_projected = call(own_projected_kernel, shape(256, 256, dtype=F32), [VMEM] * 2, (own, projector_t), 24, 4 * 10 ** 8)
    mismatch, up, down = call(
        second_kernel,
        [shape(512, 256), shape(4, 96, 256), shape(4, 96, 256)],
        [SMEM] + [VMEM] * 4,
        (place, own, other, projector_t, own_projected),
        32,
        8 * 10 ** 8,
    )
    far_below, far_above = from_z(up, -2), from_z(down, 2)
    up, down = call(
        first_kernel, [shape(8, 96, 256), shape(8, 96, 256)], [SMEM] + [VMEM] * 3, (place, own, other, mismatch), 32, 4 * 10 ** 8
    )
    below, above = from_z(up, -1), from_z(down, 1)
    kept = call(kept_kernel, shape(8, 96, 256, dtype=F32), [SMEM] + [VMEM] * 3, (place, own, other, mismatch), 32, 2 * 10 ** 8)
    near = call(add_kernel, shape(8, 96, 256), [VMEM] * 5, (kept, below, above, far_below, far_above), 16)
    grad = call(final_kernel, shape(96, 256, dtype=F32), [VMEM], (lax.all_to_all(near, ("zh", "yl"), 0, 0),), 8)
    return grad, attended


def solution(mesh):
    fine = Mesh(mesh.devices.reshape(4, 4, 2, 2, 2, 2, 2), ("zh", "zl", "yl", "yh", "xh", "xl", "c"))
    return jax.shard_map(
        on_device,
        mesh=fine,
        in_specs=(
            P(CTX, HID),
            P(CTX, None),
            P(CTX, None),
            P(CTX),
            P(CTX, HID),
            P(None, HID),
            P(None, HID),
            P(CTX + HID, None),
        ),
        out_specs=(P(CTX, HID), P(CTX, HID)),
        check_vma=False,
    )
```

```python
import functools

import jax
import jax.numpy as jnp
from jax import lax
from jax.experimental import pallas as pl
from jax.experimental.pallas import tpu as pltpu
from jax.sharding import Mesh
from jax.sharding import PartitionSpec as P

HEAD = 128
SCALE2 = HEAD ** -0.5 * 1.4426950408889634
EMPTY = -1e30
MASKED = -2e30
BF = jnp.bfloat16
F32 = jnp.float32
CTX = ("zh", "zl", "yl")
HID = ("yh", "xh", "xl", "c")
GROUP = ("xl", "c")
OCTET = ("yl", "xl", "c")
HEADSETS = ("yh", "xh")
CHIPS = ("xl", "yh", "xh")
BLOCKS = 4


def start_kernel(place, keys, values, docs, packed, doc_rows):
    rows = jnp.concatenate([docs[...].astype(F32), jnp.zeros((12, 128), F32)], axis=0).astype(BF)
    for copy in range(4):
        packed[copy, 0:128, :] = keys[...]
        packed[copy, 128:256, :] = values[...]
        packed[copy, 256:272, :] = rows
    doc_rows[...] = rows


def attend_kernel(place, kv0, kv1, kv2, kv3_low, kv3_high, q_own, q_other, early, out, kv, q_all, v_turned, s_buf, info_v, info, sem):
    j, yl, z = place[0], place[4], place[5]
    copies = [
        pltpu.make_async_copy(src, dst, sem.at[i])
        for i, (src, dst) in enumerate((
            (kv0, kv.at[0]), (kv1, kv.at[1]), (kv2, kv.at[2]), (kv3_low, kv.at[3, pl.ds(0, 2)]), (kv3_high, kv.at[3, pl.ds(2, 2)]),
            (q_own, q_all.at[0]), (q_other, q_all.at[1]),
        ))
    ]
    for copy in copies:
        copy.start()
    for copy in copies:
        copy.wait()
    for side in range(2):
        info_v[16 + 4 * side:20 + 4 * side, :] = q_all[side, 2048:2064, :].astype(F32)[0:4].astype(jnp.int32)
    block_docs = []
    for ch in range(4):
        for i in range(BLOCKS):
            rows = kv[i, ch, 256:272, :].astype(F32)
            block_docs.append(jnp.concatenate([rows[r:r + 1] for r in range(4)], axis=1))
    block_docs = jnp.concatenate(block_docs, axis=0)
    lane = lax.broadcasted_iota(jnp.int32, (16, 128), 1)
    counts = jnp.zeros((16, 128), F32)
    for d in range(8):
        below = jnp.sum((block_docs < d).astype(F32), axis=1, keepdims=True)
        counts = jnp.where(lane == d, below, counts)
    info_v[0:16, :] = counts.astype(jnp.int32)
    to_scalars = pltpu.make_async_copy(info_v, info, sem.at[7])
    to_scalars.start()
    for ch in range(4):
        for i in range(BLOCKS):
            v_turned[:, (ch * BLOCKS + i) * 128:(ch * BLOCKS + i + 1) * 128] = kv[i, ch, 128:256, :].T
    to_scalars.wait()
    where = [(z + shift) % 4 for shift in (0, 3, 1, 2)]
    key_iota = lax.broadcasted_iota(jnp.int32, (128, 512), 0)
    row_iota = lax.broadcasted_iota(jnp.int32, (1, 512), 1) % 128

    def one_tile(tile, carry):
        side, rc = tile // 4, tile % 4
        yl_q = jnp.where(side == 0, yl, 1 - yl)
        dest = yl_q * 4 + rc
        row0 = pl.multiple_of(rc * 128, 128)
        q = jnp.concatenate([q_all[side, pl.ds(pl.multiple_of((h ^ j) * 512, 512) + row0, 128), :] for h in range(4)], axis=0)
        row_docs = jnp.concatenate([info_v[pl.ds(16 + tile, 1), :]] * 4, axis=1)
        first, last = info[16 + tile, 0], info[16 + tile, 127]
        q_min = (2 * z + yl_q) * 512 + row0
        q_pos = q_min + row_iota

        def scores(ch):
            keys = jnp.concatenate([kv[i, ch, 0:128, :] for i in range(BLOCKS)], axis=0)
            return lax.dot_general(keys, q, (((1,), (1,)), ((), ())), preferred_element_type=F32) * SCALE2

        def mask(ch, s):
            parts = []
            for i in range(BLOCKS):
                low = jnp.zeros((1, 512), jnp.int32)
                for d in range(8):
                    low = jnp.where(row_docs == d, info[ch * BLOCKS + i, d], low)
                low = low - j * 128
                high = q_pos - ((2 * (ch * 4 + where[i]) + yl) * 512 + j * 128)
                ok = (key_iota >= low) & (key_iota <= high)
                parts.append(jnp.where(ok, s[i * 128:(i + 1) * 128], MASKED))
            return jnp.concatenate(parts, axis=0)

        def find_max(ch, run_max):
            most = functools.reduce(jnp.maximum, [info[ch * BLOCKS + i, last] for i in range(BLOCKS)])
            k_max = (2 * (ch * BLOCKS + BLOCKS - 1) + yl) * 512 + j * 128 + 127
            full = (k_max <= q_min) & (most <= j * 128)

            def keep(s):
                s_buf[ch] = s
                return jnp.max(s, axis=0, keepdims=True)

            return jnp.maximum(run_max, lax.cond(full, lambda: keep(scores(ch)), lambda: keep(mask(ch, scores(ch)))))

        def add_up(ch, state):
            run_sum, acc = state
            w = jnp.exp2(s_buf[ch] - run_max)
            cols = pl.ds(pl.multiple_of(ch * (BLOCKS * 128), BLOCKS * 128), BLOCKS * 128)
            blended = jnp.dot(v_turned[:, cols], w.astype(BF), preferred_element_type=F32)
            return run_sum + jnp.sum(w, axis=0, keepdims=True), acc + blended

        begin = jnp.int32(0)
        for ch in range(4):
            fewest = functools.reduce(jnp.minimum, [info[ch * BLOCKS + i, first] for i in range(BLOCKS)])
            begin = begin + (fewest >= (j + 1) * 128).astype(jnp.int32)
        end = z // BLOCKS + 1
        run_max = lax.fori_loop(begin, end, find_max, jnp.full((1, 512), EMPTY, F32))
        run_sum, acc = lax.fori_loop(begin, end, add_up, (jnp.zeros((1, 512), F32), jnp.zeros((128, 512), F32)))
        seen = run_sum > 0
        o = (acc * (1.0 / jnp.where(seen, run_sum, 1.0))).astype(BF)
        lse = jnp.where(seen, run_max + jnp.log2(jnp.where(seen, run_sum, 1.0)), EMPTY)
        hi = lse.astype(BF).astype(F32)
        mid = (lse - hi).astype(BF).astype(F32)
        lo = lse - hi - mid
        rows = [part[:, h * 128:(h + 1) * 128] for part in (hi, mid, lo) for h in range(4)]
        rows.append(jnp.zeros((4, 128), F32))
        for h in range(4):
            out[dest, h * 128:(h + 1) * 128, :] = o[:, h * 128:(h + 1) * 128]
        out[dest, 512:528, :] = jnp.concatenate(rows, axis=0).astype(BF)
        return carry

    lax.fori_loop(0, 8, one_tile, 0)


def combine_kernel(parts, out, copies):
    count = parts.shape[0]
    tails = [parts[s, 512:528, :].astype(F32) for s in range(count)]
    for h in range(4):
        lses = [t[h:h + 1] + t[4 + h:5 + h] + t[8 + h:9 + h] for t in tails]
        top = functools.reduce(jnp.maximum, lses)
        weights = [jnp.exp2(v - top) for v in lses]
        inverse = 1.0 / sum(weights)
        rows = slice(h * 128, (h + 1) * 128)
        total = sum(w * inverse * parts[s, rows, :].astype(F32) for s, w in enumerate(weights)).astype(BF)
        out[rows, :] = total
        for copy in range(copies.shape[0]):
            copies[copy, rows, :] = total


def student_kernel(place, gathered, att, teacher, out, weights, hidden, sem):
    copies = []
    own_rows = pl.ds(pl.multiple_of(2048 + place[0] * 128, 128), 128)
    hidden_copy = pltpu.make_async_copy(gathered.at[:, own_rows], hidden, sem.at[4])
    for part in range(4):
        rows = pl.ds(part * 192, 192)
        copies.append(pltpu.make_async_copy(gathered.at[rows, pl.ds(0, 2048)], weights.at[rows], sem.at[part]))
    copies[0].start()
    hidden_copy.start()
    for copy in copies[1:]:
        copy.start()
    for chip in range(8):
        first = (chip % 4 * 4 + chip // 4 * 2) * 256
        for i in range(4):
            out[chip, 768 + i * 32:800 + i * 32, :] = teacher[:, first + i * 128:first + (i + 1) * 128]
    att_all = att[...].reshape(2048, 128)
    hidden_copy.wait()
    for part in range(4):
        copies[part].wait()
        rows = slice(part * 192, (part + 1) * 192)
        mixed = jnp.dot(weights[rows, :], att_all, preferred_element_type=F32)
        student = (hidden[rows, :].astype(F32) + mixed).astype(BF)
        for copy in range(8):
            out[copy, rows, :] = student


def projected(student, projector_t):
    total = 0.0
    for g in range(4):
        both = jnp.concatenate([student[g, 0:768, :], student[4 + g, 0:768, :]], axis=1)
        total = total + jnp.dot(projector_t[:, g * 768:(g + 1) * 768], both, preferred_element_type=F32)
    return total


def teacher_rows(own, other, core, chunk_core):
    pieces = []
    for xl in range(2):
        for t in range(4):
            source = t // 2 * 4 + xl * 2 + chunk_core
            halves = []
            for i in range(2):
                rows = pl.ds(pl.multiple_of(768 + core * 64 + i * 32, 32), 32)
                halves.append(jnp.where(core == t % 2, own[source, rows, :].astype(F32), other[source, rows, :].astype(F32)))
            pieces.append(jnp.concatenate(halves, axis=1))
    return jnp.concatenate(pieces, axis=0)


def gradient_rows(own, other, mismatch, near):
    rows = []
    for zh in range(4):
        cut = pl.ds(pl.multiple_of(near * 192, 64), 192)
        rows.append(jnp.concatenate([ref[xl * 4 + zh, cut, :] for ref in (own, other) for xl in range(2)], axis=1))
    return jnp.dot(jnp.concatenate(rows, axis=0), mismatch[...], preferred_element_type=F32).reshape(8, 96, 256)


def own_projected_kernel(own, projector_t, out):
    out[...] = projected(own, projector_t).T


def second_kernel(place, own, other, projector_t, own_projected, mismatch, up, down):
    core = place[2]
    mismatch[0:256, :] = (own_projected[...] - teacher_rows(own, other, core, core)).astype(BF)
    mismatch[256:512, :] = (projected(other, projector_t).T - teacher_rows(own, other, core, 1 - core)).astype(BF)
    grad = gradient_rows(own, other, mismatch, (place[6] + 2) % 4).astype(BF)
    up[...] = grad[0:4]
    down[...] = grad[4:8]


def first_kernel(place, own, other, mismatch, up, down):
    up[...] = gradient_rows(own, other, mismatch, (place[6] + 1) % 4).astype(BF)
    down[...] = gradient_rows(own, other, mismatch, (place[6] + 3) % 4).astype(BF)


def kept_kernel(place, own, other, mismatch, out):
    out[...] = gradient_rows(own, other, mismatch, place[6])


def add_kernel(kept, below, above, far_below, far_above, out):
    near = kept[...] + below[...].astype(F32) + above[...].astype(F32)
    out[0:4] = (near[0:4] + far_below[...].astype(F32)).astype(BF)
    out[4:8] = (near[4:8] + far_above[...].astype(F32)).astype(BF)


def final_kernel(terms, out):
    out[...] = sum(terms[i].astype(F32) for i in range(terms.shape[0])) * (16384 ** -0.5)


VMEM = pl.BlockSpec(memory_space=pltpu.VMEM)
SMEM = pl.BlockSpec(memory_space=pltpu.SMEM)
ANY = pl.BlockSpec(memory_space=pl.ANY)
HBM = pl.BlockSpec(memory_space=pltpu.HBM)


def call(kernel, out_shape, specs, operands, limit, flops=0, scratch=()):
    single = not isinstance(out_shape, list)
    return pl.pallas_call(
        kernel,
        out_shape=out_shape,
        in_specs=specs,
        out_specs=VMEM if single else [VMEM] * len(out_shape),
        scratch_shapes=list(scratch),
        compiler_params=pltpu.CompilerParams(vmem_limit_bytes=limit * 1024 * 1024),
        cost_estimate=pl.CostEstimate(flops=flops, bytes_accessed=4 * 1024 * 1024, transcendentals=0),
    )(*operands)


def shape(*dims, dtype=BF):
    return jax.ShapeDtypeStruct(dims, dtype)


def start(place, keys, values, docs):
    def block(*dims):
        return pl.BlockSpec(dims, lambda i, place: (0,) * len(dims))

    picked = pl.BlockSpec((128, 128), lambda i, place: (place[0], place[1]))
    outs = [(4, 272, 128), (16, 128)]
    return pl.pallas_call(
        start_kernel,
        grid_spec=pltpu.PrefetchScalarGridSpec(
            num_scalar_prefetch=1,
            grid=(1,),
            in_specs=[picked, picked, block(4, 128)],
            out_specs=[block(*dims) for dims in outs],
        ),
        out_shape=[shape(*dims) for dims in outs],
    )(place, keys, values, docs)


def on_device(queries, keys, values, doc_ids, hidden, out_weight, projector, teacher):
    zl, yl, c = lax.axis_index("zl"), lax.axis_index("yl"), lax.axis_index("c")
    j = lax.axis_index("xl") * 2 + c
    z = lax.axis_index("zh") * 4 + zl
    g = lax.axis_index("yh") * 2 + lax.axis_index("xh")
    swap = [(0, 1), (1, 0)]
    place = jnp.stack([j, g, c, c, yl, z, zl]).astype(jnp.int32)

    def from_z(x, shift):
        return lax.ppermute(x, ("zh", "zl"), [((i + shift) % 16, i) for i in range(16)])

    docs = doc_ids.reshape(4, 128)
    packed, doc_rows = start(place, keys, values, docs)
    kv_own = lax.all_to_all(packed, "zh", 0, 0)
    kv_below, kv_above = from_z(kv_own, -1), from_z(kv_own, 1)
    kv_low, kv_high = from_z(kv_own[0:2], -2), from_z(kv_own[2:4], 2)

    q_two = jnp.concatenate([queries, lax.ppermute(queries, "c", swap)], axis=0)
    q_own = jnp.concatenate([q_two, lax.ppermute(q_two, "xl", swap), doc_rows], axis=0)
    q_other = lax.ppermute(q_own, "yl", swap)
    gathered = lax.all_gather(jnp.concatenate([out_weight.T, hidden.T], axis=1), GROUP, axis=0, tiled=True)
    projector_t = projector.T

    partial = call(
        attend_kernel,
        shape(8, 528, 128),
        [SMEM] + [ANY] * 8,
        (place, kv_own, kv_below, kv_above, kv_low, kv_high, q_own, q_other, projector_t),
        40,
        2 * 10 ** 10,
        scratch=[
            pltpu.VMEM((4, 4, 272, 128), BF),
            pltpu.VMEM((2, 2064, 128), BF),
            pltpu.VMEM((128, 2048), BF),
            pltpu.VMEM((4, 512, 512), F32),
            pltpu.VMEM((24, 128), jnp.int32),
            pltpu.SMEM((24, 128), jnp.int32),
            pltpu.SemaphoreType.DMA((8,)),
        ],
    )
    att_rows, att_copies = call(
        combine_kernel, [shape(512, 128), shape(4, 512, 128)], [VMEM], (lax.all_to_all(partial, OCTET, 0, 0),), 16
    )

    att_head = lax.all_to_all(att_rows.reshape(4, 128, 128), GROUP, 0, 0)
    attended = jnp.transpose(att_head, (0, 2, 1)).reshape(512, 128)

    att_all = lax.all_to_all(att_copies, HEADSETS, 0, 0)
    student = call(
        student_kernel,
        shape(8, 896, 128),
        [SMEM, HBM, VMEM, VMEM],
        (place, gathered, att_all, teacher),
        24,
        scratch=[pltpu.VMEM((768, 2048), BF), pltpu.VMEM((768, 128), BF), pltpu.SemaphoreType.DMA((5,))],
    )
    own = lax.all_to_all(student, CHIPS, 0, 0)
    other = lax.ppermute(own, "c", swap)

    own_projected = call(own_projected_kernel, shape(256, 256, dtype=F32), [VMEM] * 2, (own, projector_t), 24, 4 * 10 ** 8)
    mismatch, up, down = call(
        second_kernel,
        [shape(512, 256), shape(4, 96, 256), shape(4, 96, 256)],
        [SMEM] + [VMEM] * 4,
        (place, own, other, projector_t, own_projected),
        32,
        8 * 10 ** 8,
    )
    far_below, far_above = from_z(up, -2), from_z(down, 2)
    up, down = call(
        first_kernel, [shape(8, 96, 256), shape(8, 96, 256)], [SMEM] + [VMEM] * 3, (place, own, other, mismatch), 32, 4 * 10 ** 8
    )
    below, above = from_z(up, -1), from_z(down, 1)
    kept = call(kept_kernel, shape(8, 96, 256, dtype=F32), [SMEM] + [VMEM] * 3, (place, own, other, mismatch), 32, 2 * 10 ** 8)
    near = call(add_kernel, shape(8, 96, 256), [VMEM] * 5, (kept, below, above, far_below, far_above), 16)
    grad = call(final_kernel, shape(96, 256, dtype=F32), [VMEM], (lax.all_to_all(near, ("zh", "yl"), 0, 0),), 8)
    return grad, attended


def solution(mesh):
    fine = Mesh(mesh.devices.reshape(4, 4, 2, 2, 2, 2, 2), ("zh", "zl", "yl", "yh", "xh", "xl", "c"))
    return jax.shard_map(
        on_device,
        mesh=fine,
        in_specs=(
            P(CTX, HID),
            P(CTX, None),
            P(CTX, None),
            P(CTX),
            P(CTX, HID),
            P(None, HID),
            P(None, HID),
            P(CTX + HID, None),
        ),
        out_specs=(P(CTX, HID), P(CTX, HID)),
        check_vma=False,
    )
```

```python
import functools

import jax
import jax.numpy as jnp
from jax import lax
from jax.experimental import pallas as pl
from jax.experimental.pallas import tpu as pltpu
from jax.sharding import Mesh
from jax.sharding import PartitionSpec as P

HEAD = 128
SCALE2 = HEAD ** -0.5 * 1.4426950408889634
EMPTY = -1e30
MASKED = -2e30
BF = jnp.bfloat16
F32 = jnp.float32
CTX = ("zh", "zl", "yl")
HID = ("yh", "xh", "xl", "c")
GROUP = ("xl", "c")
OCTET = ("yl", "xl", "c")
HEADSETS = ("yh", "xh")
CHIPS = ("xl", "yh", "xh")
BLOCKS = 4


def start_kernel(place, keys, values, docs, packed, doc_rows):
    rows = jnp.concatenate([docs[...].astype(F32), jnp.zeros((12, 128), F32)], axis=0).astype(BF)
    for copy in range(4):
        packed[copy, 0:128, :] = keys[...]
        packed[copy, 128:256, :] = values[...]
        packed[copy, 256:272, :] = rows
    doc_rows[...] = rows


def attend_kernel(place, kv, q_own, q_other, early, out, q_all, v_turned, s_buf, info_v, info, sem):
    j, yl, z = place[0], place[4], place[5]
    copies = [pltpu.make_async_copy(src, q_all.at[i], sem.at[i]) for i, src in enumerate((q_own, q_other))]
    for copy in copies:
        copy.start()
    for copy in copies:
        copy.wait()
    for side in range(2):
        info_v[16 + 4 * side:20 + 4 * side, :] = q_all[side, 2048:2064, :].astype(F32)[0:4].astype(jnp.int32)
    block_docs = []
    for ch in range(4):
        for i in range(BLOCKS):
            rows = kv[i, ch, 256:272, :].astype(F32)
            block_docs.append(jnp.concatenate([rows[r:r + 1] for r in range(4)], axis=1))
    block_docs = jnp.concatenate(block_docs, axis=0)
    lane = lax.broadcasted_iota(jnp.int32, (16, 128), 1)
    counts = jnp.zeros((16, 128), F32)
    for d in range(8):
        below = jnp.sum((block_docs < d).astype(F32), axis=1, keepdims=True)
        counts = jnp.where(lane == d, below, counts)
    info_v[0:16, :] = counts.astype(jnp.int32)
    to_scalars = pltpu.make_async_copy(info_v, info, sem.at[2])
    to_scalars.start()
    for ch in range(4):
        for i in range(BLOCKS):
            v_turned[:, (ch * BLOCKS + i) * 128:(ch * BLOCKS + i + 1) * 128] = kv[i, ch, 128:256, :].T
    to_scalars.wait()
    key_iota = lax.broadcasted_iota(jnp.int32, (128, 512), 0)
    row_iota = lax.broadcasted_iota(jnp.int32, (1, 512), 1) % 128

    def one_tile(tile, carry):
        side, rc = tile // 4, tile % 4
        yl_q = jnp.where(side == 0, yl, 1 - yl)
        dest = yl_q * 4 + rc
        row0 = pl.multiple_of(rc * 128, 128)
        q = jnp.concatenate([q_all[side, pl.ds(pl.multiple_of((h ^ j) * 512, 512) + row0, 128), :] for h in range(4)], axis=0)
        row_docs = jnp.concatenate([info_v[pl.ds(16 + tile, 1), :]] * 4, axis=1)
        first, last = info[16 + tile, 0], info[16 + tile, 127]
        q_min = (2 * z + yl_q) * 512 + row0
        q_pos = q_min + row_iota

        def scores(ch):
            keys = jnp.concatenate([kv[i, ch, 0:128, :] for i in range(BLOCKS)], axis=0)
            return lax.dot_general(keys, q, (((1,), (1,)), ((), ())), preferred_element_type=F32) * SCALE2

        def mask(ch, s):
            parts = []
            for i in range(BLOCKS):
                low = jnp.zeros((1, 512), jnp.int32)
                for d in range(8):
                    low = jnp.where(row_docs == d, info[ch * BLOCKS + i, d], low)
                low = low - j * 128
                high = q_pos - ((2 * (ch * 4 + i) + yl) * 512 + j * 128)
                ok = (key_iota >= low) & (key_iota <= high)
                parts.append(jnp.where(ok, s[i * 128:(i + 1) * 128], MASKED))
            return jnp.concatenate(parts, axis=0)

        def find_max(ch, run_max):
            most = info[ch * BLOCKS, last]
            k_max = (2 * (ch * BLOCKS + BLOCKS - 1) + yl) * 512 + j * 128 + 127
            full = (k_max <= q_min) & (most <= j * 128)

            def keep(s):
                s_buf[ch] = s
                return jnp.max(s, axis=0, keepdims=True)

            return jnp.maximum(run_max, lax.cond(full, lambda: keep(scores(ch)), lambda: keep(mask(ch, scores(ch)))))

        def add_up(ch, state):
            run_sum, acc = state
            w = jnp.exp2(s_buf[ch] - run_max)
            cols = pl.ds(pl.multiple_of(ch * (BLOCKS * 128), BLOCKS * 128), BLOCKS * 128)
            blended = jnp.dot(v_turned[:, cols], w.astype(BF), preferred_element_type=F32)
            return run_sum + jnp.sum(w, axis=0, keepdims=True), acc + blended

        begin = jnp.int32(0)
        for ch in range(4):
            fewest = info[ch * BLOCKS + BLOCKS - 1, first]
            begin = begin + (fewest >= (j + 1) * 128).astype(jnp.int32)
        end = z // BLOCKS + 1
        run_max = lax.fori_loop(begin, end, find_max, jnp.full((1, 512), EMPTY, F32))
        run_sum, acc = lax.fori_loop(begin, end, add_up, (jnp.zeros((1, 512), F32), jnp.zeros((128, 512), F32)))
        seen = run_sum > 0
        o = (acc * (1.0 / jnp.where(seen, run_sum, 1.0))).astype(BF)
        lse = jnp.where(seen, run_max + jnp.log2(jnp.where(seen, run_sum, 1.0)), EMPTY)
        hi = lse.astype(BF).astype(F32)
        mid = (lse - hi).astype(BF).astype(F32)
        lo = lse - hi - mid
        rows = [part[:, h * 128:(h + 1) * 128] for part in (hi, mid, lo) for h in range(4)]
        rows.append(jnp.zeros((4, 128), F32))
        for h in range(4):
            out[dest, h * 128:(h + 1) * 128, :] = o[:, h * 128:(h + 1) * 128]
        out[dest, 512:528, :] = jnp.concatenate(rows, axis=0).astype(BF)
        return carry

    lax.fori_loop(0, 8, one_tile, 0)


def combine_kernel(parts, out, copies):
    count = parts.shape[0]
    tails = [parts[s, 512:528, :].astype(F32) for s in range(count)]
    for h in range(4):
        lses = [t[h:h + 1] + t[4 + h:5 + h] + t[8 + h:9 + h] for t in tails]
        top = functools.reduce(jnp.maximum, lses)
        weights = [jnp.exp2(v - top) for v in lses]
        inverse = 1.0 / sum(weights)
        rows = slice(h * 128, (h + 1) * 128)
        total = sum(w * inverse * parts[s, rows, :].astype(F32) for s, w in enumerate(weights)).astype(BF)
        out[rows, :] = total
        for copy in range(copies.shape[0]):
            copies[copy, rows, :] = total


def student_kernel(place, weight_t, hidden_t, att, teacher, out, weights, hidden, sem):
    copies = []
    own_rows = pl.ds(pl.multiple_of(place[0] * 128, 128), 128)
    hidden_copy = pltpu.make_async_copy(hidden_t.at[:, own_rows], hidden, sem.at[4])
    for part in range(4):
        rows = pl.ds(part * 192, 192)
        copies.append(pltpu.make_async_copy(weight_t.at[rows], weights.at[rows], sem.at[part]))
    copies[0].start()
    hidden_copy.start()
    for copy in copies[1:]:
        copy.start()
    for chip in range(8):
        first = (chip % 4 * 4 + chip // 4 * 2) * 256
        for i in range(4):
            out[chip, 768 + i * 32:800 + i * 32, :] = teacher[:, first + i * 128:first + (i + 1) * 128]
    att_all = att[...].reshape(2048, 128)
    hidden_copy.wait()
    for part in range(4):
        copies[part].wait()
        rows = slice(part * 192, (part + 1) * 192)
        mixed = jnp.dot(weights[rows, :], att_all, preferred_element_type=F32)
        student = (hidden[rows, :].astype(F32) + mixed).astype(BF)
        for copy in range(8):
            out[copy, rows, :] = student


def projected(student, projector_t):
    total = 0.0
    for g in range(4):
        both = jnp.concatenate([student[g, 0:768, :], student[4 + g, 0:768, :]], axis=1)
        total = total + jnp.dot(projector_t[:, g * 768:(g + 1) * 768], both, preferred_element_type=F32)
    return total


def teacher_rows(own, other, core, chunk_core):
    pieces = []
    for xl in range(2):
        for t in range(4):
            source = t // 2 * 4 + xl * 2 + chunk_core
            halves = []
            for i in range(2):
                rows = pl.ds(pl.multiple_of(768 + core * 64 + i * 32, 32), 32)
                halves.append(jnp.where(core == t % 2, own[source, rows, :].astype(F32), other[source, rows, :].astype(F32)))
            pieces.append(jnp.concatenate(halves, axis=1))
    return jnp.concatenate(pieces, axis=0)


def gradient_rows(own, other, mismatch, near):
    rows = []
    for zh in range(4):
        cut = slice(near * 192, (near + 1) * 192)
        rows.append(jnp.concatenate([ref[xl * 4 + zh, cut, :] for ref in (own, other) for xl in range(2)], axis=1))
    return jnp.dot(jnp.concatenate(rows, axis=0), mismatch[...], preferred_element_type=F32).reshape(8, 96, 256)


def own_projected_kernel(own, projector_t, out):
    out[...] = projected(own, projector_t).T


def gradient_kernel(place, own, other, projector_t, own_projected, out, mismatch):
    core = place[2]
    mismatch[0:256, :] = (own_projected[...] - teacher_rows(own, other, core, core)).astype(BF)
    mismatch[256:512, :] = (projected(other, projector_t).T - teacher_rows(own, other, core, 1 - core)).astype(BF)
    for near in range(4):
        out[near] = gradient_rows(own, other, mismatch, near).astype(BF)


def add_kernel(terms, out):
    out[...] = sum(terms[i].astype(F32) for i in range(terms.shape[0])).astype(BF)


def final_kernel(terms, out):
    out[...] = sum(terms[i].astype(F32) for i in range(terms.shape[0])) * (16384 ** -0.5)


VMEM = pl.BlockSpec(memory_space=pltpu.VMEM)
SMEM = pl.BlockSpec(memory_space=pltpu.SMEM)
ANY = pl.BlockSpec(memory_space=pl.ANY)
HBM = pl.BlockSpec(memory_space=pltpu.HBM)


def call(kernel, out_shape, specs, operands, limit, flops=0, scratch=()):
    single = not isinstance(out_shape, list)
    return pl.pallas_call(
        kernel,
        out_shape=out_shape,
        in_specs=specs,
        out_specs=VMEM if single else [VMEM] * len(out_shape),
        scratch_shapes=list(scratch),
        compiler_params=pltpu.CompilerParams(vmem_limit_bytes=limit * 1024 * 1024),
        cost_estimate=pl.CostEstimate(flops=flops, bytes_accessed=4 * 1024 * 1024, transcendentals=0),
    )(*operands)


def shape(*dims, dtype=BF):
    return jax.ShapeDtypeStruct(dims, dtype)


def start(place, keys, values, docs):
    def block(*dims):
        return pl.BlockSpec(dims, lambda i, place: (0,) * len(dims))

    picked = pl.BlockSpec((128, 128), lambda i, place: (place[0], place[1]))
    outs = [(4, 272, 128), (16, 128)]
    return pl.pallas_call(
        start_kernel,
        grid_spec=pltpu.PrefetchScalarGridSpec(
            num_scalar_prefetch=1,
            grid=(1,),
            in_specs=[picked, picked, block(4, 128)],
            out_specs=[block(*dims) for dims in outs],
        ),
        out_shape=[shape(*dims) for dims in outs],
    )(place, keys, values, docs)


def on_device(queries, keys, values, doc_ids, hidden, out_weight, projector, teacher):
    yl, c = lax.axis_index("yl"), lax.axis_index("c")
    j = lax.axis_index("xl") * 2 + c
    z = lax.axis_index("zh") * 4 + lax.axis_index("zl")
    g = lax.axis_index("yh") * 2 + lax.axis_index("xh")
    swap = [(0, 1), (1, 0)]
    place = jnp.stack([j, g, c, c, yl, z]).astype(jnp.int32)

    docs = doc_ids.reshape(4, 128)
    packed, doc_rows = start(place, keys, values, docs)
    kv_own = lax.all_to_all(packed, "zh", 0, 0)
    kv = lax.all_to_all(jnp.broadcast_to(kv_own[None], (4, 4, 272, 128)), "zl", 0, 0)

    q_two = jnp.concatenate([queries, lax.ppermute(queries, "c", swap)], axis=0)
    q_own = jnp.concatenate([q_two, lax.ppermute(q_two, "xl", swap), doc_rows], axis=0)
    q_other = lax.ppermute(q_own, "yl", swap)
    weight_t = lax.all_gather(out_weight.T, GROUP, axis=0, tiled=True)
    hidden_t = lax.all_gather(hidden.T, GROUP, axis=0, tiled=True)
    projector_t = projector.T

    partial = call(
        attend_kernel,
        shape(8, 528, 128),
        [SMEM, VMEM] + [ANY] * 3,
        (place, kv, q_own, q_other, projector_t),
        58,
        2 * 10 ** 10,
        scratch=[
            pltpu.VMEM((2, 2064, 128), BF),
            pltpu.VMEM((128, 2048), BF),
            pltpu.VMEM((4, 512, 512), F32),
            pltpu.VMEM((24, 128), jnp.int32),
            pltpu.SMEM((24, 128), jnp.int32),
            pltpu.SemaphoreType.DMA((3,)),
        ],
    )
    att_rows, att_copies = call(
        combine_kernel, [shape(512, 128), shape(4, 512, 128)], [VMEM], (lax.all_to_all(partial, OCTET, 0, 0),), 16
    )

    att_head = lax.all_to_all(att_rows.reshape(4, 128, 128), GROUP, 0, 0)
    attended = jnp.transpose(att_head, (0, 2, 1)).reshape(512, 128)

    att_all = lax.all_to_all(att_copies, HEADSETS, 0, 0)
    student = call(
        student_kernel,
        shape(8, 896, 128),
        [SMEM, HBM, HBM, VMEM, VMEM],
        (place, weight_t, hidden_t, att_all, teacher),
        58,
        scratch=[pltpu.VMEM((768, 2048), BF), pltpu.VMEM((768, 128), BF), pltpu.SemaphoreType.DMA((5,))],
    )
    own = lax.all_to_all(student, CHIPS, 0, 0)
    other = lax.ppermute(own, "c", swap)

    own_projected = call(own_projected_kernel, shape(256, 256, dtype=F32), [VMEM] * 2, (own, projector_t), 24, 4 * 10 ** 8)
    share = call(
        gradient_kernel,
        shape(4, 8, 96, 256),
        [SMEM] + [VMEM] * 4,
        (place, own, other, projector_t, own_projected),
        32,
        8 * 10 ** 8,
        scratch=[pltpu.VMEM((512, 256), BF)],
    )
    near = call(add_kernel, shape(8, 96, 256), [VMEM], (lax.all_to_all(share, "zl", 0, 0),), 16)
    grad = call(final_kernel, shape(96, 256, dtype=F32), [VMEM], (lax.all_to_all(near, ("zh", "yl"), 0, 0),), 8)
    return grad, attended


def solution(mesh):
    fine = Mesh(mesh.devices.reshape(4, 4, 2, 2, 2, 2, 2), ("zh", "zl", "yl", "yh", "xh", "xl", "c"))
    return jax.shard_map(
        on_device,
        mesh=fine,
        in_specs=(
            P(CTX, HID),
            P(CTX, None),
            P(CTX, None),
            P(CTX),
            P(CTX, HID),
            P(None, HID),
            P(None, HID),
            P(CTX + HID, None),
        ),
        out_specs=(P(CTX, HID), P(CTX, HID)),
        check_vma=False,
    )
```

```python
import functools

import jax
import jax.numpy as jnp
from jax import lax
from jax.experimental import pallas as pl
from jax.experimental.pallas import tpu as pltpu
from jax.sharding import Mesh
from jax.sharding import PartitionSpec as P

HEAD = 128
SCALE2 = HEAD ** -0.5 * 1.4426950408889634
EMPTY = -1e30
MASKED = -2e30
BF = jnp.bfloat16
F32 = jnp.float32
CTX = ("zh", "zl", "yl")
HID = ("yh", "xh", "xl", "c")
GROUP = ("xl", "c")
OCTET = ("yl", "xl", "c")
HEADSETS = ("yh", "xh")
CHIPS = ("xl", "yh", "xh")
BLOCKS = 4


def start_kernel(place, keys, values, docs, queries, hidden_t, packed, doc_rows, sent, kept):
    rows = jnp.concatenate([docs[...].astype(F32), jnp.zeros((12, 128), F32)], axis=0).astype(BF)
    for copy in range(4):
        packed[copy, 0:128, :] = keys[...]
        packed[copy, 128:256, :] = values[...]
        packed[copy, 256:272, :] = rows
    doc_rows[...] = rows
    sent[0:512, :] = queries[...]
    for xl in range(2):
        kept[xl] = hidden_t[:, pl.ds(pl.multiple_of((xl * 2 + place[2]) * 128, 128), 128)]
        other = pl.ds(pl.multiple_of((xl * 2 + 1 - place[2]) * 128, 128), 128)
        sent[512 + xl * 192:704 + xl * 192, :] = hidden_t[:, other]


def turn_kernel(place, sent, received, kept, two, kept_out):
    xl = place[3]
    two[0:512, :] = sent[0:512, :]
    two[512:1024, :] = received[0:512, :]
    two[1024:1216, :] = kept[1 - xl]
    two[1216:1408, :] = received[pl.ds(pl.multiple_of(512 + (1 - xl) * 192, 64), 192), :]
    kept_out[0] = kept[xl]
    kept_out[1] = received[pl.ds(pl.multiple_of(512 + xl * 192, 64), 192), :]


def join_kernel(two, received, doc_rows, token, q_own, hidden_out):
    q_own[0:1024, :] = two[0:1024, :]
    q_own[1024:2048, :] = received[0:1024, :]
    q_own[2048:2064, :] = doc_rows[...]
    for i in range(2):
        hidden_out[i] = received[1024 + i * 192:1216 + i * 192, :]


def transpose_kernel(x, out, token):
    out[...] = x[...].T
    token[...] = jnp.zeros((8, 128), F32)


def attend_kernel(place, kv0, kv1, kv2, kv3_low, kv3_high, q_own, q_other, out, kv, q_all, v_turned, q_even, q_odd, s_even, s_odd, max_even, max_odd, acc, total, info_v, info, sem):
    j, yl, z = place[0], place[4], place[5]
    copies = [
        pltpu.make_async_copy(src, dst, sem.at[i])
        for i, (src, dst) in enumerate((
            (kv0, kv.at[0]), (kv1, kv.at[1]), (kv2, kv.at[2]), (kv3_low, kv.at[3, pl.ds(0, 2)]), (kv3_high, kv.at[3, pl.ds(2, 2)]),
            (q_own, q_all.at[0]), (q_other, q_all.at[1]),
        ))
    ]
    for copy in copies:
        copy.start()
    for copy in copies:
        copy.wait()
    for side in range(2):
        info_v[16 + 4 * side:20 + 4 * side, :] = q_all[side, 2048:2064, :].astype(F32)[0:4].astype(jnp.int32)
    block_docs = []
    for ch in range(4):
        for i in range(BLOCKS):
            rows = kv[i, ch, 256:272, :].astype(F32)
            block_docs.append(jnp.concatenate([rows[r:r + 1] for r in range(4)], axis=1))
    block_docs = jnp.concatenate(block_docs, axis=0)
    lane = lax.broadcasted_iota(jnp.int32, (16, 128), 1)
    counts = jnp.zeros((16, 128), F32)
    for d in range(8):
        below = jnp.sum((block_docs < d).astype(F32), axis=1, keepdims=True)
        counts = jnp.where(lane == d, below, counts)
    info_v[0:16, :] = counts.astype(jnp.int32)
    to_scalars = pltpu.make_async_copy(info_v, info, sem.at[7])
    to_scalars.start()
    for ch in range(4):
        for i in range(BLOCKS):
            v_turned[:, (ch * BLOCKS + i) * 128:(ch * BLOCKS + i + 1) * 128] = kv[i, ch, 128:256, :].T
    to_scalars.wait()
    where = [(z + shift) % 4 for shift in (0, 3, 1, 2)]
    key_iota = lax.broadcasted_iota(jnp.int32, (128, 512), 0)
    row_iota = lax.broadcasted_iota(jnp.int32, (1, 512), 1) % 128

    first_doc = jnp.minimum(info[16, 0], info[20, 0])
    begin = jnp.int32(0)
    for ch in range(4):
        fewest = functools.reduce(jnp.minimum, [info[ch * BLOCKS + i, first_doc] for i in range(BLOCKS)])
        begin = begin + (fewest >= (j + 1) * 128).astype(jnp.int32)
    end = z // BLOCKS + 1

    def begin_scores(tile, q_ref, max_ref):
        side, row0 = tile // 4, pl.multiple_of(tile % 4 * 128, 128)
        for h in range(4):
            q_ref[h * 128:(h + 1) * 128, :] = q_all[side, pl.ds(pl.multiple_of((h ^ j) * 512, 512) + row0, 128), :]
        max_ref[...] = jnp.full((1, 512), EMPTY, F32)

    def is_full(tile, ch):
        yl_q = jnp.where(tile // 4 == 0, yl, 1 - yl)
        q_min = (2 * z + yl_q) * 512 + tile % 4 * 128
        last = info[16 + tile, 127]
        most = functools.reduce(jnp.maximum, [info[ch * BLOCKS + i, last] for i in range(BLOCKS)])
        k_max = (2 * (ch * BLOCKS + BLOCKS - 1) + yl) * 512 + j * 128 + 127
        return (k_max <= q_min) & (most <= j * 128)

    def put_scores(tile, ch, masked, q_ref, s_ref, max_ref):
        keys = jnp.concatenate([kv[i, ch, 0:128, :] for i in range(BLOCKS)], axis=0)
        s = lax.dot_general(keys, q_ref[...], (((1,), (1,)), ((), ())), preferred_element_type=F32) * SCALE2
        if masked:
            yl_q = jnp.where(tile // 4 == 0, yl, 1 - yl)
            q_pos = (2 * z + yl_q) * 512 + tile % 4 * 128 + row_iota
            row_docs = jnp.concatenate([info_v[pl.ds(16 + tile, 1), :]] * 4, axis=1)
            parts = []
            for i in range(BLOCKS):
                low = jnp.zeros((1, 512), jnp.int32)
                for d in range(8):
                    low = jnp.where(row_docs == d, info[ch * BLOCKS + i, d], low)
                low = low - j * 128
                high = q_pos - ((2 * (ch * 4 + where[i]) + yl) * 512 + j * 128)
                ok = (key_iota >= low) & (key_iota <= high)
                parts.append(jnp.where(ok, s[i * 128:(i + 1) * 128], MASKED))
            s = jnp.concatenate(parts, axis=0)
        s_ref[ch] = s
        max_ref[...] = jnp.maximum(max_ref[...], jnp.max(s, axis=0, keepdims=True))

    def add_up(ch, s_ref, max_ref):
        w = jnp.exp2(s_ref[ch] - max_ref[...])
        cols = pl.ds(pl.multiple_of(ch * (BLOCKS * 128), BLOCKS * 128), BLOCKS * 128)
        acc[...] += jnp.dot(v_turned[:, cols], w.astype(BF), preferred_element_type=F32)
        total[...] += jnp.sum(w, axis=0, keepdims=True)

    def finish(tile, max_ref):
        run_sum, run_max = total[...], max_ref[...]
        seen = run_sum > 0
        o = (acc[...] * (1.0 / jnp.where(seen, run_sum, 1.0))).astype(BF)
        lse = jnp.where(seen, run_max + jnp.log2(jnp.where(seen, run_sum, 1.0)), EMPTY)
        hi = lse.astype(BF).astype(F32)
        mid = (lse - hi).astype(BF).astype(F32)
        lo = lse - hi - mid
        dest = jnp.where(tile // 4 == 0, yl, 1 - yl) * 4 + tile % 4
        rows = [part[:, h * 128:(h + 1) * 128] for part in (hi, mid, lo) for h in range(4)]
        rows.append(jnp.zeros((4, 128), F32))
        for h in range(4):
            out[dest, h * 128:(h + 1) * 128, :] = o[:, h * 128:(h + 1) * 128]
        out[dest, 512:528, :] = jnp.concatenate(rows, axis=0).astype(BF)
        acc[...] = jnp.zeros((128, 512), F32)
        total[...] = jnp.zeros((1, 512), F32)

    def sweep(tile, put, use):
        if put is not None:
            begin_scores(tile, put[0], put[2])

        def one(ch, carry):
            def work(masked):
                if put is not None:
                    put_scores(tile, ch, masked, *put)
                if use is not None:
                    add_up(ch, use[1], use[2])

            if put is None:
                work(False)
            else:
                full = is_full(tile, ch)
                pl.when(full)(lambda: work(False))
                pl.when(jnp.logical_not(full))(lambda: work(True))
            return carry

        lax.fori_loop(begin, end, one, 0)
        if use is not None:
            finish(tile - 1, use[2])

    even, odd = (q_even, s_even, max_even), (q_odd, s_odd, max_odd)
    acc[...] = jnp.zeros((128, 512), F32)
    total[...] = jnp.zeros((1, 512), F32)
    sweep(0, even, None)

    def two_tiles(pair, carry):
        sweep(2 * pair + 1, odd, even)
        sweep(2 * pair + 2, even, odd)
        return carry

    lax.fori_loop(0, 3, two_tiles, 0)
    sweep(7, odd, even)
    sweep(8, None, odd)


def combine_kernel(parts, out, copies):
    count = parts.shape[0]
    tails = [parts[s, 512:528, :].astype(F32) for s in range(count)]
    for h in range(4):
        lses = [t[h:h + 1] + t[4 + h:5 + h] + t[8 + h:9 + h] for t in tails]
        top = functools.reduce(jnp.maximum, lses)
        weights = [jnp.exp2(v - top) for v in lses]
        inverse = 1.0 / sum(weights)
        rows = slice(h * 128, (h + 1) * 128)
        total = sum(w * inverse * parts[s, rows, :].astype(F32) for s, w in enumerate(weights)).astype(BF)
        out[rows, :] = total
        for copy in range(copies.shape[0]):
            copies[copy, rows, :] = total


def student_kernel(place, weight_t, att, kept, received, teacher, out, weights, sem):
    copies = []
    for part in range(4):
        rows = pl.ds(part * 192, 192)
        copies.append(pltpu.make_async_copy(weight_t.at[rows], weights.at[rows], sem.at[part]))
    for copy in copies:
        copy.start()
    for chip in range(8):
        first = (chip % 4 * 4 + chip // 4 * 2) * 256
        for i in range(4):
            out[chip, 768 + i * 32:800 + i * 32, :] = teacher[:, first + i * 128:first + (i + 1) * 128]
    att_all = att[...].reshape(2048, 128)
    for part in range(4):
        source = part ^ place[0]
        hidden = jnp.where(source < 2, kept[source % 2].astype(F32), received[source % 2].astype(F32))
        copies[part].wait()
        rows = slice(part * 192, (part + 1) * 192)
        mixed = jnp.dot(weights[rows, :], att_all, preferred_element_type=F32)
        student = (hidden + mixed).astype(BF)
        for copy in range(8):
            out[copy, rows, :] = student


def projected(student, projector_t):
    total = 0.0
    for g in range(4):
        both = jnp.concatenate([student[g, 0:768, :], student[4 + g, 0:768, :]], axis=1)
        total = total + jnp.dot(projector_t[:, g * 768:(g + 1) * 768], both, preferred_element_type=F32)
    return total


def teacher_rows(own, other, core, chunk_core):
    pieces = []
    for xl in range(2):
        for t in range(4):
            source = t // 2 * 4 + xl * 2 + chunk_core
            halves = []
            for i in range(2):
                rows = pl.ds(pl.multiple_of(768 + core * 64 + i * 32, 32), 32)
                halves.append(jnp.where(core == t % 2, own[source, rows, :].astype(F32), other[source, rows, :].astype(F32)))
            pieces.append(jnp.concatenate(halves, axis=1))
    return jnp.concatenate(pieces, axis=0)


def gradient_rows(own, other, mismatch, near):
    rows = []
    for zh in range(4):
        cut = pl.ds(pl.multiple_of(near * 192, 64), 192)
        rows.append(jnp.concatenate([ref[xl * 4 + zh, cut, :] for ref in (own, other) for xl in range(2)], axis=1))
    return jnp.dot(jnp.concatenate(rows, axis=0), mismatch[...], preferred_element_type=F32).reshape(8, 96, 256)


def own_projected_kernel(own, projector_t, out):
    out[...] = projected(own, projector_t).T


def second_kernel(place, own, other, projector_t, own_projected, mismatch, up, down):
    core = place[2]
    mismatch[0:256, :] = (own_projected[...] - teacher_rows(own, other, core, core)).astype(BF)
    mismatch[256:512, :] = (projected(other, projector_t).T - teacher_rows(own, other, core, 1 - core)).astype(BF)
    grad = gradient_rows(own, other, mismatch, (place[6] + 2) % 4).astype(BF)
    up[...] = grad[0:4]
    down[...] = grad[4:8]


def first_kernel(place, own, other, mismatch, up, down):
    up[...] = gradient_rows(own, other, mismatch, (place[6] + 1) % 4).astype(BF)
    down[...] = gradient_rows(own, other, mismatch, (place[6] + 3) % 4).astype(BF)


def kept_kernel(place, own, other, mismatch, out):
    out[...] = gradient_rows(own, other, mismatch, place[6])


def add_kernel(kept, below, above, far_below, far_above, out):
    near = kept[...] + below[...].astype(F32) + above[...].astype(F32)
    out[0:4] = (near[0:4] + far_below[...].astype(F32)).astype(BF)
    out[4:8] = (near[4:8] + far_above[...].astype(F32)).astype(BF)


def final_kernel(terms, out):
    out[...] = sum(terms[i].astype(F32) for i in range(terms.shape[0])) * (16384 ** -0.5)


VMEM = pl.BlockSpec(memory_space=pltpu.VMEM)
SMEM = pl.BlockSpec(memory_space=pltpu.SMEM)
ANY = pl.BlockSpec(memory_space=pl.ANY)
HBM = pl.BlockSpec(memory_space=pltpu.HBM)


def call(kernel, out_shape, specs, operands, limit, flops=0, scratch=()):
    single = not isinstance(out_shape, list)
    return pl.pallas_call(
        kernel,
        out_shape=out_shape,
        in_specs=specs,
        out_specs=VMEM if single else [VMEM] * len(out_shape),
        scratch_shapes=list(scratch),
        compiler_params=pltpu.CompilerParams(vmem_limit_bytes=limit * 1024 * 1024),
        cost_estimate=pl.CostEstimate(flops=flops, bytes_accessed=4 * 1024 * 1024, transcendentals=0),
    )(*operands)


def shape(*dims, dtype=BF):
    return jax.ShapeDtypeStruct(dims, dtype)


def start(place, keys, values, docs, queries, hidden_t):
    def block(*dims):
        return pl.BlockSpec(dims, lambda i, place: (0,) * len(dims))

    picked = pl.BlockSpec((128, 128), lambda i, place: (place[0], place[1]))
    outs = [(4, 272, 128), (16, 128), (896, 128), (2, 192, 128)]
    return pl.pallas_call(
        start_kernel,
        grid_spec=pltpu.PrefetchScalarGridSpec(
            num_scalar_prefetch=1,
            grid=(1,),
            in_specs=[picked, picked, block(4, 128), block(512, 128), block(192, 512)],
            out_specs=[block(*dims) for dims in outs],
        ),
        out_shape=[shape(*dims) for dims in outs],
    )(place, keys, values, docs, queries, hidden_t)


def transposed(x):
    rows, columns = x.shape
    return pl.pallas_call(
        transpose_kernel,
        grid=(4,),
        in_specs=[pl.BlockSpec((rows // 4, columns), lambda i: (i, 0))],
        out_specs=[pl.BlockSpec((columns, rows // 4), lambda i: (0, i)), pl.BlockSpec((8, 128), lambda i: (0, 0))],
        out_shape=[shape(columns, rows), shape(8, 128, dtype=F32)],
        compiler_params=pltpu.CompilerParams(vmem_limit_bytes=58 * 1024 * 1024),
    )(x)


def on_device(queries, keys, values, doc_ids, hidden, out_weight, projector, teacher):
    zl, yl, xl, c = lax.axis_index("zl"), lax.axis_index("yl"), lax.axis_index("xl"), lax.axis_index("c")
    j = xl * 2 + c
    z = lax.axis_index("zh") * 4 + zl
    g = lax.axis_index("yh") * 2 + lax.axis_index("xh")
    swap = [(0, 1), (1, 0)]
    place = jnp.stack([j, g, c, xl, yl, z, zl]).astype(jnp.int32)

    def from_z(x, shift):
        return lax.ppermute(x, ("zh", "zl"), [((i + shift) % 16, i) for i in range(16)])

    docs = doc_ids.reshape(4, 128)
    packed, doc_rows, sent, hidden_kept = start(place, keys, values, docs, queries, hidden.T)
    kv_own = lax.all_to_all(packed, "zh", 0, 0)
    kv_below, kv_above = from_z(kv_own, -1), from_z(kv_own, 1)
    kv_low, kv_high = from_z(kv_own[0:2], -2), from_z(kv_own[2:4], 2)

    projector_t, token = transposed(projector)
    half = shape(2, 192, 128)
    two, hidden_kept = call(
        turn_kernel, [shape(1408, 128), half], [SMEM] + [VMEM] * 3, (place, sent, lax.ppermute(sent, "c", swap), hidden_kept), 16
    )
    q_own, hidden_received = call(
        join_kernel, [shape(2064, 128), half], [VMEM] * 4, (two, lax.ppermute(two, "xl", swap), doc_rows, token), 16
    )
    q_other = lax.ppermute(q_own, "yl", swap)
    weight_t = lax.all_gather(out_weight.T, GROUP, axis=0, tiled=True)
    partial = call(
        attend_kernel,
        shape(8, 528, 128),
        [SMEM] + [ANY] * 7,
        (place, kv_own, kv_below, kv_above, kv_low, kv_high, q_own, q_other),
        40,
        2 * 10 ** 10,
        scratch=[
            pltpu.VMEM((4, 4, 272, 128), BF),
            pltpu.VMEM((2, 2064, 128), BF),
            pltpu.VMEM((128, 2048), BF),
            pltpu.VMEM((512, 128), BF),
            pltpu.VMEM((512, 128), BF),
            pltpu.VMEM((4, 512, 512), F32),
            pltpu.VMEM((4, 512, 512), F32),
            pltpu.VMEM((1, 512), F32),
            pltpu.VMEM((1, 512), F32),
            pltpu.VMEM((128, 512), F32),
            pltpu.VMEM((1, 512), F32),
            pltpu.VMEM((24, 128), jnp.int32),
            pltpu.SMEM((24, 128), jnp.int32),
            pltpu.SemaphoreType.DMA((8,)),
        ],
    )
    att_rows, att_copies = call(
        combine_kernel, [shape(512, 128), shape(4, 512, 128)], [VMEM], (lax.all_to_all(partial, OCTET, 0, 0),), 16
    )

    att_head = lax.all_to_all(att_rows.reshape(4, 128, 128), GROUP, 0, 0)
    attended = jnp.transpose(att_head, (0, 2, 1)).reshape(512, 128)

    att_all = lax.all_to_all(att_copies, HEADSETS, 0, 0)
    student = call(
        student_kernel,
        shape(8, 896, 128),
        [SMEM, HBM] + [VMEM] * 4,
        (place, weight_t, att_all, hidden_kept, hidden_received, teacher),
        24,
        scratch=[pltpu.VMEM((768, 2048), BF), pltpu.SemaphoreType.DMA((4,))],
    )
    own = lax.all_to_all(student, CHIPS, 0, 0)
    other = lax.ppermute(own, "c", swap)

    own_projected = call(own_projected_kernel, shape(256, 256, dtype=F32), [VMEM] * 2, (own, projector_t), 24, 4 * 10 ** 8)
    mismatch, up, down = call(
        second_kernel,
        [shape(512, 256), shape(4, 96, 256), shape(4, 96, 256)],
        [SMEM] + [VMEM] * 4,
        (place, own, other, projector_t, own_projected),
        32,
        8 * 10 ** 8,
    )
    far_below, far_above = from_z(up, -2), from_z(down, 2)
    up, down = call(
        first_kernel, [shape(8, 96, 256), shape(8, 96, 256)], [SMEM] + [VMEM] * 3, (place, own, other, mismatch), 32, 4 * 10 ** 8
    )
    below, above = from_z(up, -1), from_z(down, 1)
    kept = call(kept_kernel, shape(8, 96, 256, dtype=F32), [SMEM] + [VMEM] * 3, (place, own, other, mismatch), 32, 2 * 10 ** 8)
    near = call(add_kernel, shape(8, 96, 256), [VMEM] * 5, (kept, below, above, far_below, far_above), 16)
    grad = call(final_kernel, shape(96, 256, dtype=F32), [VMEM], (lax.all_to_all(near, ("zh", "yl"), 0, 0),), 8)
    return grad, attended


def solution(mesh):
    fine = Mesh(mesh.devices.reshape(4, 4, 2, 2, 2, 2, 2), ("zh", "zl", "yl", "yh", "xh", "xl", "c"))
    return jax.shard_map(
        on_device,
        mesh=fine,
        in_specs=(
            P(CTX, HID),
            P(CTX, None),
            P(CTX, None),
            P(CTX),
            P(CTX, HID),
            P(None, HID),
            P(None, HID),
            P(CTX + HID, None),
        ),
        out_specs=(P(CTX, HID), P(CTX, HID)),
        check_vma=False,
    )
```

```python
import functools

import jax
import jax.numpy as jnp
from jax import lax
from jax.experimental import pallas as pl
from jax.experimental.pallas import tpu as pltpu
from jax.sharding import Mesh
from jax.sharding import PartitionSpec as P

HEAD = 128
SCALE2 = HEAD ** -0.5 * 1.4426950408889634
EMPTY = -1e30
MASKED = -2e30
BF = jnp.bfloat16
F32 = jnp.float32
CTX = ("zh", "zl", "yl")
HID = ("yh", "xh", "xl", "c")
GROUP = ("xl", "c")
OCTET = ("yl", "xl", "c")
HEADSETS = ("yh", "xh")
CHIPS = ("xl", "yh", "xh")
BLOCKS = 4


def start_kernel(place, keys, values, docs, weight_t, hidden_t, packed, doc_rows, both, sem):
    copies = [
        pltpu.make_async_copy(weight_t, both.at[:, pl.ds(0, 2048)], sem.at[0]),
        pltpu.make_async_copy(hidden_t, both.at[:, pl.ds(2048, 512)], sem.at[1]),
    ]
    for copy in copies:
        copy.start()
    rows = jnp.concatenate([docs[...].astype(F32), jnp.zeros((12, 128), F32)], axis=0).astype(BF)
    for i in range(4):
        packed[i, 0:128, :] = keys[...]
        packed[i, 128:256, :] = values[...]
        packed[i, 256:272, :] = rows
    doc_rows[...] = rows
    for copy in copies:
        copy.wait()


def attend_kernel(place, kv0, kv1, kv2, kv3_low, kv3_high, q_own, q_other, out, kv, q_all, v_turned, q_even, q_odd, s_even, s_odd, max_even, max_odd, acc, total, info_v, info, sem):
    j, yl, z = place[0], place[4], place[5]
    copies = [
        pltpu.make_async_copy(src, dst, sem.at[i])
        for i, (src, dst) in enumerate((
            (kv0, kv.at[0]), (kv1, kv.at[1]), (kv2, kv.at[2]), (kv3_low, kv.at[3, pl.ds(0, 2)]), (kv3_high, kv.at[3, pl.ds(2, 2)]),
            (q_own, q_all.at[0]), (q_other, q_all.at[1]),
        ))
    ]
    for copy in copies:
        copy.start()
    for copy in copies:
        copy.wait()
    for side in range(2):
        info_v[16 + 4 * side:20 + 4 * side, :] = q_all[side, 2048:2064, :].astype(F32)[0:4].astype(jnp.int32)
    block_docs = []
    for ch in range(4):
        for i in range(BLOCKS):
            rows = kv[i, ch, 256:272, :].astype(F32)
            block_docs.append(jnp.concatenate([rows[r:r + 1] for r in range(4)], axis=1))
    block_docs = jnp.concatenate(block_docs, axis=0)
    lane = lax.broadcasted_iota(jnp.int32, (16, 128), 1)
    counts = jnp.zeros((16, 128), F32)
    for d in range(8):
        below = jnp.sum((block_docs < d).astype(F32), axis=1, keepdims=True)
        counts = jnp.where(lane == d, below, counts)
    info_v[0:16, :] = counts.astype(jnp.int32)
    to_scalars = pltpu.make_async_copy(info_v, info, sem.at[7])
    to_scalars.start()
    for ch in range(4):
        for i in range(BLOCKS):
            v_turned[:, (ch * BLOCKS + i) * 128:(ch * BLOCKS + i + 1) * 128] = kv[i, ch, 128:256, :].T
    to_scalars.wait()
    where = [(z + shift) % 4 for shift in (0, 3, 1, 2)]
    key_iota = lax.broadcasted_iota(jnp.int32, (128, 512), 0)
    row_iota = lax.broadcasted_iota(jnp.int32, (1, 512), 1) % 128

    first_doc = jnp.minimum(info[16, 0], info[20, 0])
    begin = jnp.int32(0)
    for ch in range(4):
        fewest = functools.reduce(jnp.minimum, [info[ch * BLOCKS + i, first_doc] for i in range(BLOCKS)])
        begin = begin + (fewest >= (j + 1) * 128).astype(jnp.int32)
    end = z // BLOCKS + 1

    def begin_scores(tile, q_ref, max_ref):
        side, row0 = tile // 4, pl.multiple_of(tile % 4 * 128, 128)
        for h in range(4):
            q_ref[h * 128:(h + 1) * 128, :] = q_all[side, pl.ds(h * 512 + row0, 128), :]
        max_ref[...] = jnp.full((1, 512), EMPTY, F32)

    def is_full(tile, ch):
        yl_q = jnp.where(tile // 4 == 0, yl, 1 - yl)
        q_min = (2 * z + yl_q) * 512 + tile % 4 * 128
        last = info[16 + tile, 127]
        most = functools.reduce(jnp.maximum, [info[ch * BLOCKS + i, last] for i in range(BLOCKS)])
        k_max = (2 * (ch * BLOCKS + BLOCKS - 1) + yl) * 512 + j * 128 + 127
        return (k_max <= q_min) & (most <= j * 128)

    def put_scores(tile, ch, masked, q_ref, s_ref, max_ref):
        keys = jnp.concatenate([kv[i, ch, 0:128, :] for i in range(BLOCKS)], axis=0)
        s = lax.dot_general(keys, q_ref[...], (((1,), (1,)), ((), ())), preferred_element_type=F32) * SCALE2
        if masked:
            yl_q = jnp.where(tile // 4 == 0, yl, 1 - yl)
            q_pos = (2 * z + yl_q) * 512 + tile % 4 * 128 + row_iota
            row_docs = jnp.concatenate([info_v[pl.ds(16 + tile, 1), :]] * 4, axis=1)
            parts = []
            for i in range(BLOCKS):
                low = jnp.zeros((1, 512), jnp.int32)
                for d in range(8):
                    low = jnp.where(row_docs == d, info[ch * BLOCKS + i, d], low)
                low = low - j * 128
                high = q_pos - ((2 * (ch * 4 + where[i]) + yl) * 512 + j * 128)
                ok = (key_iota >= low) & (key_iota <= high)
                parts.append(jnp.where(ok, s[i * 128:(i + 1) * 128], MASKED))
            s = jnp.concatenate(parts, axis=0)
        s_ref[ch] = s
        max_ref[...] = jnp.maximum(max_ref[...], jnp.max(s, axis=0, keepdims=True))

    def add_up(ch, s_ref, max_ref):
        w = jnp.exp2(s_ref[ch] - max_ref[...])
        cols = pl.ds(pl.multiple_of(ch * (BLOCKS * 128), BLOCKS * 128), BLOCKS * 128)
        acc[...] += jnp.dot(v_turned[:, cols], w.astype(BF), preferred_element_type=F32)
        total[...] += jnp.sum(w, axis=0, keepdims=True)

    def finish(tile, max_ref):
        run_sum, run_max = total[...], max_ref[...]
        seen = run_sum > 0
        o = (acc[...] * (1.0 / jnp.where(seen, run_sum, 1.0))).astype(BF)
        lse = jnp.where(seen, run_max + jnp.log2(jnp.where(seen, run_sum, 1.0)), EMPTY)
        hi = lse.astype(BF).astype(F32)
        mid = (lse - hi).astype(BF).astype(F32)
        lo = lse - hi - mid
        dest = jnp.where(tile // 4 == 0, yl, 1 - yl) * 4 + tile % 4
        rows = [part[:, h * 128:(h + 1) * 128] for part in (hi, mid, lo) for h in range(4)]
        rows.append(jnp.zeros((4, 128), F32))
        for h in range(4):
            out[dest, h * 128:(h + 1) * 128, :] = o[:, h * 128:(h + 1) * 128]
        out[dest, 512:528, :] = jnp.concatenate(rows, axis=0).astype(BF)
        acc[...] = jnp.zeros((128, 512), F32)
        total[...] = jnp.zeros((1, 512), F32)

    def sweep(tile, put, use):
        if put is not None:
            begin_scores(tile, put[0], put[2])

        def one(ch, carry):
            def work(masked):
                if put is not None:
                    put_scores(tile, ch, masked, *put)
                if use is not None:
                    add_up(ch, use[1], use[2])

            if put is None:
                work(False)
            else:
                full = is_full(tile, ch)
                pl.when(full)(lambda: work(False))
                pl.when(jnp.logical_not(full))(lambda: work(True))
            return carry

        lax.fori_loop(begin, end, one, 0)
        if use is not None:
            finish(tile - 1, use[2])

    even, odd = (q_even, s_even, max_even), (q_odd, s_odd, max_odd)
    acc[...] = jnp.zeros((128, 512), F32)
    total[...] = jnp.zeros((1, 512), F32)
    sweep(0, even, None)

    def two_tiles(pair, carry):
        sweep(2 * pair + 1, odd, even)
        sweep(2 * pair + 2, even, odd)
        return carry

    lax.fori_loop(0, 3, two_tiles, 0)
    sweep(7, odd, even)
    sweep(8, None, odd)


def combine_kernel(parts, out, copies):
    count = parts.shape[0]
    tails = [parts[s, 512:528, :].astype(F32) for s in range(count)]
    for h in range(4):
        lses = [t[h:h + 1] + t[4 + h:5 + h] + t[8 + h:9 + h] for t in tails]
        top = functools.reduce(jnp.maximum, lses)
        weights = [jnp.exp2(v - top) for v in lses]
        inverse = 1.0 / sum(weights)
        rows = slice(h * 128, (h + 1) * 128)
        total = sum(w * inverse * parts[s, rows, :].astype(F32) for s, w in enumerate(weights)).astype(BF)
        out[rows, :] = total
        for copy in range(copies.shape[0]):
            copies[copy, rows, :] = total


def student_kernel(place, gathered, att, teacher, out, weights, hidden, sem):
    copies = []
    own_rows = pl.ds(pl.multiple_of(2048 + place[0] * 128, 128), 128)
    hidden_copy = pltpu.make_async_copy(gathered.at[:, own_rows], hidden, sem.at[4])
    for part in range(4):
        rows = pl.ds(part * 192, 192)
        copies.append(pltpu.make_async_copy(gathered.at[rows, pl.ds(0, 2048)], weights.at[rows], sem.at[part]))
    copies[0].start()
    hidden_copy.start()
    for copy in copies[1:]:
        copy.start()
    for chip in range(8):
        first = (chip % 4 * 4 + chip // 4 * 2) * 256
        for i in range(4):
            out[chip, 768 + i * 32:800 + i * 32, :] = teacher[:, first + i * 128:first + (i + 1) * 128]
    att_all = att[...].reshape(2048, 128)
    hidden_copy.wait()
    for part in range(4):
        copies[part].wait()
        rows = slice(part * 192, (part + 1) * 192)
        mixed = jnp.dot(weights[rows, :], att_all, preferred_element_type=F32)
        student = (hidden[rows, :].astype(F32) + mixed).astype(BF)
        for copy in range(8):
            out[copy, rows, :] = student


def projected(student, projector_t):
    total = 0.0
    for g in range(4):
        both = jnp.concatenate([student[g, 0:768, :], student[4 + g, 0:768, :]], axis=1)
        total = total + jnp.dot(projector_t[:, g * 768:(g + 1) * 768], both, preferred_element_type=F32)
    return total


def teacher_rows(own, other, core, chunk_core):
    pieces = []
    for xl in range(2):
        for t in range(4):
            source = t // 2 * 4 + xl * 2 + chunk_core
            halves = []
            for i in range(2):
                rows = pl.ds(pl.multiple_of(768 + core * 64 + i * 32, 32), 32)
                halves.append(jnp.where(core == t % 2, own[source, rows, :].astype(F32), other[source, rows, :].astype(F32)))
            pieces.append(jnp.concatenate(halves, axis=1))
    return jnp.concatenate(pieces, axis=0)


def gradient_rows(own, other, mismatch, near):
    rows = []
    for zh in range(4):
        cut = pl.ds(pl.multiple_of(near * 192, 64), 192)
        rows.append(jnp.concatenate([ref[xl * 4 + zh, cut, :] for ref in (own, other) for xl in range(2)], axis=1))
    return jnp.dot(jnp.concatenate(rows, axis=0), mismatch[...], preferred_element_type=F32).reshape(8, 96, 256)


def own_projected_kernel(own, projector, projector_t, out):
    for g in range(4):
        projector_t[:, g * 768:(g + 1) * 768] = projector[g * 768:(g + 1) * 768, :].T
    out[...] = projected(own, projector_t).T


def second_kernel(place, own, other, projector_t, own_projected, mismatch, up, down):
    core = place[2]
    mismatch[0:256, :] = (own_projected[...] - teacher_rows(own, other, core, core)).astype(BF)
    mismatch[256:512, :] = (projected(other, projector_t).T - teacher_rows(own, other, core, 1 - core)).astype(BF)
    grad = gradient_rows(own, other, mismatch, (place[6] + 2) % 4).astype(BF)
    up[...] = grad[0:4]
    down[...] = grad[4:8]


def first_kernel(place, own, other, mismatch, up, down):
    up[...] = gradient_rows(own, other, mismatch, (place[6] + 1) % 4).astype(BF)
    down[...] = gradient_rows(own, other, mismatch, (place[6] + 3) % 4).astype(BF)


def kept_kernel(place, own, other, mismatch, out):
    out[...] = gradient_rows(own, other, mismatch, place[6])


def add_kernel(kept, below, above, far_below, far_above, out):
    near = kept[...] + below[...].astype(F32) + above[...].astype(F32)
    out[0:4] = (near[0:4] + far_below[...].astype(F32)).astype(BF)
    out[4:8] = (near[4:8] + far_above[...].astype(F32)).astype(BF)


def final_kernel(terms, out):
    out[...] = sum(terms[i].astype(F32) for i in range(terms.shape[0])) * (16384 ** -0.5)


VMEM = pl.BlockSpec(memory_space=pltpu.VMEM)
SMEM = pl.BlockSpec(memory_space=pltpu.SMEM)
ANY = pl.BlockSpec(memory_space=pl.ANY)
HBM = pl.BlockSpec(memory_space=pltpu.HBM)


def call(kernel, out_shape, specs, operands, limit, flops=0, scratch=()):
    single = not isinstance(out_shape, list)
    return pl.pallas_call(
        kernel,
        out_shape=out_shape,
        in_specs=specs,
        out_specs=VMEM if single else [VMEM] * len(out_shape),
        scratch_shapes=list(scratch),
        compiler_params=pltpu.CompilerParams(vmem_limit_bytes=limit * 1024 * 1024),
        cost_estimate=pl.CostEstimate(flops=flops, bytes_accessed=4 * 1024 * 1024, transcendentals=0),
    )(*operands)


def shape(*dims, dtype=BF):
    return jax.ShapeDtypeStruct(dims, dtype)


def start(place, keys, values, docs, weight_t, hidden_t):
    def block(*dims):
        return pl.BlockSpec(dims, lambda i, place: (0,) * len(dims))

    picked = pl.BlockSpec((128, 128), lambda i, place: (place[0], place[1]))
    return pl.pallas_call(
        start_kernel,
        grid_spec=pltpu.PrefetchScalarGridSpec(
            num_scalar_prefetch=1,
            grid=(1,),
            in_specs=[picked, picked, block(4, 128), ANY, ANY],
            out_specs=[block(4, 272, 128), block(16, 128), ANY],
            scratch_shapes=[pltpu.SemaphoreType.DMA((2,))],
        ),
        out_shape=[shape(4, 272, 128), shape(16, 128), shape(192, 2560)],
    )(place, keys, values, docs, weight_t, hidden_t)


def on_device(queries, keys, values, doc_ids, hidden, out_weight, projector, teacher):
    zl, yl, xl, c = lax.axis_index("zl"), lax.axis_index("yl"), lax.axis_index("xl"), lax.axis_index("c")
    j = xl * 2 + c
    z = lax.axis_index("zh") * 4 + zl
    g = lax.axis_index("yh") * 2 + lax.axis_index("xh")
    swap = [(0, 1), (1, 0)]
    place = jnp.stack([j, g, c, xl, yl, z, zl]).astype(jnp.int32)

    def from_z(x, shift):
        return lax.ppermute(x, ("zh", "zl"), [((i + shift) % 16, i) for i in range(16)])

    docs = doc_ids.reshape(4, 128)
    packed, doc_rows, both = start(place, keys, values, docs, out_weight.T, hidden.T)
    kv_own = lax.all_to_all(packed, "zh", 0, 0)
    kv_below, kv_above = from_z(kv_own, -1), from_z(kv_own, 1)
    kv_low, kv_high = from_z(kv_own[0:2], -2), from_z(kv_own[2:4], 2)

    q_own = jnp.concatenate([lax.all_gather(queries, GROUP, axis=0, tiled=True), doc_rows], axis=0)
    q_other = lax.ppermute(q_own, "yl", swap)
    gathered = lax.all_gather(both, GROUP, axis=0, tiled=True)

    partial = call(
        attend_kernel,
        shape(8, 528, 128),
        [SMEM] + [ANY] * 7,
        (place, kv_own, kv_below, kv_above, kv_low, kv_high, q_own, q_other),
        40,
        2 * 10 ** 10,
        scratch=[
            pltpu.VMEM((4, 4, 272, 128), BF),
            pltpu.VMEM((2, 2064, 128), BF),
            pltpu.VMEM((128, 2048), BF),
            pltpu.VMEM((512, 128), BF),
            pltpu.VMEM((512, 128), BF),
            pltpu.VMEM((4, 512, 512), F32),
            pltpu.VMEM((4, 512, 512), F32),
            pltpu.VMEM((1, 512), F32),
            pltpu.VMEM((1, 512), F32),
            pltpu.VMEM((128, 512), F32),
            pltpu.VMEM((1, 512), F32),
            pltpu.VMEM((24, 128), jnp.int32),
            pltpu.SMEM((24, 128), jnp.int32),
            pltpu.SemaphoreType.DMA((8,)),
        ],
    )
    att_rows, att_copies = call(
        combine_kernel, [shape(512, 128), shape(4, 512, 128)], [VMEM], (lax.all_to_all(partial, OCTET, 0, 0),), 16
    )

    att_head = lax.all_to_all(att_rows.reshape(4, 128, 128), GROUP, 0, 0)
    attended = jnp.transpose(att_head, (0, 2, 1)).reshape(512, 128)

    att_all = lax.all_to_all(att_copies, HEADSETS, 0, 0)
    student = call(
        student_kernel,
        shape(8, 896, 128),
        [SMEM, HBM, VMEM, VMEM],
        (place, gathered, att_all, teacher),
        24,
        scratch=[pltpu.VMEM((768, 2048), BF), pltpu.VMEM((768, 128), BF), pltpu.SemaphoreType.DMA((5,))],
    )
    own = lax.all_to_all(student, CHIPS, 0, 0)
    other = lax.ppermute(own, "c", swap)

    projector_t, own_projected = call(
        own_projected_kernel, [shape(256, 3072), shape(256, 256, dtype=F32)], [VMEM] * 2, (own, projector), 24, 4 * 10 ** 8
    )
    mismatch, up, down = call(
        second_kernel,
        [shape(512, 256), shape(4, 96, 256), shape(4, 96, 256)],
        [SMEM] + [VMEM] * 4,
        (place, own, other, projector_t, own_projected),
        32,
        8 * 10 ** 8,
    )
    far_below, far_above = from_z(up, -2), from_z(down, 2)
    up, down = call(
        first_kernel, [shape(8, 96, 256), shape(8, 96, 256)], [SMEM] + [VMEM] * 3, (place, own, other, mismatch), 32, 4 * 10 ** 8
    )
    below, above = from_z(up, -1), from_z(down, 1)
    kept = call(kept_kernel, shape(8, 96, 256, dtype=F32), [SMEM] + [VMEM] * 3, (place, own, other, mismatch), 32, 2 * 10 ** 8)
    near = call(add_kernel, shape(8, 96, 256), [VMEM] * 5, (kept, below, above, far_below, far_above), 16)
    grad = call(final_kernel, shape(96, 256, dtype=F32), [VMEM], (lax.all_to_all(near, ("zh", "yl"), 0, 0),), 8)
    return grad, attended


def solution(mesh):
    fine = Mesh(mesh.devices.reshape(4, 4, 2, 2, 2, 2, 2), ("zh", "zl", "yl", "yh", "xh", "xl", "c"))
    return jax.shard_map(
        on_device,
        mesh=fine,
        in_specs=(
            P(CTX, HID),
            P(CTX, None),
            P(CTX, None),
            P(CTX),
            P(CTX, HID),
            P(None, HID),
            P(None, HID),
            P(CTX + HID, None),
        ),
        out_specs=(P(CTX, HID), P(CTX, HID)),
        check_vma=False,
    )
```

```python
import functools

import jax
import jax.numpy as jnp
from jax import lax
from jax.experimental import pallas as pl
from jax.experimental.pallas import tpu as pltpu
from jax.sharding import Mesh
from jax.sharding import PartitionSpec as P

HEAD = 128
SCALE2 = HEAD ** -0.5 * 1.4426950408889634
EMPTY = -1e30
MASKED = -2e30
BF = jnp.bfloat16
F32 = jnp.float32
CTX = ("zh", "zl", "yl")
HID = ("yh", "xh", "xl", "c")
GROUP = ("xl", "c")
OCTET = ("yl", "xl", "c")
HEADSETS = ("yh", "xh")
CHIPS = ("xl", "yh", "xh")
BLOCKS = 4


def start_kernel(place, keys, values, docs, weight_t, hidden_t, packed, doc_rows, both, joined, sem):
    copies = [
        pltpu.make_async_copy(weight_t, joined.at[:, pl.ds(0, 2048)], sem.at[0]),
        pltpu.make_async_copy(hidden_t, joined.at[:, pl.ds(2048, 512)], sem.at[1]),
    ]
    for copy in copies:
        copy.start()
    rows = jnp.concatenate([docs[...].astype(F32), jnp.zeros((12, 128), F32)], axis=0).astype(BF)
    for i in range(4):
        packed[i, 0:128, :] = keys[...]
        packed[i, 128:256, :] = values[...]
        packed[i, 256:272, :] = rows
    doc_rows[...] = rows
    for copy in copies:
        copy.wait()
    last = pltpu.make_async_copy(joined, both, sem.at[2])
    last.start()
    last.wait()


def attend_kernel(place, kv0, kv1, kv2, kv3_low, kv3_high, q_own, q_other, out, kv, q_all, v_turned, q_even, q_odd, s_even, s_odd, max_even, max_odd, acc, total, info_v, info, sem):
    j, yl, z = place[0], place[4], place[5]
    copies = [
        pltpu.make_async_copy(src, dst, sem.at[i])
        for i, (src, dst) in enumerate((
            (kv0, kv.at[0]), (kv1, kv.at[1]), (kv2, kv.at[2]), (kv3_low, kv.at[3, pl.ds(0, 2)]), (kv3_high, kv.at[3, pl.ds(2, 2)]),
            (q_own, q_all.at[0]), (q_other, q_all.at[1]),
        ))
    ]
    for copy in copies:
        copy.start()
    for copy in copies:
        copy.wait()
    for side in range(2):
        info_v[16 + 4 * side:20 + 4 * side, :] = q_all[side, 2048:2064, :].astype(F32)[0:4].astype(jnp.int32)
    block_docs = []
    for ch in range(4):
        for i in range(BLOCKS):
            rows = kv[i, ch, 256:272, :].astype(F32)
            block_docs.append(jnp.concatenate([rows[r:r + 1] for r in range(4)], axis=1))
    block_docs = jnp.concatenate(block_docs, axis=0)
    lane = lax.broadcasted_iota(jnp.int32, (16, 128), 1)
    counts = jnp.zeros((16, 128), F32)
    for d in range(8):
        below = jnp.sum((block_docs < d).astype(F32), axis=1, keepdims=True)
        counts = jnp.where(lane == d, below, counts)
    info_v[0:16, :] = counts.astype(jnp.int32)
    to_scalars = pltpu.make_async_copy(info_v, info, sem.at[7])
    to_scalars.start()
    for ch in range(4):
        for i in range(BLOCKS):
            v_turned[:, (ch * BLOCKS + i) * 128:(ch * BLOCKS + i + 1) * 128] = kv[i, ch, 128:256, :].T
    to_scalars.wait()
    where = [(z + shift) % 4 for shift in (0, 3, 1, 2)]
    key_iota = lax.broadcasted_iota(jnp.int32, (128, 512), 0)
    row_iota = lax.broadcasted_iota(jnp.int32, (1, 512), 1) % 128

    first_doc = jnp.minimum(info[16, 0], info[20, 0])
    begin = jnp.int32(0)
    for ch in range(4):
        fewest = functools.reduce(jnp.minimum, [info[ch * BLOCKS + i, first_doc] for i in range(BLOCKS)])
        begin = begin + (fewest >= (j + 1) * 128).astype(jnp.int32)
    end = z // BLOCKS + 1

    def begin_scores(tile, q_ref, max_ref):
        side, row0 = tile // 4, pl.multiple_of(tile % 4 * 128, 128)
        for h in range(4):
            q_ref[h * 128:(h + 1) * 128, :] = q_all[side, pl.ds(h * 512 + row0, 128), :]
        max_ref[...] = jnp.full((1, 512), EMPTY, F32)

    def is_full(tile, ch):
        yl_q = jnp.where(tile // 4 == 0, yl, 1 - yl)
        q_min = (2 * z + yl_q) * 512 + tile % 4 * 128
        last = info[16 + tile, 127]
        most = functools.reduce(jnp.maximum, [info[ch * BLOCKS + i, last] for i in range(BLOCKS)])
        k_max = (2 * (ch * BLOCKS + BLOCKS - 1) + yl) * 512 + j * 128 + 127
        return (k_max <= q_min) & (most <= j * 128)

    def put_scores(tile, ch, masked, q_ref, s_ref, max_ref):
        keys = jnp.concatenate([kv[i, ch, 0:128, :] for i in range(BLOCKS)], axis=0)
        s = lax.dot_general(keys, q_ref[...], (((1,), (1,)), ((), ())), preferred_element_type=F32) * SCALE2
        if masked:
            yl_q = jnp.where(tile // 4 == 0, yl, 1 - yl)
            q_pos = (2 * z + yl_q) * 512 + tile % 4 * 128 + row_iota
            row_docs = jnp.concatenate([info_v[pl.ds(16 + tile, 1), :]] * 4, axis=1)
            parts = []
            for i in range(BLOCKS):
                low = jnp.zeros((1, 512), jnp.int32)
                for d in range(8):
                    low = jnp.where(row_docs == d, info[ch * BLOCKS + i, d], low)
                low = low - j * 128
                high = q_pos - ((2 * (ch * 4 + where[i]) + yl) * 512 + j * 128)
                ok = (key_iota >= low) & (key_iota <= high)
                parts.append(jnp.where(ok, s[i * 128:(i + 1) * 128], MASKED))
            s = jnp.concatenate(parts, axis=0)
        s_ref[ch] = s
        max_ref[...] = jnp.maximum(max_ref[...], jnp.max(s, axis=0, keepdims=True))

    def add_up(ch, s_ref, max_ref):
        w = jnp.exp2(s_ref[ch] - max_ref[...])
        cols = pl.ds(pl.multiple_of(ch * (BLOCKS * 128), BLOCKS * 128), BLOCKS * 128)
        acc[...] += jnp.dot(v_turned[:, cols], w.astype(BF), preferred_element_type=F32)
        total[...] += jnp.sum(w, axis=0, keepdims=True)

    def finish(tile, max_ref):
        run_sum, run_max = total[...], max_ref[...]
        seen = run_sum > 0
        o = (acc[...] * (1.0 / jnp.where(seen, run_sum, 1.0))).astype(BF)
        lse = jnp.where(seen, run_max + jnp.log2(jnp.where(seen, run_sum, 1.0)), EMPTY)
        hi = lse.astype(BF).astype(F32)
        mid = (lse - hi).astype(BF).astype(F32)
        lo = lse - hi - mid
        dest = jnp.where(tile // 4 == 0, yl, 1 - yl) * 4 + tile % 4
        rows = [part[:, h * 128:(h + 1) * 128] for part in (hi, mid, lo) for h in range(4)]
        rows.append(jnp.zeros((4, 128), F32))
        for h in range(4):
            out[dest, h * 128:(h + 1) * 128, :] = o[:, h * 128:(h + 1) * 128]
        out[dest, 512:528, :] = jnp.concatenate(rows, axis=0).astype(BF)
        acc[...] = jnp.zeros((128, 512), F32)
        total[...] = jnp.zeros((1, 512), F32)

    def sweep(tile, put, use):
        if put is not None:
            begin_scores(tile, put[0], put[2])

        def one(ch, carry):
            def work(masked):
                if put is not None:
                    put_scores(tile, ch, masked, *put)
                if use is not None:
                    add_up(ch, use[1], use[2])

            if put is None:
                work(False)
            else:
                full = is_full(tile, ch)
                pl.when(full)(lambda: work(False))
                pl.when(jnp.logical_not(full))(lambda: work(True))
            return carry

        lax.fori_loop(begin, end, one, 0)
        if use is not None:
            finish(tile - 1, use[2])

    even, odd = (q_even, s_even, max_even), (q_odd, s_odd, max_odd)
    acc[...] = jnp.zeros((128, 512), F32)
    total[...] = jnp.zeros((1, 512), F32)
    sweep(0, even, None)

    def two_tiles(pair, carry):
        sweep(2 * pair + 1, odd, even)
        sweep(2 * pair + 2, even, odd)
        return carry

    lax.fori_loop(0, 3, two_tiles, 0)
    sweep(7, odd, even)
    sweep(8, None, odd)


def combine_kernel(parts, out, copies):
    count = parts.shape[0]
    tails = [parts[s, 512:528, :].astype(F32) for s in range(count)]
    for h in range(4):
        lses = [t[h:h + 1] + t[4 + h:5 + h] + t[8 + h:9 + h] for t in tails]
        top = functools.reduce(jnp.maximum, lses)
        weights = [jnp.exp2(v - top) for v in lses]
        inverse = 1.0 / sum(weights)
        rows = slice(h * 128, (h + 1) * 128)
        total = sum(w * inverse * parts[s, rows, :].astype(F32) for s, w in enumerate(weights)).astype(BF)
        out[rows, :] = total
        for copy in range(copies.shape[0]):
            copies[copy, rows, :] = total


def student_kernel(place, gathered, att, teacher, out, weights, hidden, sem):
    copies = []
    own_rows = pl.ds(pl.multiple_of(2048 + place[0] * 128, 128), 128)
    hidden_copy = pltpu.make_async_copy(gathered.at[:, own_rows], hidden, sem.at[4])
    for part in range(4):
        rows = pl.ds(part * 192, 192)
        copies.append(pltpu.make_async_copy(gathered.at[rows, pl.ds(0, 2048)], weights.at[rows], sem.at[part]))
    copies[0].start()
    hidden_copy.start()
    for copy in copies[1:]:
        copy.start()
    for chip in range(8):
        first = (chip % 4 * 4 + chip // 4 * 2) * 256
        for i in range(4):
            out[chip, 768 + i * 32:800 + i * 32, :] = teacher[:, first + i * 128:first + (i + 1) * 128]
    att_all = att[...].reshape(2048, 128)
    hidden_copy.wait()
    for part in range(4):
        copies[part].wait()
        rows = slice(part * 192, (part + 1) * 192)
        mixed = jnp.dot(weights[rows, :], att_all, preferred_element_type=F32)
        student = (hidden[rows, :].astype(F32) + mixed).astype(BF)
        for copy in range(8):
            out[copy, rows, :] = student


def projected(student, projector_t):
    total = 0.0
    for g in range(4):
        both = jnp.concatenate([student[g, 0:768, :], student[4 + g, 0:768, :]], axis=1)
        total = total + jnp.dot(projector_t[:, g * 768:(g + 1) * 768], both, preferred_element_type=F32)
    return total


def teacher_rows(own, other, core, chunk_core):
    pieces = []
    for xl in range(2):
        for t in range(4):
            source = t // 2 * 4 + xl * 2 + chunk_core
            halves = []
            for i in range(2):
                rows = pl.ds(pl.multiple_of(768 + core * 64 + i * 32, 32), 32)
                halves.append(jnp.where(core == t % 2, own[source, rows, :].astype(F32), other[source, rows, :].astype(F32)))
            pieces.append(jnp.concatenate(halves, axis=1))
    return jnp.concatenate(pieces, axis=0)


def gradient_rows(own, other, mismatch, near):
    rows = []
    for zh in range(4):
        cut = pl.ds(pl.multiple_of(near * 192, 64), 192)
        rows.append(jnp.concatenate([ref[xl * 4 + zh, cut, :] for ref in (own, other) for xl in range(2)], axis=1))
    return jnp.dot(jnp.concatenate(rows, axis=0), mismatch[...], preferred_element_type=F32).reshape(8, 96, 256)


def own_projected_kernel(own, projector, projector_t, out):
    for g in range(4):
        projector_t[:, g * 768:(g + 1) * 768] = projector[g * 768:(g + 1) * 768, :].T
    out[...] = projected(own, projector_t).T


def second_kernel(place, own, other, projector_t, own_projected, mismatch, up, down):
    core = place[2]
    mismatch[0:256, :] = (own_projected[...] - teacher_rows(own, other, core, core)).astype(BF)
    mismatch[256:512, :] = (projected(other, projector_t).T - teacher_rows(own, other, core, 1 - core)).astype(BF)
    grad = gradient_rows(own, other, mismatch, (place[6] + 2) % 4).astype(BF)
    up[...] = grad[0:4]
    down[...] = grad[4:8]


def first_kernel(place, own, other, mismatch, up, down):
    up[...] = gradient_rows(own, other, mismatch, (place[6] + 1) % 4).astype(BF)
    down[...] = gradient_rows(own, other, mismatch, (place[6] + 3) % 4).astype(BF)


def kept_kernel(place, own, other, mismatch, out):
    out[...] = gradient_rows(own, other, mismatch, place[6])


def add_kernel(kept, below, above, far_below, far_above, out):
    near = kept[...] + below[...].astype(F32) + above[...].astype(F32)
    out[0:4] = (near[0:4] + far_below[...].astype(F32)).astype(BF)
    out[4:8] = (near[4:8] + far_above[...].astype(F32)).astype(BF)


def final_kernel(terms, out):
    out[...] = sum(terms[i].astype(F32) for i in range(terms.shape[0])) * (16384 ** -0.5)


VMEM = pl.BlockSpec(memory_space=pltpu.VMEM)
SMEM = pl.BlockSpec(memory_space=pltpu.SMEM)
ANY = pl.BlockSpec(memory_space=pl.ANY)
HBM = pl.BlockSpec(memory_space=pltpu.HBM)


def call(kernel, out_shape, specs, operands, limit, flops=0, scratch=()):
    single = not isinstance(out_shape, list)
    return pl.pallas_call(
        kernel,
        out_shape=out_shape,
        in_specs=specs,
        out_specs=VMEM if single else [VMEM] * len(out_shape),
        scratch_shapes=list(scratch),
        compiler_params=pltpu.CompilerParams(vmem_limit_bytes=limit * 1024 * 1024),
        cost_estimate=pl.CostEstimate(flops=flops, bytes_accessed=4 * 1024 * 1024, transcendentals=0),
    )(*operands)


def shape(*dims, dtype=BF):
    return jax.ShapeDtypeStruct(dims, dtype)


def start(place, keys, values, docs, weight_t, hidden_t):
    def block(*dims):
        return pl.BlockSpec(dims, lambda i, place: (0,) * len(dims))

    picked = pl.BlockSpec((128, 128), lambda i, place: (place[0], place[1]))
    return pl.pallas_call(
        start_kernel,
        grid_spec=pltpu.PrefetchScalarGridSpec(
            num_scalar_prefetch=1,
            grid=(1,),
            in_specs=[picked, picked, block(4, 128), ANY, ANY],
            out_specs=[block(4, 272, 128), block(16, 128), ANY],
            scratch_shapes=[pltpu.VMEM((192, 2560), BF), pltpu.SemaphoreType.DMA((3,))],
        ),
        out_shape=[shape(4, 272, 128), shape(16, 128), shape(192, 2560)],
    )(place, keys, values, docs, weight_t, hidden_t)


def on_device(queries, keys, values, doc_ids, hidden, out_weight, projector, teacher):
    zl, yl, xl, c = lax.axis_index("zl"), lax.axis_index("yl"), lax.axis_index("xl"), lax.axis_index("c")
    j = xl * 2 + c
    z = lax.axis_index("zh") * 4 + zl
    g = lax.axis_index("yh") * 2 + lax.axis_index("xh")
    swap = [(0, 1), (1, 0)]
    place = jnp.stack([j, g, c, xl, yl, z, zl]).astype(jnp.int32)

    def from_z(x, shift):
        return lax.ppermute(x, ("zh", "zl"), [((i + shift) % 16, i) for i in range(16)])

    docs = doc_ids.reshape(4, 128)
    packed, doc_rows, both = start(place, keys, values, docs, out_weight.T, hidden.T)
    kv_own = lax.all_to_all(packed, "zh", 0, 0)
    kv_below, kv_above = from_z(kv_own, -1), from_z(kv_own, 1)
    kv_low, kv_high = from_z(kv_own[0:2], -2), from_z(kv_own[2:4], 2)

    q_own = jnp.concatenate([lax.all_gather(queries, GROUP, axis=0, tiled=True), doc_rows], axis=0)
    q_other = lax.ppermute(q_own, "yl", swap)
    gathered = lax.all_gather(both, GROUP, axis=0, tiled=True)

    partial = call(
        attend_kernel,
        shape(8, 528, 128),
        [SMEM] + [ANY] * 7,
        (place, kv_own, kv_below, kv_above, kv_low, kv_high, q_own, q_other),
        40,
        2 * 10 ** 10,
        scratch=[
            pltpu.VMEM((4, 4, 272, 128), BF),
            pltpu.VMEM((2, 2064, 128), BF),
            pltpu.VMEM((128, 2048), BF),
            pltpu.VMEM((512, 128), BF),
            pltpu.VMEM((512, 128), BF),
            pltpu.VMEM((4, 512, 512), F32),
            pltpu.VMEM((4, 512, 512), F32),
            pltpu.VMEM((1, 512), F32),
            pltpu.VMEM((1, 512), F32),
            pltpu.VMEM((128, 512), F32),
            pltpu.VMEM((1, 512), F32),
            pltpu.VMEM((24, 128), jnp.int32),
            pltpu.SMEM((24, 128), jnp.int32),
            pltpu.SemaphoreType.DMA((8,)),
        ],
    )
    att_rows, att_copies = call(
        combine_kernel, [shape(512, 128), shape(4, 512, 128)], [VMEM], (lax.all_to_all(partial, OCTET, 0, 0),), 16
    )

    att_head = lax.all_to_all(att_rows.reshape(4, 128, 128), GROUP, 0, 0)
    attended = jnp.transpose(att_head, (0, 2, 1)).reshape(512, 128)

    att_all = lax.all_to_all(att_copies, HEADSETS, 0, 0)
    student = call(
        student_kernel,
        shape(8, 896, 128),
        [SMEM, HBM, VMEM, VMEM],
        (place, gathered, att_all, teacher),
        24,
        scratch=[pltpu.VMEM((768, 2048), BF), pltpu.VMEM((768, 128), BF), pltpu.SemaphoreType.DMA((5,))],
    )
    own = lax.all_to_all(student, CHIPS, 0, 0)
    other = lax.ppermute(own, "c", swap)

    projector_t, own_projected = call(
        own_projected_kernel, [shape(256, 3072), shape(256, 256, dtype=F32)], [VMEM] * 2, (own, projector), 24, 4 * 10 ** 8
    )
    mismatch, up, down = call(
        second_kernel,
        [shape(512, 256), shape(4, 96, 256), shape(4, 96, 256)],
        [SMEM] + [VMEM] * 4,
        (place, own, other, projector_t, own_projected),
        32,
        8 * 10 ** 8,
    )
    far_below, far_above = from_z(up, -2), from_z(down, 2)
    up, down = call(
        first_kernel, [shape(8, 96, 256), shape(8, 96, 256)], [SMEM] + [VMEM] * 3, (place, own, other, mismatch), 32, 4 * 10 ** 8
    )
    below, above = from_z(up, -1), from_z(down, 1)
    kept = call(kept_kernel, shape(8, 96, 256, dtype=F32), [SMEM] + [VMEM] * 3, (place, own, other, mismatch), 32, 2 * 10 ** 8)
    near = call(add_kernel, shape(8, 96, 256), [VMEM] * 5, (kept, below, above, far_below, far_above), 16)
    grad = call(final_kernel, shape(96, 256, dtype=F32), [VMEM], (lax.all_to_all(near, ("zh", "yl"), 0, 0),), 8)
    return grad, attended


def solution(mesh):
    fine = Mesh(mesh.devices.reshape(4, 4, 2, 2, 2, 2, 2), ("zh", "zl", "yl", "yh", "xh", "xl", "c"))
    return jax.shard_map(
        on_device,
        mesh=fine,
        in_specs=(
            P(CTX, HID),
            P(CTX, None),
            P(CTX, None),
            P(CTX),
            P(CTX, HID),
            P(None, HID),
            P(None, HID),
            P(CTX + HID, None),
        ),
        out_specs=(P(CTX, HID), P(CTX, HID)),
        check_vma=False,
    )
```

```python
import functools

import jax
import jax.numpy as jnp
from jax import lax
from jax.experimental import pallas as pl
from jax.experimental.pallas import tpu as pltpu
from jax.sharding import Mesh
from jax.sharding import PartitionSpec as P

HEAD = 128
SCALE2 = HEAD ** -0.5 * 1.4426950408889634
EMPTY = -1e30
MASKED = -2e30
BF = jnp.bfloat16
F32 = jnp.float32
CTX = ("zh", "zl", "yl")
HID = ("yh", "xh", "xl", "c")
GROUP = ("xl", "c")
OCTET = ("yl", "xl", "c")
HEADSETS = ("yh", "xh")
CHIPS = ("xl", "yh", "xh")
BLOCKS = 4


def start_kernel(keys, values, docs, weight_t, hidden_t, packed, doc_rows, both, block, joined, sem):
    j = lax.axis_index("xl") * 2 + lax.axis_index("c")
    g = lax.axis_index("yh") * 2 + lax.axis_index("xh")
    rows, columns = pl.ds(pl.multiple_of(j * 128, 128), 128), pl.ds(pl.multiple_of(g * 128, 128), 128)
    taken = [
        pltpu.make_async_copy(keys.at[rows, columns], block.at[pl.ds(0, 128)], sem.at[0]),
        pltpu.make_async_copy(values.at[rows, columns], block.at[pl.ds(128, 128)], sem.at[1]),
        pltpu.make_async_copy(weight_t, joined.at[:, pl.ds(0, 2048)], sem.at[2]),
        pltpu.make_async_copy(hidden_t, joined.at[:, pl.ds(2048, 512)], sem.at[3]),
    ]
    for copy in taken:
        copy.start()
    row_docs = jnp.concatenate([docs[...].astype(F32), jnp.zeros((12, 128), F32)], axis=0).astype(BF)
    block[256:272, :] = row_docs
    doc_rows[...] = row_docs
    given = [pltpu.make_async_copy(block, packed.at[i], sem.at[4 + i]) for i in range(4)]
    given.append(pltpu.make_async_copy(joined, both, sem.at[8]))
    taken[0].wait()
    taken[1].wait()
    for copy in given[:4]:
        copy.start()
    taken[2].wait()
    taken[3].wait()
    given[4].start()
    for copy in given:
        copy.wait()


def attend_kernel(place, kv0, kv1, kv2, kv3_low, kv3_high, q_own, q_other, out, kv, q_all, v_turned, q_even, q_odd, s_even, s_odd, max_even, max_odd, acc, total, info_v, info, sem):
    j, yl, z = place[0], place[4], place[5]
    copies = [
        pltpu.make_async_copy(src, dst, sem.at[i])
        for i, (src, dst) in enumerate((
            (kv0, kv.at[0]), (kv1, kv.at[1]), (kv2, kv.at[2]), (kv3_low, kv.at[3, pl.ds(0, 2)]), (kv3_high, kv.at[3, pl.ds(2, 2)]),
            (q_own, q_all.at[0]), (q_other, q_all.at[1]),
        ))
    ]
    for copy in copies:
        copy.start()
    for copy in copies[:5]:
        copy.wait()
    block_docs = []
    for ch in range(4):
        for i in range(BLOCKS):
            rows = kv[i, ch, 256:272, :].astype(F32)
            block_docs.append(jnp.concatenate([rows[r:r + 1] for r in range(4)], axis=1))
    block_docs = jnp.concatenate(block_docs, axis=0)
    lane = lax.broadcasted_iota(jnp.int32, (16, 128), 1)
    counts = jnp.zeros((16, 128), F32)
    for d in range(8):
        below = jnp.sum((block_docs < d).astype(F32), axis=1, keepdims=True)
        counts = jnp.where(lane == d, below, counts)
    info_v[0:16, :] = counts.astype(jnp.int32)
    for copy in copies[5:]:
        copy.wait()
    for side in range(2):
        info_v[16 + 4 * side:20 + 4 * side, :] = q_all[side, 2048:2064, :].astype(F32)[0:4].astype(jnp.int32)
    to_scalars = pltpu.make_async_copy(info_v, info, sem.at[7])
    to_scalars.start()
    for ch in range(4):
        for i in range(BLOCKS):
            v_turned[:, (ch * BLOCKS + i) * 128:(ch * BLOCKS + i + 1) * 128] = kv[i, ch, 128:256, :].T
    to_scalars.wait()
    where = [(z + shift) % 4 for shift in (0, 3, 1, 2)]
    key_iota = lax.broadcasted_iota(jnp.int32, (128, 512), 0)
    row_iota = lax.broadcasted_iota(jnp.int32, (1, 512), 1) % 128

    first_doc = jnp.minimum(info[16, 0], info[20, 0])
    begin = jnp.int32(0)
    for ch in range(4):
        fewest = functools.reduce(jnp.minimum, [info[ch * BLOCKS + i, first_doc] for i in range(BLOCKS)])
        begin = begin + (fewest >= (j + 1) * 128).astype(jnp.int32)
    end = z // BLOCKS + 1

    def begin_scores(tile, q_ref, max_ref):
        side, row0 = tile // 4, pl.multiple_of(tile % 4 * 128, 128)
        for h in range(4):
            q_ref[h * 128:(h + 1) * 128, :] = q_all[side, pl.ds(h * 512 + row0, 128), :]
        max_ref[...] = jnp.full((1, 512), EMPTY, F32)

    def is_full(tile, ch):
        yl_q = jnp.where(tile // 4 == 0, yl, 1 - yl)
        q_min = (2 * z + yl_q) * 512 + tile % 4 * 128
        last = info[16 + tile, 127]
        most = functools.reduce(jnp.maximum, [info[ch * BLOCKS + i, last] for i in range(BLOCKS)])
        k_max = (2 * (ch * BLOCKS + BLOCKS - 1) + yl) * 512 + j * 128 + 127
        return (k_max <= q_min) & (most <= j * 128)

    def put_scores(tile, ch, masked, q_ref, s_ref, max_ref):
        keys = jnp.concatenate([kv[i, ch, 0:128, :] for i in range(BLOCKS)], axis=0)
        s = lax.dot_general(keys, q_ref[...], (((1,), (1,)), ((), ())), preferred_element_type=F32) * SCALE2
        if masked:
            yl_q = jnp.where(tile // 4 == 0, yl, 1 - yl)
            q_pos = (2 * z + yl_q) * 512 + tile % 4 * 128 + row_iota
            row_docs = jnp.concatenate([info_v[pl.ds(16 + tile, 1), :]] * 4, axis=1)
            parts = []
            for i in range(BLOCKS):
                low = jnp.zeros((1, 512), jnp.int32)
                for d in range(8):
                    low = jnp.where(row_docs == d, info[ch * BLOCKS + i, d], low)
                low = low - j * 128
                high = q_pos - ((2 * (ch * 4 + where[i]) + yl) * 512 + j * 128)
                ok = (key_iota >= low) & (key_iota <= high)
                parts.append(jnp.where(ok, s[i * 128:(i + 1) * 128], MASKED))
            s = jnp.concatenate(parts, axis=0)
        s_ref[ch] = s
        max_ref[...] = jnp.maximum(max_ref[...], jnp.max(s, axis=0, keepdims=True))

    def add_up(ch, s_ref, max_ref):
        w = jnp.exp2(s_ref[ch] - max_ref[...])
        cols = pl.ds(pl.multiple_of(ch * (BLOCKS * 128), BLOCKS * 128), BLOCKS * 128)
        acc[...] += jnp.dot(v_turned[:, cols], w.astype(BF), preferred_element_type=F32)
        total[...] += jnp.sum(w, axis=0, keepdims=True)

    def finish(tile, max_ref):
        run_sum, run_max = total[...], max_ref[...]
        seen = run_sum > 0
        o = (acc[...] * (1.0 / jnp.where(seen, run_sum, 1.0))).astype(BF)
        lse = jnp.where(seen, run_max + jnp.log2(jnp.where(seen, run_sum, 1.0)), EMPTY)
        hi = lse.astype(BF).astype(F32)
        mid = (lse - hi).astype(BF).astype(F32)
        lo = lse - hi - mid
        dest = jnp.where(tile // 4 == 0, yl, 1 - yl) * 4 + tile % 4
        rows = [part[:, h * 128:(h + 1) * 128] for part in (hi, mid, lo) for h in range(4)]
        rows.append(jnp.zeros((4, 128), F32))
        for h in range(4):
            out[dest, h * 128:(h + 1) * 128, :] = o[:, h * 128:(h + 1) * 128]
        out[dest, 512:528, :] = jnp.concatenate(rows, axis=0).astype(BF)
        acc[...] = jnp.zeros((128, 512), F32)
        total[...] = jnp.zeros((1, 512), F32)

    def sweep(tile, put, use):
        if put is not None:
            begin_scores(tile, put[0], put[2])

        def one(ch, carry):
            def work(masked):
                if put is not None:
                    put_scores(tile, ch, masked, *put)
                if use is not None:
                    add_up(ch, use[1], use[2])

            if put is None:
                work(False)
            else:
                full = is_full(tile, ch)
                pl.when(full)(lambda: work(False))
                pl.when(jnp.logical_not(full))(lambda: work(True))
            return carry

        lax.fori_loop(begin, end, one, 0)
        if use is not None:
            finish(tile - 1, use[2])

    even, odd = (q_even, s_even, max_even), (q_odd, s_odd, max_odd)
    acc[...] = jnp.zeros((128, 512), F32)
    total[...] = jnp.zeros((1, 512), F32)
    sweep(0, even, None)

    def two_tiles(pair, carry):
        sweep(2 * pair + 1, odd, even)
        sweep(2 * pair + 2, even, odd)
        return carry

    lax.fori_loop(0, 3, two_tiles, 0)
    sweep(7, odd, even)
    sweep(8, None, odd)


def combine_kernel(parts, out, copies):
    count = parts.shape[0]
    tails = [parts[s, 512:528, :].astype(F32) for s in range(count)]
    for h in range(4):
        lses = [t[h:h + 1] + t[4 + h:5 + h] + t[8 + h:9 + h] for t in tails]
        top = functools.reduce(jnp.maximum, lses)
        weights = [jnp.exp2(v - top) for v in lses]
        inverse = 1.0 / sum(weights)
        rows = slice(h * 128, (h + 1) * 128)
        total = sum(w * inverse * parts[s, rows, :].astype(F32) for s, w in enumerate(weights)).astype(BF)
        out[rows, :] = total
        for copy in range(copies.shape[0]):
            copies[copy, rows, :] = total


def student_kernel(place, gathered, att, teacher, out, weights, hidden, sem):
    copies = []
    own_rows = pl.ds(pl.multiple_of(2048 + place[0] * 128, 128), 128)
    hidden_copy = pltpu.make_async_copy(gathered.at[:, own_rows], hidden, sem.at[4])
    for part in range(4):
        rows = pl.ds(part * 192, 192)
        copies.append(pltpu.make_async_copy(gathered.at[rows, pl.ds(0, 2048)], weights.at[rows], sem.at[part]))
    copies[0].start()
    hidden_copy.start()
    for copy in copies[1:]:
        copy.start()
    for chip in range(8):
        first = (chip % 4 * 4 + chip // 4 * 2) * 256
        for i in range(4):
            out[chip, 768 + i * 32:800 + i * 32, :] = teacher[:, first + i * 128:first + (i + 1) * 128]
    att_all = att[...].reshape(2048, 128)
    hidden_copy.wait()
    for part in range(4):
        copies[part].wait()
        rows = slice(part * 192, (part + 1) * 192)
        mixed = jnp.dot(weights[rows, :], att_all, preferred_element_type=F32)
        student = (hidden[rows, :].astype(F32) + mixed).astype(BF)
        for copy in range(8):
            out[copy, rows, :] = student


def projected(student, projector_t):
    total = 0.0
    for g in range(4):
        both = jnp.concatenate([student[g, 0:768, :], student[4 + g, 0:768, :]], axis=1)
        total = total + jnp.dot(projector_t[:, g * 768:(g + 1) * 768], both, preferred_element_type=F32)
    return total


def teacher_rows(own, other, core, chunk_core):
    pieces = []
    for xl in range(2):
        for t in range(4):
            source = t // 2 * 4 + xl * 2 + chunk_core
            halves = []
            for i in range(2):
                rows = pl.ds(pl.multiple_of(768 + core * 64 + i * 32, 32), 32)
                halves.append(jnp.where(core == t % 2, own[source, rows, :].astype(F32), other[source, rows, :].astype(F32)))
            pieces.append(jnp.concatenate(halves, axis=1))
    return jnp.concatenate(pieces, axis=0)


def gradient_rows(own, other, mismatch, near):
    rows = []
    for zh in range(4):
        cut = pl.ds(pl.multiple_of(near * 192, 64), 192)
        rows.append(jnp.concatenate([ref[xl * 4 + zh, cut, :] for ref in (own, other) for xl in range(2)], axis=1))
    return jnp.dot(jnp.concatenate(rows, axis=0), mismatch[...], preferred_element_type=F32).reshape(8, 96, 256)


def own_projected_kernel(own, projector, projector_t, out):
    for g in range(4):
        projector_t[:, g * 768:(g + 1) * 768] = projector[g * 768:(g + 1) * 768, :].T
    out[...] = projected(own, projector_t).T


def sent_kernel(place, own, other, projector_t, own_projected, mismatch, far_up, far_down, up, down):
    core, near = place[2], place[6]
    mismatch[0:256, :] = (own_projected[...] - teacher_rows(own, other, core, core)).astype(BF)
    mismatch[256:512, :] = (projected(other, projector_t).T - teacher_rows(own, other, core, 1 - core)).astype(BF)
    up[...] = gradient_rows(own, other, mismatch, (near + 1) % 4).astype(BF)
    down[...] = gradient_rows(own, other, mismatch, (near + 3) % 4).astype(BF)
    far = gradient_rows(own, other, mismatch, (near + 2) % 4).astype(BF)
    far_up[...] = far[0:4]
    far_down[...] = far[4:8]


def kept_kernel(place, own, other, mismatch, out):
    out[...] = gradient_rows(own, other, mismatch, place[6])


def add_kernel(kept, below, above, far_below, far_above, out):
    near = kept[...] + below[...].astype(F32) + above[...].astype(F32)
    out[0:4] = (near[0:4] + far_below[...].astype(F32)).astype(BF)
    out[4:8] = (near[4:8] + far_above[...].astype(F32)).astype(BF)


def final_kernel(terms, out):
    out[...] = sum(terms[i].astype(F32) for i in range(terms.shape[0])) * (16384 ** -0.5)


VMEM = pl.BlockSpec(memory_space=pltpu.VMEM)
SMEM = pl.BlockSpec(memory_space=pltpu.SMEM)
ANY = pl.BlockSpec(memory_space=pl.ANY)
HBM = pl.BlockSpec(memory_space=pltpu.HBM)


def call(kernel, out_shape, specs, operands, limit, flops=0, scratch=()):
    single = not isinstance(out_shape, list)
    return pl.pallas_call(
        kernel,
        out_shape=out_shape,
        in_specs=specs,
        out_specs=VMEM if single else [VMEM] * len(out_shape),
        scratch_shapes=list(scratch),
        compiler_params=pltpu.CompilerParams(vmem_limit_bytes=limit * 1024 * 1024),
        cost_estimate=pl.CostEstimate(flops=flops, bytes_accessed=4 * 1024 * 1024, transcendentals=0),
    )(*operands)


def shape(*dims, dtype=BF):
    return jax.ShapeDtypeStruct(dims, dtype)


def start(keys, values, docs, weight_t, hidden_t):
    return pl.pallas_call(
        start_kernel,
        in_specs=[ANY, ANY, VMEM, ANY, ANY],
        out_specs=[ANY, VMEM, ANY],
        scratch_shapes=[pltpu.VMEM((272, 128), BF), pltpu.VMEM((192, 2560), BF), pltpu.SemaphoreType.DMA((9,))],
        out_shape=[shape(4, 272, 128), shape(16, 128), shape(192, 2560)],
    )(keys, values, docs, weight_t, hidden_t)


def on_device(queries, keys, values, doc_ids, hidden, out_weight, projector, teacher):
    zl, yl, xl, c = lax.axis_index("zl"), lax.axis_index("yl"), lax.axis_index("xl"), lax.axis_index("c")
    j = xl * 2 + c
    z = lax.axis_index("zh") * 4 + zl
    g = lax.axis_index("yh") * 2 + lax.axis_index("xh")
    swap = [(0, 1), (1, 0)]
    place = jnp.stack([j, g, c, xl, yl, z, zl]).astype(jnp.int32)

    def from_z(x, shift):
        return lax.ppermute(x, ("zh", "zl"), [((i + shift) % 16, i) for i in range(16)])

    docs = doc_ids.reshape(4, 128)
    packed, doc_rows, both = start(keys, values, docs, out_weight.T, hidden.T)
    kv_own = lax.all_to_all(packed, "zh", 0, 0)
    kv_below, kv_above = from_z(kv_own, -1), from_z(kv_own, 1)
    kv_low, kv_high = from_z(kv_own[0:2], -2), from_z(kv_own[2:4], 2)

    q_own = jnp.concatenate([lax.all_gather(queries, GROUP, axis=0, tiled=True), doc_rows], axis=0)
    q_other = lax.ppermute(q_own, "yl", swap)
    gathered = lax.all_gather(both, GROUP, axis=0, tiled=True)

    partial = call(
        attend_kernel,
        shape(8, 528, 128),
        [SMEM] + [ANY] * 7,
        (place, kv_own, kv_below, kv_above, kv_low, kv_high, q_own, q_other),
        40,
        2 * 10 ** 10,
        scratch=[
            pltpu.VMEM((4, 4, 272, 128), BF),
            pltpu.VMEM((2, 2064, 128), BF),
            pltpu.VMEM((128, 2048), BF),
            pltpu.VMEM((512, 128), BF),
            pltpu.VMEM((512, 128), BF),
            pltpu.VMEM((4, 512, 512), F32),
            pltpu.VMEM((4, 512, 512), F32),
            pltpu.VMEM((1, 512), F32),
            pltpu.VMEM((1, 512), F32),
            pltpu.VMEM((128, 512), F32),
            pltpu.VMEM((1, 512), F32),
            pltpu.VMEM((24, 128), jnp.int32),
            pltpu.SMEM((24, 128), jnp.int32),
            pltpu.SemaphoreType.DMA((8,)),
        ],
    )
    att_rows, att_copies = call(
        combine_kernel, [shape(512, 128), shape(4, 512, 128)], [VMEM], (lax.all_to_all(partial, OCTET, 0, 0),), 16
    )

    att_head = lax.all_to_all(att_rows.reshape(4, 128, 128), GROUP, 0, 0)
    attended = jnp.transpose(att_head, (0, 2, 1)).reshape(512, 128)

    att_all = lax.all_to_all(att_copies, HEADSETS, 0, 0)
    student = call(
        student_kernel,
        shape(8, 896, 128),
        [SMEM, HBM, VMEM, VMEM],
        (place, gathered, att_all, teacher),
        24,
        scratch=[pltpu.VMEM((768, 2048), BF), pltpu.VMEM((768, 128), BF), pltpu.SemaphoreType.DMA((5,))],
    )
    own = lax.all_to_all(student, CHIPS, 0, 0)
    other = lax.ppermute(own, "c", swap)

    projector_t, own_projected = call(
        own_projected_kernel, [shape(256, 3072), shape(256, 256, dtype=F32)], [VMEM] * 2, (own, projector), 24, 4 * 10 ** 8
    )
    eight = shape(8, 96, 256)
    mismatch, far_up, far_down, up, down = call(
        sent_kernel,
        [shape(512, 256), shape(4, 96, 256), shape(4, 96, 256), eight, eight],
        [SMEM] + [VMEM] * 4,
        (place, own, other, projector_t, own_projected),
        32,
        8 * 10 ** 8,
    )
    below, above = from_z(up, -1), from_z(down, 1)
    far_below, far_above = from_z(far_up, -2), from_z(far_down, 2)
    kept = call(kept_kernel, shape(8, 96, 256, dtype=F32), [SMEM] + [VMEM] * 3, (place, own, other, mismatch), 32, 2 * 10 ** 8)
    near = call(add_kernel, shape(8, 96, 256), [VMEM] * 5, (kept, below, above, far_below, far_above), 16)
    grad = call(final_kernel, shape(96, 256, dtype=F32), [VMEM], (lax.all_to_all(near, ("zh", "yl"), 0, 0),), 8)
    return grad, attended


def solution(mesh):
    fine = Mesh(mesh.devices.reshape(4, 4, 2, 2, 2, 2, 2), ("zh", "zl", "yl", "yh", "xh", "xl", "c"))
    return jax.shard_map(
        on_device,
        mesh=fine,
        in_specs=(
            P(CTX, HID),
            P(CTX, None),
            P(CTX, None),
            P(CTX),
            P(CTX, HID),
            P(None, HID),
            P(None, HID),
            P(CTX + HID, None),
        ),
        out_specs=(P(CTX, HID), P(CTX, HID)),
        check_vma=False,
    )
```

```python
import functools

import jax
import jax.numpy as jnp
from jax import lax
from jax.experimental import pallas as pl
from jax.experimental.pallas import tpu as pltpu
from jax.sharding import Mesh
from jax.sharding import PartitionSpec as P

HEAD = 128
SCALE2 = HEAD ** -0.5 * 1.4426950408889634
EMPTY = -1e30
MASKED = -2e30
BF = jnp.bfloat16
F32 = jnp.float32
CTX = ("zh", "zl", "yl")
HID = ("yh", "xh", "xl", "c")
GROUP = ("xl", "c")
OCTET = ("yl", "xl", "c")
HEADSETS = ("yh", "xh")
CHIPS = ("xl", "yh", "xh")
BLOCKS = 4


def start_kernel(keys, values, docs, weight_t, hidden_t, packed, doc_rows, both, block, joined, sem):
    j = lax.axis_index("xl") * 2 + lax.axis_index("c")
    g = lax.axis_index("yh") * 2 + lax.axis_index("xh")
    rows, columns = pl.ds(pl.multiple_of(j * 128, 128), 128), pl.ds(pl.multiple_of(g * 128, 128), 128)
    taken = [
        pltpu.make_async_copy(keys.at[rows, columns], block.at[pl.ds(0, 128)], sem.at[0]),
        pltpu.make_async_copy(values.at[rows, columns], block.at[pl.ds(128, 128)], sem.at[1]),
        pltpu.make_async_copy(weight_t, joined.at[:, pl.ds(0, 2048)], sem.at[2]),
        pltpu.make_async_copy(hidden_t, joined.at[:, pl.ds(2048, 512)], sem.at[3]),
    ]
    for copy in taken:
        copy.start()
    row_docs = jnp.concatenate([docs[...].astype(F32), jnp.zeros((12, 128), F32)], axis=0).astype(BF)
    block[256:272, :] = row_docs
    doc_rows[...] = row_docs
    given = [pltpu.make_async_copy(block, packed.at[i], sem.at[4 + i]) for i in range(4)]
    given.append(pltpu.make_async_copy(joined, both, sem.at[8]))
    taken[0].wait()
    taken[1].wait()
    for copy in given[:4]:
        copy.start()
    taken[2].wait()
    taken[3].wait()
    given[4].start()
    for copy in given:
        copy.wait()


def attend_kernel(place, kv0, kv1, kv2, kv3_low, kv3_high, q_own, q_other, out, kv, q_all, v_turned, q_even, q_odd, s_even, s_odd, max_even, max_odd, acc, total, info_v, info, sem):
    j, yl, z = place[0], place[4], place[5]
    copies = [
        pltpu.make_async_copy(src, dst, sem.at[i])
        for i, (src, dst) in enumerate((
            (kv0, kv.at[0]), (kv1, kv.at[1]), (kv2, kv.at[2]), (kv3_low, kv.at[3, pl.ds(0, 2)]), (kv3_high, kv.at[3, pl.ds(2, 2)]),
            (q_own, q_all.at[0]), (q_other, q_all.at[1]),
        ))
    ]
    for copy in copies:
        copy.start()
    for copy in copies[:5]:
        copy.wait()
    block_docs = []
    for ch in range(4):
        for i in range(BLOCKS):
            rows = kv[i, ch, 256:272, :].astype(F32)
            block_docs.append(jnp.concatenate([rows[r:r + 1] for r in range(4)], axis=1))
    block_docs = jnp.concatenate(block_docs, axis=0)
    lane = lax.broadcasted_iota(jnp.int32, (16, 128), 1)
    counts = jnp.zeros((16, 128), F32)
    for d in range(8):
        below = jnp.sum((block_docs < d).astype(F32), axis=1, keepdims=True)
        counts = jnp.where(lane == d, below, counts)
    info_v[0:16, :] = counts.astype(jnp.int32)
    for copy in copies[5:]:
        copy.wait()
    for side in range(2):
        info_v[16 + 4 * side:20 + 4 * side, :] = q_all[side, 2048:2064, :].astype(F32)[0:4].astype(jnp.int32)
    to_scalars = pltpu.make_async_copy(info_v, info, sem.at[7])
    to_scalars.start()
    for ch in range(4):
        for i in range(BLOCKS):
            v_turned[:, (ch * BLOCKS + i) * 128:(ch * BLOCKS + i + 1) * 128] = kv[i, ch, 128:256, :].T
    to_scalars.wait()
    where = [(z + shift) % 4 for shift in (0, 3, 1, 2)]
    key_iota = lax.broadcasted_iota(jnp.int32, (128, 512), 0)
    row_iota = lax.broadcasted_iota(jnp.int32, (1, 512), 1) % 128

    first_doc = jnp.minimum(info[16, 0], info[20, 0])
    begin = jnp.int32(0)
    for ch in range(4):
        fewest = functools.reduce(jnp.minimum, [info[ch * BLOCKS + i, first_doc] for i in range(BLOCKS)])
        begin = begin + (fewest >= (j + 1) * 128).astype(jnp.int32)
    end = z // BLOCKS + 1

    def begin_scores(tile, q_ref, max_ref):
        side, row0 = tile // 4, pl.multiple_of(tile % 4 * 128, 128)
        for h in range(4):
            q_ref[h * 128:(h + 1) * 128, :] = q_all[side, pl.ds(h * 512 + row0, 128), :]
        max_ref[...] = jnp.full((1, 512), EMPTY, F32)

    def is_full(tile, ch):
        yl_q = jnp.where(tile // 4 == 0, yl, 1 - yl)
        q_min = (2 * z + yl_q) * 512 + tile % 4 * 128
        last = info[16 + tile, 127]
        most = functools.reduce(jnp.maximum, [info[ch * BLOCKS + i, last] for i in range(BLOCKS)])
        k_max = (2 * (ch * BLOCKS + BLOCKS - 1) + yl) * 512 + j * 128 + 127
        return (k_max <= q_min) & (most <= j * 128)

    def put_scores(tile, ch, masked, q_ref, s_ref, max_ref):
        keys = jnp.concatenate([kv[i, ch, 0:128, :] for i in range(BLOCKS)], axis=0)
        s = lax.dot_general(keys, q_ref[...], (((1,), (1,)), ((), ())), preferred_element_type=F32) * SCALE2
        if masked:
            yl_q = jnp.where(tile // 4 == 0, yl, 1 - yl)
            q_pos = (2 * z + yl_q) * 512 + tile % 4 * 128 + row_iota
            row_docs = jnp.concatenate([info_v[pl.ds(16 + tile, 1), :]] * 4, axis=1)
            parts = []
            for i in range(BLOCKS):
                low = jnp.zeros((1, 512), jnp.int32)
                for d in range(8):
                    low = jnp.where(row_docs == d, info[ch * BLOCKS + i, d], low)
                low = low - j * 128
                high = q_pos - ((2 * (ch * 4 + where[i]) + yl) * 512 + j * 128)
                ok = (key_iota >= low) & (key_iota <= high)
                parts.append(jnp.where(ok, s[i * 128:(i + 1) * 128], MASKED))
            s = jnp.concatenate(parts, axis=0)
        s_ref[ch] = s
        max_ref[...] = jnp.maximum(max_ref[...], jnp.max(s, axis=0, keepdims=True))

    def add_up(ch, s_ref, max_ref):
        w = jnp.exp2(s_ref[ch] - max_ref[...])
        cols = pl.ds(pl.multiple_of(ch * (BLOCKS * 128), BLOCKS * 128), BLOCKS * 128)
        acc[...] += jnp.dot(v_turned[:, cols], w.astype(BF), preferred_element_type=F32)
        total[...] += jnp.sum(w, axis=0, keepdims=True)

    def finish(tile, max_ref):
        run_sum, run_max = total[...], max_ref[...]
        seen = run_sum > 0
        o = (acc[...] * (1.0 / jnp.where(seen, run_sum, 1.0))).astype(BF)
        lse = jnp.where(seen, run_max + jnp.log2(jnp.where(seen, run_sum, 1.0)), EMPTY)
        hi = lse.astype(BF).astype(F32)
        mid = (lse - hi).astype(BF).astype(F32)
        lo = lse - hi - mid
        dest = jnp.where(tile // 4 == 0, yl, 1 - yl) * 4 + tile % 4
        rows = [part[:, h * 128:(h + 1) * 128] for part in (hi, mid, lo) for h in range(4)]
        rows.append(jnp.zeros((4, 128), F32))
        for h in range(4):
            out[dest, h * 128:(h + 1) * 128, :] = o[:, h * 128:(h + 1) * 128]
        out[dest, 512:528, :] = jnp.concatenate(rows, axis=0).astype(BF)
        acc[...] = jnp.zeros((128, 512), F32)
        total[...] = jnp.zeros((1, 512), F32)

    def sweep(tile, put, use):
        if put is not None:
            begin_scores(tile, put[0], put[2])

        def one(ch, carry):
            def work(masked):
                if put is not None:
                    put_scores(tile, ch, masked, *put)
                if use is not None:
                    add_up(ch, use[1], use[2])

            if put is None:
                work(False)
            else:
                full = is_full(tile, ch)
                pl.when(full)(lambda: work(False))
                pl.when(jnp.logical_not(full))(lambda: work(True))
            return carry

        lax.fori_loop(begin, end, one, 0)
        if use is not None:
            finish(tile - 1, use[2])

    even, odd = (q_even, s_even, max_even), (q_odd, s_odd, max_odd)
    acc[...] = jnp.zeros((128, 512), F32)
    total[...] = jnp.zeros((1, 512), F32)
    sweep(0, even, None)

    def two_tiles(pair, carry):
        sweep(2 * pair + 1, odd, even)
        sweep(2 * pair + 2, even, odd)
        return carry

    lax.fori_loop(0, 3, two_tiles, 0)
    sweep(7, odd, even)
    sweep(8, None, odd)


def combine_kernel(parts, out, copies):
    count = parts.shape[0]
    tails = [parts[s, 512:528, :].astype(F32) for s in range(count)]
    for h in range(4):
        lses = [t[h:h + 1] + t[4 + h:5 + h] + t[8 + h:9 + h] for t in tails]
        top = functools.reduce(jnp.maximum, lses)
        weights = [jnp.exp2(v - top) for v in lses]
        inverse = 1.0 / sum(weights)
        rows = slice(h * 128, (h + 1) * 128)
        total = sum(w * inverse * parts[s, rows, :].astype(F32) for s, w in enumerate(weights)).astype(BF)
        out[rows, :] = total
        for copy in range(copies.shape[0]):
            copies[copy, rows, :] = total


def student_kernel(place, gathered, att, teacher, out, weights, hidden, taught, student, sem):
    own_rows = pl.ds(pl.multiple_of(2048 + place[0] * 128, 128), 128)
    hidden_copy = pltpu.make_async_copy(gathered.at[:, own_rows], hidden, sem.at[4])
    copies = []
    for part in range(4):
        rows = pl.ds(part * 192, 192)
        copies.append(pltpu.make_async_copy(gathered.at[rows, pl.ds(0, 2048)], weights.at[rows], sem.at[part]))
    copies[0].start()
    hidden_copy.start()
    for copy in copies[1:]:
        copy.start()
    given = []
    for chip in range(8):
        first = (chip % 4 * 4 + chip // 4 * 2) * 256
        for i in range(4):
            taught[chip, i * 32:(i + 1) * 32, :] = teacher[:, first + i * 128:first + (i + 1) * 128]
        given.append(pltpu.make_async_copy(taught.at[chip], out.at[chip, pl.ds(768, 128)], sem.at[5 + chip]))
        given[-1].start()
    att_all = att[...].reshape(2048, 128)
    hidden_copy.wait()
    for part in range(4):
        copies[part].wait()
        rows = slice(part * 192, (part + 1) * 192)
        mixed = jnp.dot(weights[rows, :], att_all, preferred_element_type=F32)
        student[rows, :] = (hidden[rows, :].astype(F32) + mixed).astype(BF)
        for chip in range(8):
            cut = pl.ds(part * 192, 192)
            given.append(pltpu.make_async_copy(student.at[cut], out.at[chip, cut], sem.at[13 + part * 8 + chip]))
            given[-1].start()
    for copy in given:
        copy.wait()


def projected(student, projector_t):
    total = 0.0
    for g in range(4):
        both = jnp.concatenate([student[g, 0:768, :], student[4 + g, 0:768, :]], axis=1)
        total = total + jnp.dot(projector_t[:, g * 768:(g + 1) * 768], both, preferred_element_type=F32)
    return total


def teacher_rows(own, other, core, chunk_core):
    pieces = []
    for xl in range(2):
        for t in range(4):
            source = t // 2 * 4 + xl * 2 + chunk_core
            halves = []
            for i in range(2):
                rows = pl.ds(pl.multiple_of(768 + core * 64 + i * 32, 32), 32)
                halves.append(jnp.where(core == t % 2, own[source, rows, :].astype(F32), other[source, rows, :].astype(F32)))
            pieces.append(jnp.concatenate(halves, axis=1))
    return jnp.concatenate(pieces, axis=0)


def gradient_rows(own, other, mismatch, near):
    rows = []
    for zh in range(4):
        cut = pl.ds(pl.multiple_of(near * 192, 64), 192)
        rows.append(jnp.concatenate([ref[xl * 4 + zh, cut, :] for ref in (own, other) for xl in range(2)], axis=1))
    return jnp.dot(jnp.concatenate(rows, axis=0), mismatch[...], preferred_element_type=F32).reshape(8, 96, 256)


def own_projected_kernel(own, projector, projector_t, out):
    for g in range(4):
        projector_t[:, g * 768:(g + 1) * 768] = projector[g * 768:(g + 1) * 768, :].T
    out[...] = projected(own, projector_t).T


def sent_kernel(place, own, other, projector_t, own_projected, mismatch, far_up, far_down, up, down):
    core, near = place[2], place[6]
    mismatch[0:256, :] = (own_projected[...] - teacher_rows(own, other, core, core)).astype(BF)
    mismatch[256:512, :] = (projected(other, projector_t).T - teacher_rows(own, other, core, 1 - core)).astype(BF)
    up[...] = gradient_rows(own, other, mismatch, (near + 1) % 4).astype(BF)
    down[...] = gradient_rows(own, other, mismatch, (near + 3) % 4).astype(BF)
    far = gradient_rows(own, other, mismatch, (near + 2) % 4).astype(BF)
    far_up[...] = far[0:4]
    far_down[...] = far[4:8]


def kept_kernel(place, own, other, mismatch, out):
    out[...] = gradient_rows(own, other, mismatch, place[6])


def add_kernel(kept, below, above, far_below, far_above, out):
    near = kept[...] + below[...].astype(F32) + above[...].astype(F32)
    out[0:4] = (near[0:4] + far_below[...].astype(F32)).astype(BF)
    out[4:8] = (near[4:8] + far_above[...].astype(F32)).astype(BF)


def final_kernel(terms, out):
    out[...] = sum(terms[i].astype(F32) for i in range(terms.shape[0])) * (16384 ** -0.5)


VMEM = pl.BlockSpec(memory_space=pltpu.VMEM)
SMEM = pl.BlockSpec(memory_space=pltpu.SMEM)
ANY = pl.BlockSpec(memory_space=pl.ANY)
HBM = pl.BlockSpec(memory_space=pltpu.HBM)


def call(kernel, out_shape, specs, operands, limit, flops=0, scratch=()):
    single = not isinstance(out_shape, list)
    return pl.pallas_call(
        kernel,
        out_shape=out_shape,
        in_specs=specs,
        out_specs=VMEM if single else [VMEM] * len(out_shape),
        scratch_shapes=list(scratch),
        compiler_params=pltpu.CompilerParams(vmem_limit_bytes=limit * 1024 * 1024),
        cost_estimate=pl.CostEstimate(flops=flops, bytes_accessed=4 * 1024 * 1024, transcendentals=0),
    )(*operands)


def shape(*dims, dtype=BF):
    return jax.ShapeDtypeStruct(dims, dtype)


def start(keys, values, docs, weight_t, hidden_t):
    return pl.pallas_call(
        start_kernel,
        in_specs=[ANY, ANY, VMEM, ANY, ANY],
        out_specs=[ANY, VMEM, ANY],
        scratch_shapes=[pltpu.VMEM((272, 128), BF), pltpu.VMEM((192, 2560), BF), pltpu.SemaphoreType.DMA((9,))],
        out_shape=[shape(4, 272, 128), shape(16, 128), shape(192, 2560)],
    )(keys, values, docs, weight_t, hidden_t)


def on_device(queries, keys, values, doc_ids, hidden, out_weight, projector, teacher):
    zl, yl, xl, c = lax.axis_index("zl"), lax.axis_index("yl"), lax.axis_index("xl"), lax.axis_index("c")
    j = xl * 2 + c
    z = lax.axis_index("zh") * 4 + zl
    g = lax.axis_index("yh") * 2 + lax.axis_index("xh")
    swap = [(0, 1), (1, 0)]
    place = jnp.stack([j, g, c, xl, yl, z, zl]).astype(jnp.int32)

    def from_z(x, shift):
        return lax.ppermute(x, ("zh", "zl"), [((i + shift) % 16, i) for i in range(16)])

    docs = doc_ids.reshape(4, 128)
    packed, doc_rows, both = start(keys, values, docs, out_weight.T, hidden.T)
    kv_own = lax.all_to_all(packed, "zh", 0, 0)
    kv_below, kv_above = from_z(kv_own, -1), from_z(kv_own, 1)
    kv_low, kv_high = from_z(kv_own[0:2], -2), from_z(kv_own[2:4], 2)

    q_own = jnp.concatenate([lax.all_gather(queries, GROUP, axis=0, tiled=True), doc_rows], axis=0)
    q_other = lax.ppermute(q_own, "yl", swap)
    gathered = lax.all_gather(both, GROUP, axis=0, tiled=True)

    partial = call(
        attend_kernel,
        shape(8, 528, 128),
        [SMEM] + [ANY] * 7,
        (place, kv_own, kv_below, kv_above, kv_low, kv_high, q_own, q_other),
        40,
        2 * 10 ** 10,
        scratch=[
            pltpu.VMEM((4, 4, 272, 128), BF),
            pltpu.VMEM((2, 2064, 128), BF),
            pltpu.VMEM((128, 2048), BF),
            pltpu.VMEM((512, 128), BF),
            pltpu.VMEM((512, 128), BF),
            pltpu.VMEM((4, 512, 512), F32),
            pltpu.VMEM((4, 512, 512), F32),
            pltpu.VMEM((1, 512), F32),
            pltpu.VMEM((1, 512), F32),
            pltpu.VMEM((128, 512), F32),
            pltpu.VMEM((1, 512), F32),
            pltpu.VMEM((24, 128), jnp.int32),
            pltpu.SMEM((24, 128), jnp.int32),
            pltpu.SemaphoreType.DMA((8,)),
        ],
    )
    att_rows, att_copies = call(
        combine_kernel, [shape(512, 128), shape(4, 512, 128)], [VMEM], (lax.all_to_all(partial, OCTET, 0, 0),), 16
    )

    att_head = lax.all_to_all(att_rows.reshape(4, 128, 128), GROUP, 0, 0)
    attended = jnp.transpose(att_head, (0, 2, 1)).reshape(512, 128)

    att_all = lax.all_to_all(att_copies, HEADSETS, 0, 0)
    student = pl.pallas_call(
        student_kernel,
        out_shape=shape(8, 896, 128),
        in_specs=[SMEM, HBM, VMEM, VMEM],
        out_specs=ANY,
        scratch_shapes=[
            pltpu.VMEM((768, 2048), BF),
            pltpu.VMEM((768, 128), BF),
            pltpu.VMEM((8, 128, 128), BF),
            pltpu.VMEM((768, 128), BF),
            pltpu.SemaphoreType.DMA((45,)),
        ],
        compiler_params=pltpu.CompilerParams(vmem_limit_bytes=59 * 1024 * 1024),
    )(place, gathered, att_all, teacher)
    own = lax.all_to_all(student, CHIPS, 0, 0)
    other = lax.ppermute(own, "c", swap)

    projector_t, own_projected = call(
        own_projected_kernel, [shape(256, 3072), shape(256, 256, dtype=F32)], [VMEM] * 2, (own, projector), 24, 4 * 10 ** 8
    )
    eight = shape(8, 96, 256)
    mismatch, far_up, far_down, up, down = call(
        sent_kernel,
        [shape(512, 256), shape(4, 96, 256), shape(4, 96, 256), eight, eight],
        [SMEM] + [VMEM] * 4,
        (place, own, other, projector_t, own_projected),
        32,
        8 * 10 ** 8,
    )
    below, above = from_z(up, -1), from_z(down, 1)
    far_below, far_above = from_z(far_up, -2), from_z(far_down, 2)
    kept = call(kept_kernel, shape(8, 96, 256, dtype=F32), [SMEM] + [VMEM] * 3, (place, own, other, mismatch), 32, 2 * 10 ** 8)
    near = call(add_kernel, shape(8, 96, 256), [VMEM] * 5, (kept, below, above, far_below, far_above), 16)
    grad = call(final_kernel, shape(96, 256, dtype=F32), [VMEM], (lax.all_to_all(near, ("zh", "yl"), 0, 0),), 8)
    return grad, attended


def solution(mesh):
    fine = Mesh(mesh.devices.reshape(4, 4, 2, 2, 2, 2, 2), ("zh", "zl", "yl", "yh", "xh", "xl", "c"))
    return jax.shard_map(
        on_device,
        mesh=fine,
        in_specs=(
            P(CTX, HID),
            P(CTX, None),
            P(CTX, None),
            P(CTX),
            P(CTX, HID),
            P(None, HID),
            P(None, HID),
            P(CTX + HID, None),
        ),
        out_specs=(P(CTX, HID), P(CTX, HID)),
        check_vma=False,
    )
```

```python
import functools

import jax
import jax.numpy as jnp
from jax import lax
from jax.experimental import pallas as pl
from jax.experimental.pallas import tpu as pltpu
from jax.sharding import Mesh
from jax.sharding import PartitionSpec as P

HEAD = 128
SCALE2 = HEAD ** -0.5 * 1.4426950408889634
EMPTY = -1e30
MASKED = -2e30
BF = jnp.bfloat16
F32 = jnp.float32
CTX = ("zh", "zl", "yl")
HID = ("yh", "xh", "xl", "c")
GROUP = ("xl", "c")
OCTET = ("yl", "xl", "c")
HEADSETS = ("yh", "xh")
CHIPS = ("xl", "yh", "xh")
BLOCKS = 4


def start_kernel(keys, values, docs, weight_t, hidden_t, packed, doc_rows, both, block, joined, sem):
    j = lax.axis_index("xl") * 2 + lax.axis_index("c")
    g = lax.axis_index("yh") * 2 + lax.axis_index("xh")
    rows, columns = pl.ds(pl.multiple_of(j * 128, 128), 128), pl.ds(pl.multiple_of(g * 128, 128), 128)
    taken = [
        pltpu.make_async_copy(keys.at[rows, columns], block.at[pl.ds(0, 128)], sem.at[0]),
        pltpu.make_async_copy(values.at[rows, columns], block.at[pl.ds(128, 128)], sem.at[1]),
        pltpu.make_async_copy(weight_t, joined.at[:, pl.ds(0, 2048)], sem.at[2]),
        pltpu.make_async_copy(hidden_t, joined.at[:, pl.ds(2048, 512)], sem.at[3]),
    ]
    for copy in taken:
        copy.start()
    row_docs = jnp.concatenate([docs[...].astype(F32), jnp.zeros((12, 128), F32)], axis=0).astype(BF)
    block[256:272, :] = row_docs
    doc_rows[...] = row_docs
    given = [pltpu.make_async_copy(block, packed.at[i], sem.at[4 + i]) for i in range(4)]
    given.append(pltpu.make_async_copy(joined, both, sem.at[8]))
    taken[0].wait()
    taken[1].wait()
    for copy in given[:4]:
        copy.start()
    taken[2].wait()
    taken[3].wait()
    given[4].start()
    for copy in given:
        copy.wait()


def attend_kernel(place, kv0, kv1, kv2, kv3_low, kv3_high, q_own, q_other, out, kv, q_all, v_turned, q_even, q_odd, s_even, s_odd, max_even, max_odd, acc, total, info_v, info, sem):
    j, yl, z = place[0], place[4], place[5]
    copies = [
        pltpu.make_async_copy(src, dst, sem.at[i])
        for i, (src, dst) in enumerate((
            (kv0, kv.at[0]), (kv1, kv.at[1]), (kv2, kv.at[2]), (kv3_low, kv.at[3, pl.ds(0, 2)]), (kv3_high, kv.at[3, pl.ds(2, 2)]),
            (q_own, q_all.at[0]), (q_other, q_all.at[1]),
        ))
    ]
    for copy in copies:
        copy.start()
    for copy in copies[:5]:
        copy.wait()
    block_docs = []
    for ch in range(4):
        for i in range(BLOCKS):
            rows = kv[i, ch, 256:272, :].astype(F32)
            block_docs.append(jnp.concatenate([rows[r:r + 1] for r in range(4)], axis=1))
    block_docs = jnp.concatenate(block_docs, axis=0)
    lane = lax.broadcasted_iota(jnp.int32, (16, 128), 1)
    counts = jnp.zeros((16, 128), F32)
    for d in range(8):
        below = jnp.sum((block_docs < d).astype(F32), axis=1, keepdims=True)
        counts = jnp.where(lane == d, below, counts)
    info_v[0:16, :] = counts.astype(jnp.int32)
    for copy in copies[5:]:
        copy.wait()
    for side in range(2):
        info_v[16 + 4 * side:20 + 4 * side, :] = q_all[side, 2048:2064, :].astype(F32)[0:4].astype(jnp.int32)
    to_scalars = pltpu.make_async_copy(info_v, info, sem.at[7])
    to_scalars.start()
    for ch in range(4):
        for i in range(BLOCKS):
            v_turned[:, (ch * BLOCKS + i) * 128:(ch * BLOCKS + i + 1) * 128] = kv[i, ch, 128:256, :].T
    to_scalars.wait()
    where = [(z + shift) % 4 for shift in (0, 3, 1, 2)]
    key_iota = lax.broadcasted_iota(jnp.int32, (128, 512), 0)
    row_iota = lax.broadcasted_iota(jnp.int32, (1, 512), 1) % 128

    first_doc = jnp.minimum(info[16, 0], info[20, 0])
    begin = jnp.int32(0)
    for ch in range(4):
        fewest = functools.reduce(jnp.minimum, [info[ch * BLOCKS + i, first_doc] for i in range(BLOCKS)])
        begin = begin + (fewest >= (j + 1) * 128).astype(jnp.int32)
    end = z // BLOCKS + 1

    def begin_scores(tile, q_ref, max_ref):
        side, row0 = tile // 4, pl.multiple_of(tile % 4 * 128, 128)
        for h in range(4):
            q_ref[h * 128:(h + 1) * 128, :] = q_all[side, pl.ds(h * 512 + row0, 128), :]
        max_ref[...] = jnp.full((1, 512), EMPTY, F32)

    def is_full(tile, ch):
        yl_q = jnp.where(tile // 4 == 0, yl, 1 - yl)
        q_min = (2 * z + yl_q) * 512 + tile % 4 * 128
        last = info[16 + tile, 127]
        most = functools.reduce(jnp.maximum, [info[ch * BLOCKS + i, last] for i in range(BLOCKS)])
        k_max = (2 * (ch * BLOCKS + BLOCKS - 1) + yl) * 512 + j * 128 + 127
        return (k_max <= q_min) & (most <= j * 128)

    def put_scores(tile, ch, masked, q_ref, s_ref, max_ref):
        keys = jnp.concatenate([kv[i, ch, 0:128, :] for i in range(BLOCKS)], axis=0)
        s = lax.dot_general(keys, q_ref[...], (((1,), (1,)), ((), ())), preferred_element_type=F32) * SCALE2
        if masked:
            yl_q = jnp.where(tile // 4 == 0, yl, 1 - yl)
            q_pos = (2 * z + yl_q) * 512 + tile % 4 * 128 + row_iota
            row_docs = jnp.concatenate([info_v[pl.ds(16 + tile, 1), :]] * 4, axis=1)
            parts = []
            for i in range(BLOCKS):
                low = jnp.zeros((1, 512), jnp.int32)
                for d in range(8):
                    low = jnp.where(row_docs == d, info[ch * BLOCKS + i, d], low)
                low = low - j * 128
                high = q_pos - ((2 * (ch * 4 + where[i]) + yl) * 512 + j * 128)
                ok = (key_iota >= low) & (key_iota <= high)
                parts.append(jnp.where(ok, s[i * 128:(i + 1) * 128], MASKED))
            s = jnp.concatenate(parts, axis=0)
        s_ref[ch] = s
        max_ref[...] = jnp.maximum(max_ref[...], jnp.max(s, axis=0, keepdims=True))

    def add_up(ch, s_ref, max_ref):
        w = jnp.exp2(s_ref[ch] - max_ref[...])
        cols = pl.ds(pl.multiple_of(ch * (BLOCKS * 128), BLOCKS * 128), BLOCKS * 128)
        acc[...] += jnp.dot(v_turned[:, cols], w.astype(BF), preferred_element_type=F32)
        total[...] += jnp.sum(w, axis=0, keepdims=True)

    def finish(tile, max_ref):
        run_sum, run_max = total[...], max_ref[...]
        seen = run_sum > 0
        o = (acc[...] * (1.0 / jnp.where(seen, run_sum, 1.0))).astype(BF)
        lse = jnp.where(seen, run_max + jnp.log2(jnp.where(seen, run_sum, 1.0)), EMPTY)
        hi = lse.astype(BF).astype(F32)
        mid = (lse - hi).astype(BF).astype(F32)
        lo = lse - hi - mid
        dest = jnp.where(tile // 4 == 0, yl, 1 - yl) * 4 + tile % 4
        rows = [part[:, h * 128:(h + 1) * 128] for part in (hi, mid, lo) for h in range(4)]
        rows.append(jnp.zeros((4, 128), F32))
        for h in range(4):
            out[dest, h * 128:(h + 1) * 128, :] = o[:, h * 128:(h + 1) * 128]
        out[dest, 512:528, :] = jnp.concatenate(rows, axis=0).astype(BF)
        acc[...] = jnp.zeros((128, 512), F32)
        total[...] = jnp.zeros((1, 512), F32)

    def sweep(tile, put, use):
        if put is not None:
            begin_scores(tile, put[0], put[2])

        def one(ch, carry):
            def work(masked):
                if put is not None:
                    put_scores(tile, ch, masked, *put)
                if use is not None:
                    add_up(ch, use[1], use[2])

            if put is None:
                work(False)
            else:
                full = is_full(tile, ch)
                pl.when(full)(lambda: work(False))
                pl.when(jnp.logical_not(full))(lambda: work(True))
            return carry

        lax.fori_loop(begin, end, one, 0)
        if use is not None:
            finish(tile - 1, use[2])

    even, odd = (q_even, s_even, max_even), (q_odd, s_odd, max_odd)
    acc[...] = jnp.zeros((128, 512), F32)
    total[...] = jnp.zeros((1, 512), F32)
    sweep(0, even, None)

    def two_tiles(pair, carry):
        sweep(2 * pair + 1, odd, even)
        sweep(2 * pair + 2, even, odd)
        return carry

    lax.fori_loop(0, 3, two_tiles, 0)
    sweep(7, odd, even)
    sweep(8, None, odd)


def combine_kernel(parts, out, copies):
    count = parts.shape[0]
    tails = [parts[s, 512:528, :].astype(F32) for s in range(count)]
    for h in range(4):
        lses = [t[h:h + 1] + t[4 + h:5 + h] + t[8 + h:9 + h] for t in tails]
        top = functools.reduce(jnp.maximum, lses)
        weights = [jnp.exp2(v - top) for v in lses]
        inverse = 1.0 / sum(weights)
        rows = slice(h * 128, (h + 1) * 128)
        total = sum(w * inverse * parts[s, rows, :].astype(F32) for s, w in enumerate(weights)).astype(BF)
        out[rows, :] = total
        for copy in range(copies.shape[0]):
            copies[copy, rows, :] = total


def student_kernel(place, gathered, att, teacher, out):
    own_rows = pl.ds(pl.multiple_of(2048 + place[0] * 128, 128), 128)
    att_all = att[...].reshape(2048, 128)
    for part in range(4):
        rows = slice(part * 192, (part + 1) * 192)
        mixed = jnp.dot(gathered[rows, 0:2048], att_all, preferred_element_type=F32)
        student = (gathered[rows, own_rows].astype(F32) + mixed).astype(BF)
        for copy in range(8):
            out[copy, rows, :] = student
    for chip in range(8):
        first = (chip % 4 * 4 + chip // 4 * 2) * 256
        for i in range(4):
            out[chip, 768 + i * 32:800 + i * 32, :] = teacher[:, first + i * 128:first + (i + 1) * 128]


def projected(student, projector_t):
    total = 0.0
    for g in range(4):
        both = jnp.concatenate([student[g, 0:768, :], student[4 + g, 0:768, :]], axis=1)
        total = total + jnp.dot(projector_t[:, g * 768:(g + 1) * 768], both, preferred_element_type=F32)
    return total


def teacher_rows(own, other, core, chunk_core):
    pieces = []
    for xl in range(2):
        for t in range(4):
            source = t // 2 * 4 + xl * 2 + chunk_core
            halves = []
            for i in range(2):
                rows = pl.ds(pl.multiple_of(768 + core * 64 + i * 32, 32), 32)
                halves.append(jnp.where(core == t % 2, own[source, rows, :].astype(F32), other[source, rows, :].astype(F32)))
            pieces.append(jnp.concatenate(halves, axis=1))
    return jnp.concatenate(pieces, axis=0)


def gradient_rows(own, other, mismatch, near):
    rows = []
    for zh in range(4):
        cut = pl.ds(pl.multiple_of(near * 192, 64), 192)
        rows.append(jnp.concatenate([ref[xl * 4 + zh, cut, :] for ref in (own, other) for xl in range(2)], axis=1))
    return jnp.dot(jnp.concatenate(rows, axis=0), mismatch[...], preferred_element_type=F32).reshape(8, 96, 256)


def own_projected_kernel(own, projector, projector_t, out):
    for g in range(4):
        projector_t[:, g * 768:(g + 1) * 768] = projector[g * 768:(g + 1) * 768, :].T
    out[...] = projected(own, projector_t).T


def sent_kernel(place, own, other, projector_t, own_projected, mismatch, far_up, far_down, up, down):
    core, near = place[2], place[6]
    mismatch[0:256, :] = (own_projected[...] - teacher_rows(own, other, core, core)).astype(BF)
    mismatch[256:512, :] = (projected(other, projector_t).T - teacher_rows(own, other, core, 1 - core)).astype(BF)
    up[...] = gradient_rows(own, other, mismatch, (near + 1) % 4).astype(BF)
    down[...] = gradient_rows(own, other, mismatch, (near + 3) % 4).astype(BF)
    far = gradient_rows(own, other, mismatch, (near + 2) % 4).astype(BF)
    far_up[...] = far[0:4]
    far_down[...] = far[4:8]


def kept_kernel(place, own, other, mismatch, out):
    out[...] = gradient_rows(own, other, mismatch, place[6])


def add_kernel(kept, below, above, far_below, far_above, out):
    near = kept[...] + below[...].astype(F32) + above[...].astype(F32)
    out[0:4] = (near[0:4] + far_below[...].astype(F32)).astype(BF)
    out[4:8] = (near[4:8] + far_above[...].astype(F32)).astype(BF)


def final_kernel(terms, out):
    out[...] = sum(terms[i].astype(F32) for i in range(terms.shape[0])) * (16384 ** -0.5)


VMEM = pl.BlockSpec(memory_space=pltpu.VMEM)
SMEM = pl.BlockSpec(memory_space=pltpu.SMEM)
ANY = pl.BlockSpec(memory_space=pl.ANY)
HBM = pl.BlockSpec(memory_space=pltpu.HBM)


def call(kernel, out_shape, specs, operands, limit, flops=0, scratch=()):
    single = not isinstance(out_shape, list)
    return pl.pallas_call(
        kernel,
        out_shape=out_shape,
        in_specs=specs,
        out_specs=VMEM if single else [VMEM] * len(out_shape),
        scratch_shapes=list(scratch),
        compiler_params=pltpu.CompilerParams(vmem_limit_bytes=limit * 1024 * 1024),
        cost_estimate=pl.CostEstimate(flops=flops, bytes_accessed=4 * 1024 * 1024, transcendentals=0),
    )(*operands)


def shape(*dims, dtype=BF):
    return jax.ShapeDtypeStruct(dims, dtype)


def start(keys, values, docs, weight_t, hidden_t):
    return pl.pallas_call(
        start_kernel,
        in_specs=[ANY, ANY, VMEM, ANY, ANY],
        out_specs=[ANY, VMEM, ANY],
        scratch_shapes=[pltpu.VMEM((272, 128), BF), pltpu.VMEM((192, 2560), BF), pltpu.SemaphoreType.DMA((9,))],
        out_shape=[shape(4, 272, 128), shape(16, 128), shape(192, 2560)],
    )(keys, values, docs, weight_t, hidden_t)


def on_device(queries, keys, values, doc_ids, hidden, out_weight, projector, teacher):
    zl, yl, xl, c = lax.axis_index("zl"), lax.axis_index("yl"), lax.axis_index("xl"), lax.axis_index("c")
    j = xl * 2 + c
    z = lax.axis_index("zh") * 4 + zl
    g = lax.axis_index("yh") * 2 + lax.axis_index("xh")
    swap = [(0, 1), (1, 0)]
    place = jnp.stack([j, g, c, xl, yl, z, zl]).astype(jnp.int32)

    def from_z(x, shift):
        return lax.ppermute(x, ("zh", "zl"), [((i + shift) % 16, i) for i in range(16)])

    docs = doc_ids.reshape(4, 128)
    packed, doc_rows, both = start(keys, values, docs, out_weight.T, hidden.T)
    kv_own = lax.all_to_all(packed, "zh", 0, 0)
    kv_below, kv_above = from_z(kv_own, -1), from_z(kv_own, 1)
    kv_low, kv_high = from_z(kv_own[0:2], -2), from_z(kv_own[2:4], 2)

    q_own = jnp.concatenate([lax.all_gather(queries, GROUP, axis=0, tiled=True), doc_rows], axis=0)
    q_other = lax.ppermute(q_own, "yl", swap)
    gathered = lax.all_gather(both, GROUP, axis=0, tiled=True)

    partial = call(
        attend_kernel,
        shape(8, 528, 128),
        [SMEM] + [ANY] * 7,
        (place, kv_own, kv_below, kv_above, kv_low, kv_high, q_own, q_other),
        40,
        2 * 10 ** 10,
        scratch=[
            pltpu.VMEM((4, 4, 272, 128), BF),
            pltpu.VMEM((2, 2064, 128), BF),
            pltpu.VMEM((128, 2048), BF),
            pltpu.VMEM((512, 128), BF),
            pltpu.VMEM((512, 128), BF),
            pltpu.VMEM((4, 512, 512), F32),
            pltpu.VMEM((4, 512, 512), F32),
            pltpu.VMEM((1, 512), F32),
            pltpu.VMEM((1, 512), F32),
            pltpu.VMEM((128, 512), F32),
            pltpu.VMEM((1, 512), F32),
            pltpu.VMEM((24, 128), jnp.int32),
            pltpu.SMEM((24, 128), jnp.int32),
            pltpu.SemaphoreType.DMA((8,)),
        ],
    )
    att_rows, att_copies = call(
        combine_kernel, [shape(512, 128), shape(4, 512, 128)], [VMEM], (lax.all_to_all(partial, OCTET, 0, 0),), 16
    )

    att_head = lax.all_to_all(att_rows.reshape(4, 128, 128), GROUP, 0, 0)
    attended = jnp.transpose(att_head, (0, 2, 1)).reshape(512, 128)

    att_all = lax.all_to_all(att_copies, HEADSETS, 0, 0)
    student = call(
        student_kernel,
        shape(8, 896, 128),
        [SMEM, VMEM, VMEM, VMEM],
        (place, gathered, att_all, teacher),
        24,
    )
    own = lax.all_to_all(student, CHIPS, 0, 0)
    other = lax.ppermute(own, "c", swap)

    projector_t, own_projected = call(
        own_projected_kernel, [shape(256, 3072), shape(256, 256, dtype=F32)], [VMEM] * 2, (own, projector), 24, 4 * 10 ** 8
    )
    eight = shape(8, 96, 256)
    mismatch, far_up, far_down, up, down = call(
        sent_kernel,
        [shape(512, 256), shape(4, 96, 256), shape(4, 96, 256), eight, eight],
        [SMEM] + [VMEM] * 4,
        (place, own, other, projector_t, own_projected),
        32,
        8 * 10 ** 8,
    )
    below, above = from_z(up, -1), from_z(down, 1)
    far_below, far_above = from_z(far_up, -2), from_z(far_down, 2)
    kept = call(kept_kernel, shape(8, 96, 256, dtype=F32), [SMEM] + [VMEM] * 3, (place, own, other, mismatch), 32, 2 * 10 ** 8)
    near = call(add_kernel, shape(8, 96, 256), [VMEM] * 5, (kept, below, above, far_below, far_above), 16)
    grad = call(final_kernel, shape(96, 256, dtype=F32), [VMEM], (lax.all_to_all(near, ("zh", "yl"), 0, 0),), 8)
    return grad, attended


def solution(mesh):
    fine = Mesh(mesh.devices.reshape(4, 4, 2, 2, 2, 2, 2), ("zh", "zl", "yl", "yh", "xh", "xl", "c"))
    return jax.shard_map(
        on_device,
        mesh=fine,
        in_specs=(
            P(CTX, HID),
            P(CTX, None),
            P(CTX, None),
            P(CTX),
            P(CTX, HID),
            P(None, HID),
            P(None, HID),
            P(CTX + HID, None),
        ),
        out_specs=(P(CTX, HID), P(CTX, HID)),
        check_vma=False,
    )
```

```python
import functools

import jax
import jax.numpy as jnp
from jax import lax
from jax.experimental import pallas as pl
from jax.experimental.pallas import tpu as pltpu
from jax.sharding import Mesh
from jax.sharding import PartitionSpec as P

HEAD = 128
SCALE2 = HEAD ** -0.5 * 1.4426950408889634
EMPTY = -1e30
MASKED = -2e30
BF = jnp.bfloat16
F32 = jnp.float32
CTX = ("zh", "zl", "yl")
HID = ("yh", "xh", "xl", "c")
GROUP = ("xl", "c")
OCTET = ("yl", "xl", "c")
HEADSETS = ("yh", "xh")
CHIPS = ("xl", "yh", "xh")
BLOCKS = 4


def start_kernel(keys, values, docs, weight_t, hidden_t, packed, doc_rows, both, block, joined, sem):
    j = lax.axis_index("xl") * 2 + lax.axis_index("c")
    g = lax.axis_index("yh") * 2 + lax.axis_index("xh")
    rows, columns = pl.ds(pl.multiple_of(j * 128, 128), 128), pl.ds(pl.multiple_of(g * 128, 128), 128)
    taken = [
        pltpu.make_async_copy(keys.at[rows, columns], block.at[pl.ds(0, 128)], sem.at[0]),
        pltpu.make_async_copy(values.at[rows, columns], block.at[pl.ds(128, 128)], sem.at[1]),
        pltpu.make_async_copy(weight_t, joined.at[:, pl.ds(0, 2048)], sem.at[2]),
        pltpu.make_async_copy(hidden_t, joined.at[:, pl.ds(2048, 512)], sem.at[3]),
    ]
    for copy in taken:
        copy.start()
    row_docs = jnp.concatenate([docs[...].astype(F32), jnp.zeros((12, 128), F32)], axis=0).astype(BF)
    block[256:272, :] = row_docs
    doc_rows[...] = row_docs
    given = [pltpu.make_async_copy(block, packed.at[i], sem.at[4 + i]) for i in range(4)]
    given.append(pltpu.make_async_copy(joined, both, sem.at[8]))
    taken[0].wait()
    taken[1].wait()
    for copy in given[:4]:
        copy.start()
    taken[2].wait()
    taken[3].wait()
    given[4].start()
    for copy in given:
        copy.wait()


def attend_kernel(place, kv0, kv1, kv2, kv3_low, kv3_high, q_own, q_other, out, kv, q_all, v_turned, q_even, q_odd, s_even, s_odd, max_even, max_odd, acc, total, info_v, info, sem):
    j, yl, z = place[0], place[4], place[5]
    copies = [
        pltpu.make_async_copy(src, dst, sem.at[i])
        for i, (src, dst) in enumerate((
            (kv0, kv.at[0]), (kv1, kv.at[1]), (kv2, kv.at[2]), (kv3_low, kv.at[3, pl.ds(0, 2)]), (kv3_high, kv.at[3, pl.ds(2, 2)]),
            (q_own, q_all.at[0]), (q_other, q_all.at[1]),
        ))
    ]
    for copy in copies:
        copy.start()
    for copy in copies[:5]:
        copy.wait()
    block_docs = []
    for ch in range(4):
        for i in range(BLOCKS):
            rows = kv[i, ch, 256:272, :].astype(F32)
            block_docs.append(jnp.concatenate([rows[r:r + 1] for r in range(4)], axis=1))
    block_docs = jnp.concatenate(block_docs, axis=0)
    lane = lax.broadcasted_iota(jnp.int32, (16, 128), 1)
    counts = jnp.zeros((16, 128), F32)
    for d in range(8):
        below = jnp.sum((block_docs < d).astype(F32), axis=1, keepdims=True)
        counts = jnp.where(lane == d, below, counts)
    info_v[0:16, :] = counts.astype(jnp.int32)
    for copy in copies[5:]:
        copy.wait()
    for side in range(2):
        info_v[16 + 4 * side:20 + 4 * side, :] = q_all[side, 2048:2064, :].astype(F32)[0:4].astype(jnp.int32)
    to_scalars = pltpu.make_async_copy(info_v, info, sem.at[7])
    to_scalars.start()
    for ch in range(4):
        for i in range(BLOCKS):
            v_turned[:, (ch * BLOCKS + i) * 128:(ch * BLOCKS + i + 1) * 128] = kv[i, ch, 128:256, :].T
    to_scalars.wait()
    where = [(z + shift) % 4 for shift in (0, 3, 1, 2)]
    key_iota = lax.broadcasted_iota(jnp.int32, (128, 512), 0)
    row_iota = lax.broadcasted_iota(jnp.int32, (1, 512), 1) % 128

    first_doc = jnp.minimum(info[16, 0], info[20, 0])
    begin = jnp.int32(0)
    for ch in range(4):
        fewest = functools.reduce(jnp.minimum, [info[ch * BLOCKS + i, first_doc] for i in range(BLOCKS)])
        begin = begin + (fewest >= (j + 1) * 128).astype(jnp.int32)
    end = z // BLOCKS + 1

    def begin_scores(tile, q_ref, max_ref):
        side, row0 = tile // 4, pl.multiple_of(tile % 4 * 128, 128)
        for h in range(4):
            q_ref[h * 128:(h + 1) * 128, :] = q_all[side, pl.ds(h * 512 + row0, 128), :]
        max_ref[...] = jnp.full((1, 512), EMPTY, F32)

    def is_full(tile, ch):
        yl_q = jnp.where(tile // 4 == 0, yl, 1 - yl)
        q_min = (2 * z + yl_q) * 512 + tile % 4 * 128
        last = info[16 + tile, 127]
        most = functools.reduce(jnp.maximum, [info[ch * BLOCKS + i, last] for i in range(BLOCKS)])
        k_max = (2 * (ch * BLOCKS + BLOCKS - 1) + yl) * 512 + j * 128 + 127
        return (k_max <= q_min) & (most <= j * 128)

    def put_scores(tile, ch, masked, q_ref, s_ref, max_ref):
        keys = jnp.concatenate([kv[i, ch, 0:128, :] for i in range(BLOCKS)], axis=0)
        s = lax.dot_general(keys, q_ref[...], (((1,), (1,)), ((), ())), preferred_element_type=F32) * SCALE2
        if masked:
            yl_q = jnp.where(tile // 4 == 0, yl, 1 - yl)
            q_pos = (2 * z + yl_q) * 512 + tile % 4 * 128 + row_iota
            row_docs = jnp.concatenate([info_v[pl.ds(16 + tile, 1), :]] * 4, axis=1)
            parts = []
            for i in range(BLOCKS):
                low = jnp.zeros((1, 512), jnp.int32)
                for d in range(8):
                    low = jnp.where(row_docs == d, info[ch * BLOCKS + i, d], low)
                low = low - j * 128
                high = q_pos - ((2 * (ch * 4 + where[i]) + yl) * 512 + j * 128)
                ok = (key_iota >= low) & (key_iota <= high)
                parts.append(jnp.where(ok, s[i * 128:(i + 1) * 128], MASKED))
            s = jnp.concatenate(parts, axis=0)
        s_ref[ch] = s
        max_ref[...] = jnp.maximum(max_ref[...], jnp.max(s, axis=0, keepdims=True))

    def add_up(ch, s_ref, max_ref):
        w = jnp.exp2(s_ref[ch] - max_ref[...])
        cols = pl.ds(pl.multiple_of(ch * (BLOCKS * 128), BLOCKS * 128), BLOCKS * 128)
        acc[...] += jnp.dot(v_turned[:, cols], w.astype(BF), preferred_element_type=F32)
        total[...] += jnp.sum(w, axis=0, keepdims=True)

    def finish(tile, max_ref):
        run_sum, run_max = total[...], max_ref[...]
        seen = run_sum > 0
        o = (acc[...] * (1.0 / jnp.where(seen, run_sum, 1.0))).astype(BF)
        lse = jnp.where(seen, run_max + jnp.log2(jnp.where(seen, run_sum, 1.0)), EMPTY)
        hi = lse.astype(BF).astype(F32)
        mid = (lse - hi).astype(BF).astype(F32)
        lo = lse - hi - mid
        dest = jnp.where(tile // 4 == 0, yl, 1 - yl) * 4 + tile % 4
        rows = [part[:, h * 128:(h + 1) * 128] for part in (hi, mid, lo) for h in range(4)]
        rows.append(jnp.zeros((4, 128), F32))
        for h in range(4):
            out[dest, h * 128:(h + 1) * 128, :] = o[:, h * 128:(h + 1) * 128]
        out[dest, 512:528, :] = jnp.concatenate(rows, axis=0).astype(BF)
        acc[...] = jnp.zeros((128, 512), F32)
        total[...] = jnp.zeros((1, 512), F32)

    def sweep(tile, put, use):
        if put is not None:
            begin_scores(tile, put[0], put[2])

        def one(ch, carry):
            def work(masked):
                if put is not None:
                    put_scores(tile, ch, masked, *put)
                if use is not None:
                    add_up(ch, use[1], use[2])

            if put is None:
                work(False)
            else:
                full = is_full(tile, ch)
                pl.when(full)(lambda: work(False))
                pl.when(jnp.logical_not(full))(lambda: work(True))
            return carry

        lax.fori_loop(begin, end, one, 0)
        if use is not None:
            finish(tile - 1, use[2])

    even, odd = (q_even, s_even, max_even), (q_odd, s_odd, max_odd)
    acc[...] = jnp.zeros((128, 512), F32)
    total[...] = jnp.zeros((1, 512), F32)
    sweep(0, even, None)

    def two_tiles(pair, carry):
        sweep(2 * pair + 1, odd, even)
        sweep(2 * pair + 2, even, odd)
        return carry

    lax.fori_loop(0, 3, two_tiles, 0)
    sweep(7, odd, even)
    sweep(8, None, odd)


def combine_kernel(parts, out, copies):
    count = parts.shape[0]
    tails = [parts[s, 512:528, :].astype(F32) for s in range(count)]
    for h in range(4):
        lses = [t[h:h + 1] + t[4 + h:5 + h] + t[8 + h:9 + h] for t in tails]
        top = functools.reduce(jnp.maximum, lses)
        weights = [jnp.exp2(v - top) for v in lses]
        inverse = 1.0 / sum(weights)
        rows = slice(h * 128, (h + 1) * 128)
        total = sum(w * inverse * parts[s, rows, :].astype(F32) for s, w in enumerate(weights)).astype(BF)
        out[rows, :] = total
        for copy in range(copies.shape[0]):
            copies[copy, rows, :] = total


def student_kernel(place, gathered, att, teacher, out):
    own_rows = pl.ds(pl.multiple_of(2048 + place[0] * 128, 128), 128)
    att_all = att[...].reshape(2048, 128)
    for part in range(4):
        rows = slice(part * 192, (part + 1) * 192)
        mixed = jnp.dot(gathered[rows, 0:2048], att_all, preferred_element_type=F32)
        student = (gathered[rows, own_rows].astype(F32) + mixed).astype(BF)
        for copy in range(8):
            out[copy, rows, :] = student
    for chip in range(8):
        first = (chip % 4 * 4 + chip // 4 * 2) * 256
        for i in range(4):
            out[chip, 768 + i * 32:800 + i * 32, :] = teacher[:, first + i * 128:first + (i + 1) * 128]


def projected(student, projector_t):
    total = 0.0
    for g in range(4):
        both = jnp.concatenate([student[g, 0:768, :], student[4 + g, 0:768, :]], axis=1)
        total = total + jnp.dot(projector_t[:, g * 768:(g + 1) * 768], both, preferred_element_type=F32)
    return total


def teacher_rows(own, other, core, chunk_core):
    pieces = []
    for xl in range(2):
        for t in range(4):
            source = t // 2 * 4 + xl * 2 + chunk_core
            halves = []
            for i in range(2):
                rows = pl.ds(pl.multiple_of(768 + core * 64 + i * 32, 32), 32)
                halves.append(jnp.where(core == t % 2, own[source, rows, :].astype(F32), other[source, rows, :].astype(F32)))
            pieces.append(jnp.concatenate(halves, axis=1))
    return jnp.concatenate(pieces, axis=0)


def gradient_rows(own, other, mismatch, near):
    rows = []
    for zh in range(4):
        cut = pl.ds(pl.multiple_of(near * 192, 64), 192)
        rows.append(jnp.concatenate([ref[xl * 4 + zh, cut, :] for ref in (own, other) for xl in range(2)], axis=1))
    return jnp.dot(jnp.concatenate(rows, axis=0), mismatch[...], preferred_element_type=F32).reshape(8, 96, 256)


def own_projected_kernel(own, projector, projector_t, out):
    for g in range(4):
        projector_t[:, g * 768:(g + 1) * 768] = projector[g * 768:(g + 1) * 768, :].T
    out[...] = projected(own, projector_t).T


def sent_kernel(place, own, other, projector_t, own_projected, mismatch, far_up, far_down, up, down):
    core, near = place[2], place[6]
    mismatch[0:256, :] = (own_projected[...] - teacher_rows(own, other, core, core)).astype(BF)
    mismatch[256:512, :] = (projected(other, projector_t).T - teacher_rows(own, other, core, 1 - core)).astype(BF)
    up[...] = gradient_rows(own, other, mismatch, (near + 1) % 4).astype(BF)
    down[...] = gradient_rows(own, other, mismatch, (near + 3) % 4).astype(BF)
    far = gradient_rows(own, other, mismatch, (near + 2) % 4).astype(BF)
    far_up[...] = far[0:4]
    far_down[...] = far[4:8]


def kept_kernel(place, own, other, mismatch, out):
    out[...] = gradient_rows(own, other, mismatch, place[6])


def add_kernel(kept, far_below, far_above, below, above, out):
    near = kept[...] + below[...].astype(F32) + above[...].astype(F32)
    out[0:4] = (near[0:4] + far_below[...].astype(F32)).astype(BF)
    out[4:8] = (near[4:8] + far_above[...].astype(F32)).astype(BF)


def final_kernel(terms, out):
    out[...] = sum(terms[i].astype(F32) for i in range(terms.shape[0])) * (16384 ** -0.5)


VMEM = pl.BlockSpec(memory_space=pltpu.VMEM)
SMEM = pl.BlockSpec(memory_space=pltpu.SMEM)
ANY = pl.BlockSpec(memory_space=pl.ANY)
HBM = pl.BlockSpec(memory_space=pltpu.HBM)


def call(kernel, out_shape, specs, operands, limit, flops=0, scratch=()):
    single = not isinstance(out_shape, list)
    return pl.pallas_call(
        kernel,
        out_shape=out_shape,
        in_specs=specs,
        out_specs=VMEM if single else [VMEM] * len(out_shape),
        scratch_shapes=list(scratch),
        compiler_params=pltpu.CompilerParams(vmem_limit_bytes=limit * 1024 * 1024),
        cost_estimate=pl.CostEstimate(flops=flops, bytes_accessed=4 * 1024 * 1024, transcendentals=0),
    )(*operands)


def shape(*dims, dtype=BF):
    return jax.ShapeDtypeStruct(dims, dtype)


def start(keys, values, docs, weight_t, hidden_t):
    return pl.pallas_call(
        start_kernel,
        in_specs=[ANY, ANY, VMEM, ANY, ANY],
        out_specs=[ANY, VMEM, ANY],
        scratch_shapes=[pltpu.VMEM((272, 128), BF), pltpu.VMEM((192, 2560), BF), pltpu.SemaphoreType.DMA((9,))],
        out_shape=[shape(4, 272, 128), shape(16, 128), shape(192, 2560)],
    )(keys, values, docs, weight_t, hidden_t)


def on_device(queries, keys, values, doc_ids, hidden, out_weight, projector, teacher):
    zl, yl, xl, c = lax.axis_index("zl"), lax.axis_index("yl"), lax.axis_index("xl"), lax.axis_index("c")
    j = xl * 2 + c
    z = lax.axis_index("zh") * 4 + zl
    g = lax.axis_index("yh") * 2 + lax.axis_index("xh")
    swap = [(0, 1), (1, 0)]
    place = jnp.stack([j, g, c, xl, yl, z, zl]).astype(jnp.int32)

    def from_z(x, shift):
        return lax.ppermute(x, ("zh", "zl"), [((i + shift) % 16, i) for i in range(16)])

    docs = doc_ids.reshape(4, 128)
    packed, doc_rows, both = start(keys, values, docs, out_weight.T, hidden.T)
    kv_own = lax.all_to_all(packed, "zh", 0, 0)
    kv_below, kv_above = from_z(kv_own, -1), from_z(kv_own, 1)
    kv_low, kv_high = from_z(kv_own[0:2], -2), from_z(kv_own[2:4], 2)

    q_own = jnp.concatenate([lax.all_gather(queries, GROUP, axis=0, tiled=True), doc_rows], axis=0)
    q_other = lax.ppermute(q_own, "yl", swap)
    gathered = lax.all_gather(both, GROUP, axis=0, tiled=True)

    partial = call(
        attend_kernel,
        shape(8, 528, 128),
        [SMEM] + [ANY] * 7,
        (place, kv_own, kv_below, kv_above, kv_low, kv_high, q_own, q_other),
        40,
        2 * 10 ** 10,
        scratch=[
            pltpu.VMEM((4, 4, 272, 128), BF),
            pltpu.VMEM((2, 2064, 128), BF),
            pltpu.VMEM((128, 2048), BF),
            pltpu.VMEM((512, 128), BF),
            pltpu.VMEM((512, 128), BF),
            pltpu.VMEM((4, 512, 512), F32),
            pltpu.VMEM((4, 512, 512), F32),
            pltpu.VMEM((1, 512), F32),
            pltpu.VMEM((1, 512), F32),
            pltpu.VMEM((128, 512), F32),
            pltpu.VMEM((1, 512), F32),
            pltpu.VMEM((24, 128), jnp.int32),
            pltpu.SMEM((24, 128), jnp.int32),
            pltpu.SemaphoreType.DMA((8,)),
        ],
    )
    att_rows, att_copies = call(
        combine_kernel, [shape(512, 128), shape(4, 512, 128)], [VMEM], (lax.all_to_all(partial, OCTET, 0, 0),), 16
    )

    att_head = lax.all_to_all(att_rows.reshape(4, 128, 128), GROUP, 0, 0)
    attended = jnp.transpose(att_head, (0, 2, 1)).reshape(512, 128)

    att_all = lax.all_to_all(att_copies, HEADSETS, 0, 0)
    student = call(
        student_kernel,
        shape(8, 896, 128),
        [SMEM, VMEM, VMEM, VMEM],
        (place, gathered, att_all, teacher),
        24,
    )
    own = lax.all_to_all(student, CHIPS, 0, 0)
    other = lax.ppermute(own, "c", swap)

    projector_t, own_projected = call(
        own_projected_kernel, [shape(256, 3072), shape(256, 256, dtype=F32)], [VMEM] * 2, (own, projector), 24, 4 * 10 ** 8
    )
    eight = shape(8, 96, 256)
    mismatch, far_up, far_down, up, down = call(
        sent_kernel,
        [shape(512, 256), shape(4, 96, 256), shape(4, 96, 256), eight, eight],
        [SMEM] + [VMEM] * 4,
        (place, own, other, projector_t, own_projected),
        32,
        8 * 10 ** 8,
    )
    below, above = from_z(up, -1), from_z(down, 1)
    far_below, far_above = from_z(far_up, -2), from_z(far_down, 2)
    kept = call(kept_kernel, shape(8, 96, 256, dtype=F32), [SMEM] + [VMEM] * 3, (place, own, other, mismatch), 32, 2 * 10 ** 8)
    near = call(add_kernel, shape(8, 96, 256), [VMEM] * 5, (kept, far_below, far_above, below, above), 16)
    grad = call(final_kernel, shape(96, 256, dtype=F32), [VMEM], (lax.all_to_all(near, ("zh", "yl"), 0, 0),), 8)
    return grad, attended


def solution(mesh):
    fine = Mesh(mesh.devices.reshape(4, 4, 2, 2, 2, 2, 2), ("zh", "zl", "yl", "yh", "xh", "xl", "c"))
    return jax.shard_map(
        on_device,
        mesh=fine,
        in_specs=(
            P(CTX, HID),
            P(CTX, None),
            P(CTX, None),
            P(CTX),
            P(CTX, HID),
            P(None, HID),
            P(None, HID),
            P(CTX + HID, None),
        ),
        out_specs=(P(CTX, HID), P(CTX, HID)),
        check_vma=False,
    )
```
